512 devices in a mesh: plane: 64 (over z, x, core), span: 8 (over y).
Axes of the slice: x: 4, y: 8, z: 8, core: 2. Of those that a mesh axis runs over, the one named last changes fastest.
Arguments:
- stress: float32 [6, 32, 7, 7, 8192], P(None, 'span', None, None, 'plane'), may hold values from -4 to 4
- velocity_grad: float32 [9, 32, 7, 7, 8192], P(None, 'span', None, None, 'plane'), may hold values from -4 to 4
- velocity: float32 [2, 32, 7, 7, 8192], P(None, 'span', None, None, 'plane'), may hold values from -4 to 4
- metric: float32 [3, 7, 7, 8192], P(None, None, None, 'plane'), may hold values from 0.3 to 3
- iteration_counts: int32 [32], replicated, may hold values from 1 to 8
Outputs:
- new_stress: float32 [6, 32, 7, 7, 8192], P(None, 'span', None, None, 'plane')
- pressure: float32 [32, 7, 7, 8192], P('span', None, None, 'plane')
The draws below stay inside these ranges and needn't reach their ends.
All inputs are finite; a program needn't handle non-finite values.
Results may differ from the reference program's by a relative error of at most 0.0003.
Values sent between devices are 32-bit elements; how exact they have to be, the bound alone decides.
No kernel may reach another device: no remote copies, remote signals or barrier semaphores. Data moves between devices by JAX's collectives and lax.ppermute only.
A program may use at most 128 MiB of HBM per device.

```python
import math
import jax
import jax.numpy as jnp
import numpy as np
from jax import lax

EX = 8
EY = 16
NODE = 7
NDY = 4
NZ = 32
ITMAX = 8
NDX = 16
ELEMS = 8192


def draw_iteration_counts(key, part):
    key = jax.random.fold_in(key, 11)
    row_ids = jnp.arange(NZ, dtype=jnp.int32)
    harmonic = jnp.where(row_ids == 1, NZ // 2, row_ids // 2)
    jitter = jax.random.randint(key, (NZ,), -1, 2)
    counts = ITMAX - harmonic * ITMAX // (NZ // 2) + jitter
    counts = jnp.clip(counts, 1, ITMAX)
    counts = jnp.where(row_ids == 0, ITMAX, counts)
    counts = jnp.where(row_ids == 1, 1, counts)
    return counts.astype(jnp.int32)


def shard_levels(rng, shape, split, smallest, largest):
    factor_of, own = 1.0, jax.random.fold_in(rng, 6)
    for position, blocks in split:
        draws = jnp.exp(jax.random.uniform(jax.random.fold_in(own, position), (blocks,), jnp.float32, smallest / len(split), largest / len(split)))
        factor_of = factor_of * jnp.repeat(draws, shape[position] // blocks).reshape([-1 if axis == position else 1 for axis in range(len(shape))])
    return factor_of


def noise(stream_key, dims, scale, most, cuts=(), kind=jnp.bfloat16):
    loudness = shard_levels(stream_key, dims, cuts, -0.22, 0.18) if cuts else 1.0
    drawn = jax.random.normal(stream_key, dims, jnp.float32) * scale * loudness
    return jnp.minimum(jnp.maximum(drawn, -most), most).astype(kind)


def setup_inputs(seed: int = 0) -> dict:
    splits = jax.random.split(jax.random.key(seed), 6)
    stress = noise(splits[0], (6, NZ, NODE, NODE, ELEMS), 0.5, 4.0, ((1, 8), (4, 64)), jnp.float32)
    velocity_grad = noise(splits[1], (9, NZ, NODE, NODE, ELEMS), 0.5, 4.0, ((1, 8), (4, 64)), jnp.float32)
    velocity = noise(splits[2], (2, NZ, NODE, NODE, ELEMS), 1.0, 4.0, ((1, 8), (4, 64)), jnp.float32)
    metric = jnp.clip(jnp.exp(math.log(3.0) - 2.3025851 * jax.random.uniform(splits[3], (3, NODE, NODE, ELEMS), jnp.float32) ** shard_levels(splits[3], (3, NODE, NODE, ELEMS), ((3, 64),), -0.2, 0.2)), 0.3, 3.0)
    iteration_counts = draw_iteration_counts(jax.random.fold_in(splits[5], 71), 0)
    return {"stress": stress, "velocity_grad": velocity_grad, "velocity": velocity, "metric": metric, "iteration_counts": iteration_counts}


HIGHEST = lax.Precision.HIGHEST
DT_STEP = 0.01
ETA_POLY = 0.5
RELAX_TIME = 1.0
SPAN_UNIT = 0.5
MASS_SCALE = 0.25
UPPER_PAIRS = ((0, 0), (1, 1), (2, 2), (0, 1), (0, 2), (1, 2))
COMPONENT_OF = {(0, 0): 0, (1, 1): 1, (2, 2): 2, (0, 1): 3, (1, 0): 3, (0, 2): 4, (2, 0): 4, (1, 2): 5, (2, 1): 5}

def node_tables():
    gll_nodes = np.array([-1.0, -0.830223896278567, -0.468848793470714, 0.0, 0.468848793470714, 0.830223896278567, 1.0])
    gll_weights = np.array([1.0 / 21.0, 0.276826047361566, 0.431745381209863, 0.487619047619048, 0.431745381209863, 0.276826047361566, 1.0 / 21.0])
    barycentric = np.array([1.0 / np.prod([gll_nodes[col_index] - gll_nodes[other_index] for other_index in range(7) if other_index != col_index]) for col_index in range(7)])
    derivative = np.zeros((7, 7))
    for row_index in range(7):
        for col_index in range(7):
            if row_index != col_index:
                derivative[row_index, col_index] = barycentric[col_index] / barycentric[row_index] / (gll_nodes[row_index] - gll_nodes[col_index])
        derivative[row_index, row_index] = -np.sum(derivative[row_index])
    return (jnp.asarray(derivative, jnp.float32), jnp.asarray(gll_weights, jnp.float32))

def span_tables(plane_count):
    row_ids = jnp.arange(plane_count, dtype=jnp.int32)
    harmonic = jnp.where(row_ids == 1, plane_count // 2, row_ids // 2)
    is_sine = (row_ids % 2 == 1) & (row_ids != 1)
    turns = harmonic[:, None] * row_ids[None, :] % plane_count
    phase = 2.0 * np.pi / plane_count * turns.astype(jnp.float32)
    basis = jnp.where(is_sine[:, None], jnp.sin(phase), jnp.cos(phase))
    scale_row = jnp.where(row_ids < 2, 1.0 / np.sqrt(plane_count), np.sqrt(2.0 / plane_count)).astype(jnp.float32)
    basis = basis * scale_row[:, None]
    wavenum = SPAN_UNIT * harmonic.astype(jnp.float32)
    partner = basis[jnp.bitwise_xor(row_ids, 1)]
    slope = jnp.where(row_ids < 2, 0.0, jnp.where(is_sine, -wavenum, wavenum)).astype(jnp.float32)
    return (basis, slope[:, None] * partner, wavenum)

def span_apply(matrix, field):
    return jnp.einsum('rz,z...->r...', matrix, field, precision=HIGHEST)

def along_first(matrix, field):
    return jnp.einsum('lm,...mjab->...ljab', matrix, field, precision=HIGHEST)

def along_second(matrix, field):
    return jnp.einsum('lm,...imab->...ilab', matrix, field, precision=HIGHEST)

def outside_traces(tau, from_left, from_right, from_below, from_above):
    left = jnp.concatenate([from_left[:, :, :, None, :], tau[:, :, 6, :, :-1, :]], axis=3)
    right = jnp.concatenate([tau[:, :, 0, :, 1:, :], from_right[:, :, :, None, :]], axis=3)
    below = jnp.concatenate([from_below[..., None], tau[:, :, :, 6, :, :-1]], axis=4)
    above = jnp.concatenate([tau[:, :, :, 0, :, 1:], from_above[..., None]], axis=4)
    return (left, right, below, above)

def forcing_terms(tau, grads):
    rows_out = []
    for first_axis, second_axis in UPPER_PAIRS:
        stretch = ETA_POLY * (grads[3 * first_axis + second_axis] + grads[3 * second_axis + first_axis])
        term_sum = (stretch - tau[COMPONENT_OF[first_axis, second_axis]]) / RELAX_TIME
        for inner_axis in range(3):
            term_sum = term_sum + grads[3 * first_axis + inner_axis] * tau[COMPONENT_OF[inner_axis, second_axis]]
            term_sum = term_sum + tau[COMPONENT_OF[first_axis, inner_axis]] * grads[3 * second_axis + inner_axis]
        rows_out.append(term_sum)
    return jnp.stack(rows_out)

def advance_stress(tau, grads, velocity_field, outside, deriv, weights):
    left, right, below, above = outside
    flow_speed = velocity_field[0]
    cross_speed = velocity_field[1]
    advect = flow_speed * (2.0 * along_first(deriv, tau)) + cross_speed * (2.0 * along_second(deriv, tau))
    lift = 2.0 / weights[0]
    advect = advect.at[:, :, 0].add(-lift * jnp.minimum(-flow_speed[:, 0], 0.0) * (tau[:, :, 0] - left))
    advect = advect.at[:, :, 6].add(-lift * jnp.minimum(flow_speed[:, 6], 0.0) * (tau[:, :, 6] - right))
    advect = advect.at[:, :, :, 0].add(-lift * jnp.minimum(-cross_speed[:, :, 0], 0.0) * (tau[:, :, :, 0] - below))
    advect = advect.at[:, :, :, 6].add(-lift * jnp.minimum(cross_speed[:, :, 6], 0.0) * (tau[:, :, :, 6] - above))
    return tau + DT_STEP * (forcing_terms(tau, grads) - advect)

def pressure_sources(tau, deriv):

    def grad_flow(field):
        return 2.0 * along_first(deriv, field)

    def grad_cross(field):
        return 2.0 * along_second(deriv, field)
    flux_flow = grad_flow(tau[0]) + grad_cross(tau[3])
    flux_cross = grad_flow(tau[3]) + grad_cross(tau[1])
    planar = grad_flow(flux_flow) + grad_cross(flux_cross)
    crossed = grad_flow(tau[4]) + grad_cross(tau[5])
    return jnp.stack([planar, crossed, tau[2]])

def quad_table(weights):
    return weights[:, None, None, None] * weights[None, :, None, None]

def share_table():
    node_ids = jnp.arange(7)
    edge_share = jnp.where((node_ids == 0) | (node_ids == 6), 0.5, 1.0).astype(jnp.float32)
    return edge_share[:, None, None, None] * edge_share[None, :, None, None]

def apply_operator(field, coef, wavesq, deriv, weights):
    quad = quad_table(weights)
    flux_first = along_first(deriv, field) * (quad * coef[0])
    flux_second = along_second(deriv, field) * (quad * coef[1])
    stiff_part = along_first(deriv.T, flux_first) + along_second(deriv.T, flux_second)
    return stiff_part + (MASS_SCALE * wavesq)[:, None, None, None, None] * (quad * coef[2]) * field

def join_first(field):
    joined = field[:, 6, :, :-1] + field[:, 0, :, 1:]
    return field.at[:, 6, :, :-1].set(joined).at[:, 0, :, 1:].set(joined)

def join_second(field):
    joined = field[:, :, 6, :, :-1] + field[:, :, 0, :, 1:]
    return field.at[:, :, 6, :, :-1].set(joined).at[:, :, 0, :, 1:].set(joined)

def interior_mask(first_count, second_count, low_first, high_first, low_second, high_second):
    node_ids = jnp.arange(7)
    first_ids = jnp.arange(first_count)
    second_ids = jnp.arange(second_count)
    left = (node_ids[:, None, None, None] == 0) & (first_ids[None, None, :, None] == 0) & low_first
    right = (node_ids[:, None, None, None] == 6) & (first_ids[None, None, :, None] == first_count - 1) & high_first
    bottom = (node_ids[None, :, None, None] == 0) & (second_ids[None, None, None, :] == 0) & low_second
    top = (node_ids[None, :, None, None] == 6) & (second_ids[None, None, None, :] == second_count - 1) & high_second
    return jnp.logical_not(left | right | bottom | top).astype(jnp.float32)

def weighted_dot(first, second, share):
    return lax.optimization_barrier(jnp.sum(first * second * share, axis=(1, 2, 3, 4)))

def to_grid(field):
    leading = field.shape[:-1]
    shaped = field.reshape(leading + (NDX, NDY, EX, EY))
    shaped = jnp.swapaxes(shaped, -3, -2)
    return shaped.reshape(leading + (NDX * EX, NDY * EY))

def from_grid(field):
    leading = field.shape[:-2]
    shaped = field.reshape(leading + (NDX, EX, NDY, EY))
    shaped = jnp.swapaxes(shaped, -3, -2)
    return shaped.reshape(leading + (NDX * NDY * EX * EY,))

def reference(stress, velocity_grad, velocity, metric, iteration_counts):
    deriv, weights = node_tables()
    tau = to_grid(stress)
    grads = to_grid(velocity_grad)
    velocity_field = to_grid(velocity)
    coef = to_grid(metric)
    slab_first = jnp.zeros(tau.shape[:3] + (tau.shape[5],), jnp.float32)
    slab_second = jnp.zeros(tau.shape[:3] + (tau.shape[4],), jnp.float32)
    outside = outside_traces(tau, slab_first, slab_first, slab_second, slab_second)
    new_tau = advance_stress(tau, grads, velocity_field, outside, deriv, weights)
    sources = pressure_sources(new_tau, deriv)
    basis, slope_basis, wavenum = span_tables(NZ)
    wavesq = wavenum * wavenum
    rows = span_apply(basis, sources[0]) - wavesq[:, None, None, None, None] * span_apply(basis, sources[2]) + 2.0 * span_apply(slope_basis, sources[1])
    mask = interior_mask(NDX * EX, NDY * EY, True, True, True, True)
    quad = quad_table(weights)
    rhs = mask * join_second(join_first(MASS_SCALE * quad * coef[2] * rows))
    share = share_table()
    solution = jnp.zeros_like(rhs)
    residual = rhs
    direction = rhs
    norm_now = weighted_dot(residual, residual, share)
    for sweep_index in range(ITMAX):
        active = iteration_counts > sweep_index
        image = mask * join_second(join_first(apply_operator(direction, coef, wavesq, deriv, weights)))
        step_size = jnp.where(active, norm_now / weighted_dot(direction, image, share), 0.0)
        solution = solution + step_size[:, None, None, None, None] * direction
        residual = residual - step_size[:, None, None, None, None] * image
        fresh = weighted_dot(residual, residual, share)
        direction = jnp.where(active[:, None, None, None, None], residual + (fresh / norm_now)[:, None, None, None, None] * direction, direction)
        norm_now = jnp.where(active, fresh, norm_now)
    pressure = span_apply(basis.T, solution)
    return (from_grid(new_tau), from_grid(pressure))
```

```python
import jax
import jax.numpy as jnp
import numpy as np
from jax import lax
from jax.experimental import pallas as pl
from jax.experimental.pallas import tpu as pltpu
from jax.sharding import Mesh
from jax.sharding import PartitionSpec as P

FLOW = ("z", "xh")
CROSS = ("xl", "core")
PLANE = ("z", "xh", "xl", "core")
SPREAD = ("z", "xl", "core")
ROWS = ("xh", "y")
SPLIT = (4, 4, 2, 2, 8)

EY = 16
NZ = 32
DT_STEP = 0.01
SPAN_UNIT = 0.5
MASS_SCALE = 0.25
MIB = 1 << 20


def node_tables():
    nodes = np.array(
        [-1.0, -0.830223896278567, -0.468848793470714, 0.0,
         0.468848793470714, 0.830223896278567, 1.0]
    )
    weights = np.array(
        [1.0 / 21.0, 0.276826047361566, 0.431745381209863, 0.487619047619048,
         0.431745381209863, 0.276826047361566, 1.0 / 21.0]
    )
    bary = np.array(
        [1.0 / np.prod([nodes[c] - nodes[o] for o in range(7) if o != c]) for c in range(7)]
    )
    deriv = np.zeros((7, 7))
    for row in range(7):
        for col in range(7):
            if row != col:
                deriv[row, col] = bary[col] / bary[row] / (nodes[row] - nodes[col])
        deriv[row, row] = -np.sum(deriv[row])
    return deriv, weights


DERIV, WEIGHTS = node_tables()
LIFT = 2.0 / WEIGHTS[0]


def span_tables():
    ids = np.arange(NZ)
    harmonic = np.where(ids == 1, NZ // 2, ids // 2)
    sine = (ids % 2 == 1) & (ids != 1)
    phase = 2.0 * np.pi / NZ * (harmonic[:, None] * ids[None, :] % NZ)
    basis = np.where(sine[:, None], np.sin(phase), np.cos(phase))
    basis = basis * np.where(ids < 2, 1.0 / np.sqrt(NZ), np.sqrt(2.0 / NZ))[:, None]
    wavenum = SPAN_UNIT * harmonic
    slope = np.where(ids < 2, 0.0, np.where(sine, -wavenum, wavenum))
    return basis, slope[:, None] * basis[ids ^ 1], wavenum


BASIS, SLOPE, WAVENUM = span_tables()
ROW_AT = np.array([4 * (q % 8) + q // 8 for q in range(NZ)])


def source_coefs():
    table = np.zeros((8, NZ, 3, 4))
    for y in range(8):
        cols = slice(4 * y, 4 * y + 4)
        table[y, :, 0] = BASIS[ROW_AT, cols]
        table[y, :, 1] = -(WAVENUM[ROW_AT] ** 2)[:, None] * BASIS[ROW_AT, cols]
        table[y, :, 2] = 2.0 * SLOPE[ROW_AT, cols]
    return table.astype(np.float32).reshape(-1)


def plane_coefs():
    table = np.stack([BASIS.T[4 * y : 4 * y + 4][:, ROW_AT] for y in range(8)])
    return table.astype(np.float32).reshape(-1)


def line_apply(mat, f):
    even = [f[m] + f[6 - m] for m in range(3)]
    odd = [f[m] - f[6 - m] for m in range(3)]
    out = [None] * 7
    for i in range(3):
        from_odd = float(0.5 * (mat[i, 0] - mat[i, 6])) * odd[0]
        from_even = float(mat[i, 3]) * f[3]
        for m in range(3):
            from_even = from_even + float(0.5 * (mat[i, m] + mat[i, 6 - m])) * even[m]
            if m:
                from_odd = from_odd + float(0.5 * (mat[i, m] - mat[i, 6 - m])) * odd[m]
        out[i] = from_odd + from_even
        out[6 - i] = from_odd - from_even
    out[3] = float(mat[3, 0]) * odd[0] + float(mat[3, 1]) * odd[1] + float(mat[3, 2]) * odd[2]
    return out


def tree_sum(terms):
    while len(terms) > 1:
        terms = [sum(terms[i : i + 2][1:], terms[i]) for i in range(0, len(terms), 2)]
    return terms[0]


def lanes():
    return lax.broadcasted_iota(jnp.int32, (8, 128), 1)


def pack_kernel(s_ref, right_ref, left_ref, up_ref, down_ref, t_ref):
    lane = lanes()
    block, inner = lane // 16, lane % 16

    def plane(z, carry):
        for c in range(6):
            for i in range(7):
                t_ref[c, i, 0:7, :] = s_ref[c, z, i]
        zero = jnp.zeros((8, 128), jnp.float32)
        right, left = zero, zero
        for c in range(6):
            right = jnp.where(block == c, pltpu.roll(t_ref[c, 6], (16 * (c + 1)) % 128, 1), right)
            left = jnp.where(block == c, pltpu.roll(t_ref[c, 0], 16 * c, 1), left)
        right_ref[z] = right
        left_ref[z] = left
        for i in range(7):
            up, down = zero, zero
            for c in range(6):
                up = jnp.where(inner == c, pltpu.roll(t_ref[c, i], (c - 15) % 128, 1), up)
                down = jnp.where(inner == c, pltpu.roll(t_ref[c, i], c, 1), down)
            up_ref[z, i : i + 1, :] = up[6:7, :]
            down_ref[z, i : i + 1, :] = down[0:1, :]
        up_ref[z, 7:8, :] = zero[0:1, :]
        down_ref[z, 7:8, :] = zero[0:1, :]
        return carry

    for c in range(6):
        for i in range(7):
            t_ref[c, i] = jnp.zeros((8, 128), jnp.float32)
    lax.fori_loop(0, 4, plane, 0)


def pack_faces(stress):
    return pl.pallas_call(
        pack_kernel,
        out_shape=[jax.ShapeDtypeStruct((4, 8, 128), jnp.float32)] * 4,
        in_specs=[pl.BlockSpec(memory_space=pltpu.VMEM)],
        out_specs=[pl.BlockSpec(memory_space=pltpu.VMEM)] * 4,
        scratch_shapes=[pltpu.VMEM((6, 7, 8, 128), jnp.float32)],
        compiler_params=pltpu.CompilerParams(vmem_limit_bytes=16 * MIB),
    )(stress)


def stress_kernel(
    coef_ref, s_ref, g_ref, v_ref, left_ref, right_ref, below_ref, above_ref, dcol_ref,
    new_ref, rows_ref, t_ref, d_ref, n_ref, f_ref, p_ref, lb_ref,
):
    lane = lanes()
    inner = lane % 16
    row = lax.broadcasted_iota(jnp.int32, (8, 128), 0)
    twice = 2.0 * DERIV
    y = lax.axis_index("y")

    def across(ref, *at):
        total = dcol_ref[0] * ref[(*at, pl.ds(0, 1), slice(None))]
        for m in range(1, 7):
            total = total + dcol_ref[m] * ref[(*at, pl.ds(m, 1), slice(None))]
        return total

    zero = jnp.zeros((8, 128), jnp.float32)
    for i in range(7):
        for c in range(6):
            t_ref[c, i] = zero
        for c in range(11):
            lb_ref[c, i] = zero

    def plane(z, carry):
        for i in range(7):
            for c in range(6):
                t_ref[c, i, 0:7, :] = s_ref[c, z, i]
            for c in range(9):
                lb_ref[c, i, 0:7, :] = g_ref[c, z, i]
            for c in range(2):
                lb_ref[9 + c, i, 0:7, :] = v_ref[c, z, i]
        for c in range(6):
            slope = line_apply(twice, [t_ref[c, i] for i in range(7)])
            for i in range(7):
                d_ref[c, i] = slope[i]
        for i in range(7):
            u, v = lb_ref[9, i], lb_ref[10, i]
            away = jnp.where(row == 0, -v, v)
            away = jnp.where((row == 0) | (row == 6), jnp.minimum(away, 0.0), 0.0) * float(-LIFT)
            if i == 0:
                along = jnp.minimum(-u, 0.0) * float(-LIFT)
            if i == 6:
                along = jnp.minimum(u, 0.0) * float(-LIFT)
            grad = [lb_ref[c, i] for c in range(9)]
            tau = [t_ref[c, i] for c in range(6)]
            xx, yy, zz = tau[0] + 0.5, tau[1] + 0.5, tau[2] + 0.5
            full = ((xx, tau[3], tau[4]), (tau[3], yy, tau[5]), (tau[4], tau[5], zz))
            prod = [
                [tree_sum([grad[3 * a + k] * full[k][b] for k in range(3)]) for b in range(3)]
                for a in range(3)
            ]
            pairs = ((0, 0), (1, 1), (2, 2), (0, 1), (0, 2), (1, 2))
            for c, (a, b) in enumerate(pairs):
                forcing = prod[a][b] + prod[b][a] - tau[c]
                advect = u * d_ref[c, i] + v * across(t_ref, c, i)
                low = jnp.broadcast_to(t_ref[c, i, 6:7, :], (8, 128))
                low = pltpu.roll(low, 1, 1)
                got = jnp.broadcast_to(below_ref[z, i : i + 1, :], (8, 128))
                low = jnp.where(inner == 0, pltpu.roll(got, (128 - c) % 128, 1), low)
                high = jnp.broadcast_to(t_ref[c, i, 0:1, :], (8, 128))
                high = pltpu.roll(high, 127, 1)
                got = jnp.broadcast_to(above_ref[z, i : i + 1, :], (8, 128))
                high = jnp.where(inner == 15, pltpu.roll(got, 15 - c, 1), high)
                advect = advect + away * (tau[c] - jnp.where(row == 0, low, high))
                if i == 0:
                    mine = pltpu.roll(t_ref[c, 6], 16, 1)
                    got = pltpu.roll(left_ref[z], (128 - 16 * c) % 128, 1)
                    advect = advect + along * (tau[c] - jnp.where(lane < 16, got, mine))
                if i == 6:
                    mine = pltpu.roll(t_ref[c, 0], 112, 1)
                    got = pltpu.roll(right_ref[z], 112 - 16 * c, 1)
                    advect = advect + along * (tau[c] - jnp.where(lane >= 112, got, mine))
                fresh = tau[c] + DT_STEP * (forcing - advect)
                n_ref[c, i] = fresh
                new_ref[c, z, i] = fresh[0:7, :]
        first = line_apply(twice, [n_ref[0, i] for i in range(7)])
        first = [first[i] + across(n_ref, 3, i) for i in range(7)]
        planar = line_apply(twice, first)
        second = line_apply(twice, [n_ref[3, i] for i in range(7)])
        for i in range(7):
            f_ref[i] = second[i] + across(n_ref, 1, i)
        crossed = line_apply(twice, [n_ref[4, i] for i in range(7)])
        for i in range(7):
            p_ref[0, z, i] = planar[i] + across(f_ref, i)
            p_ref[1, z, i] = n_ref[2, i]
            p_ref[2, z, i] = crossed[i] + across(n_ref, 5, i)
        return carry

    lax.fori_loop(0, 4, plane, 0)

    def one_row(q, carry):
        base = (y * NZ + q) * 12
        coefs = [coef_ref[base + k] for k in range(12)]
        for i in range(7):
            rows_ref[q, i] = tree_sum(
                [coefs[4 * s + z] * p_ref[s, z, i] for s in range(3) for z in range(4)]
            )
        return carry

    lax.fori_loop(0, NZ, one_row, 0)


def stress_step(stress, grad, velocity, faces):
    dcol = np.zeros((7, 8, 128))
    dcol[:, :7, :] = 2.0 * DERIV.T[:, :, None]
    vmem = pl.BlockSpec(memory_space=pltpu.VMEM)
    return pl.pallas_call(
        stress_kernel,
        out_shape=[
            jax.ShapeDtypeStruct((6, 4, 7, 7, 128), jnp.float32),
            jax.ShapeDtypeStruct((NZ, 7, 8, 128), jnp.float32),
        ],
        in_specs=[pl.BlockSpec(memory_space=pltpu.SMEM)] + [vmem] * 8,
        out_specs=[vmem] * 2,
        scratch_shapes=[
            pltpu.VMEM((6, 7, 8, 128), jnp.float32),
            pltpu.VMEM((6, 7, 8, 128), jnp.float32),
            pltpu.VMEM((6, 7, 8, 128), jnp.float32),
            pltpu.VMEM((7, 8, 128), jnp.float32),
            pltpu.VMEM((3, 4, 7, 8, 128), jnp.float32),
            pltpu.VMEM((11, 7, 8, 128), jnp.float32),
        ],
        compiler_params=pltpu.CompilerParams(vmem_limit_bytes=24 * MIB),
    )(
        jnp.asarray(source_coefs()), stress, grad, velocity, *faces,
        jnp.asarray(dcol, jnp.float32),
    )


def turn(load, k, i, store):
    block = jnp.stack([load(k, s, i) for s in range(8)])
    block = jnp.swapaxes(block, 0, 1)
    for j in range(7):
        store(i * 7 + j, k, block[j])


def metric_kernel(m_ref, q_ref):
    def chunk(k, carry):
        here = pl.ds(pl.multiple_of(k * 8, 8), 8)
        for c in range(3):
            for i in range(7):
                def load(k, s, i):
                    return m_ref[((k % 2) * 8 + s) * 4 + k // 2, c, i]

                def store(n, k, value):
                    scale = WEIGHTS[n // 7] * WEIGHTS[n % 7] * (MASS_SCALE if c == 2 else 1.0)
                    q_ref[c, n, here, :] = float(scale) * value

                turn(load, k, i, store)
        return carry

    lax.fori_loop(0, 8, chunk, 0)


def metric_fields(gathered):
    vmem = pl.BlockSpec(memory_space=pltpu.VMEM)
    return pl.pallas_call(
        metric_kernel,
        out_shape=jax.ShapeDtypeStruct((3, 49, 64, 128), jnp.float32),
        in_specs=[vmem],
        out_specs=vmem,
        compiler_params=pltpu.CompilerParams(vmem_limit_bytes=24 * MIB),
    )(gathered)


def solve_kernel(count_ref, rows_ref, q_ref, out_ref, r_ref, d_ref, im_ref, mk_ref, x_ref, t_ref):
    z, xh, y = lax.axis_index("z"), lax.axis_index("xh"), lax.axis_index("y")
    e = lax.axis_index("xl") * 2 + lax.axis_index("core")
    row_id = 4 * y + xh
    harmonic = jnp.where(row_id == 1, NZ // 2, row_id // 2).astype(jnp.float32)
    wavesq = harmonic * harmonic * (SPAN_UNIT * SPAN_UNIT)
    own = pl.ds(pl.multiple_of((e * 2 + z // 2) * 8, 8), 8)
    flipped = DERIV.T
    zero = jnp.zeros((8, 128), jnp.float32)

    def here(k):
        return pl.ds(pl.multiple_of(k * 8, 8), 8)

    def chunk_in(k, carry):
        def load(k, s, i):
            return rows_ref[(k % 2) * 2 + s // 4, k // 2, s % 4, i]

        def store(n, k, value):
            mass = q_ref[2, n, here(k), :]
            im_ref[n, here(k), :] = mass * value
            mk_ref[n, here(k), :] = wavesq * mass
            d_ref[n, here(k), :] = zero

        for i in range(7):
            turn(load, k, i, store)
        return carry

    lax.fori_loop(0, 8, chunk_in, 0)
    for n in range(49):
        x_ref[n] = zero

    lane = lax.broadcasted_iota(jnp.int32, (64, 128), 1)
    spot = lax.broadcasted_iota(jnp.int32, (64, 128), 0)
    inner, c_pos = lane % 16, spot % 16
    wall = (
        (c_pos == 0) & (lane < 16),
        (c_pos == 15) & (lane >= 112),
        (spot < 16) & (inner == 0),
        (spot >= 48) & (inner == 15),
    )

    def join():
        for j in range(7):
            low, high = im_ref[j], im_ref[42 + j]
            moved = pltpu.roll(high, 16, 1)
            moved = jnp.where(lane < 16, pltpu.roll(moved, 1, 0), moved)
            back = pltpu.roll(low, 112, 1)
            back = jnp.where(lane >= 112, pltpu.roll(back, 63, 0), back)
            im_ref[j] = jnp.where(wall[0], 0.0, low + moved)
            im_ref[42 + j] = jnp.where(wall[1], 0.0, high + back)
        for i in range(7):
            low, high = im_ref[7 * i], im_ref[7 * i + 6]
            other = pltpu.roll(pltpu.roll(high, 113, 1), 16, 0)
            moved = jnp.where(inner == 0, other, pltpu.roll(high, 1, 1))
            other = pltpu.roll(pltpu.roll(low, 15, 1), 48, 0)
            back = jnp.where(inner == 15, other, pltpu.roll(low, 127, 1))
            im_ref[7 * i] = jnp.where(wall[2], 0.0, low + moved)
            im_ref[7 * i + 6] = jnp.where(wall[3], 0.0, high + back)

    def total(acc):
        return jnp.broadcast_to(jnp.sum(acc, axis=(0, 1), keepdims=True), (8, 128))

    def square(line, ends):
        inside = tree_sum([line[m] * line[m] for m in range(1, 6)])
        return ends * (inside + 0.5 * (line[0] * line[0] + line[6] * line[6]))

    def set_residual(k, acc):
        for i in range(7):
            line = []
            for j in range(7):
                value = im_ref[i * 7 + j, here(k), :]
                r_ref[i * 7 + j, here(k), :] = value
                line.append(value)
            acc = acc + square(line, 0.5 if i in (0, 6) else 1.0)
        return acc

    join()
    rho = total(lax.fori_loop(0, 8, set_residual, zero))

    def sweep(t, state):
        rho, beta = state

        def image(k, acc):
            at = here(k)
            for j in range(7):
                line = []
                for i in range(7):
                    n = i * 7 + j
                    value = r_ref[n, at, :] + beta * d_ref[n, at, :]
                    d_ref[n, at, :] = value
                    line.append(value)
                flux = line_apply(DERIV, line)
                flux = [flux[i] * q_ref[0, i * 7 + j, at, :] for i in range(7)]
                part = line_apply(flipped, flux)
                for i in range(7):
                    n = i * 7 + j
                    part[i] = part[i] + mk_ref[n, at, :] * line[i]
                    im_ref[n, at, :] = part[i]
                acc = acc + tree_sum([part[i] * line[i] for i in range(7)])
            for i in range(7):
                line = [d_ref[i * 7 + j, at, :] for j in range(7)]
                flux = line_apply(DERIV, line)
                flux = [flux[j] * q_ref[1, i * 7 + j, at, :] for j in range(7)]
                part = line_apply(flipped, flux)
                for j in range(7):
                    n = i * 7 + j
                    im_ref[n, at, :] = im_ref[n, at, :] + part[j]
                acc = acc + tree_sum([part[j] * line[j] for j in range(7)])
            return acc

        step = rho / total(lax.fori_loop(0, 8, image, zero))
        join()
        for n in range(49):
            x_ref[n] = x_ref[n] + step * d_ref[n, own, :]

        def descend(k, acc):
            at = here(k)
            for i in range(7):
                line = []
                for j in range(7):
                    n = i * 7 + j
                    value = r_ref[n, at, :] - step * im_ref[n, at, :]
                    r_ref[n, at, :] = value
                    line.append(value)
                acc = acc + square(line, 0.5 if i in (0, 6) else 1.0)
            return acc

        fresh = total(lax.fori_loop(0, 8, descend, zero))
        return fresh, fresh / rho

    lax.fori_loop(0, count_ref[row_id], sweep, (rho, zero))

    for i in range(7):
        block = jnp.stack([x_ref[i * 7 + j] for j in range(7)] + [zero])
        block = jnp.swapaxes(block, 0, 1)
        for s in range(8):
            t_ref[s, i] = block[s]
    first = (z % 2) * 4
    for to in range(4):
        for i in range(7):
            value = t_ref[first + to, i]
            for copy in range(8):
                out_ref[to * 8 + copy, i] = value


def solve(counts, rows, metrics):
    vmem = pl.BlockSpec(memory_space=pltpu.VMEM)
    field = pltpu.VMEM((49, 64, 128), jnp.float32)
    return pl.pallas_call(
        solve_kernel,
        out_shape=jax.ShapeDtypeStruct((NZ, 7, 8, 128), jnp.float32),
        in_specs=[pl.BlockSpec(memory_space=pltpu.SMEM), vmem, vmem],
        out_specs=vmem,
        scratch_shapes=[
            field, field, field, field,
            pltpu.VMEM((49, 8, 128), jnp.float32),
            pltpu.VMEM((8, 7, 8, 128), jnp.float32),
        ],
        compiler_params=pltpu.CompilerParams(vmem_limit_bytes=40 * MIB),
    )(counts, rows, metrics)


def pressure_kernel(coef_ref, rows_ref, out_ref):
    y = lax.axis_index("y")
    for zl in range(4):
        coefs = [coef_ref[(y * 4 + zl) * NZ + q] for q in range(NZ)]
        for i in range(7):
            value = tree_sum([coefs[q] * rows_ref[q, i] for q in range(NZ)])
            out_ref[zl, i] = value[0:7, :]


def pressure_planes(rows):
    vmem = pl.BlockSpec(memory_space=pltpu.VMEM)
    return pl.pallas_call(
        pressure_kernel,
        out_shape=jax.ShapeDtypeStruct((4, 7, 7, 128), jnp.float32),
        in_specs=[pl.BlockSpec(memory_space=pltpu.SMEM), vmem],
        out_specs=vmem,
        compiler_params=pltpu.CompilerParams(vmem_limit_bytes=16 * MIB),
    )(jnp.asarray(plane_coefs()), rows)


def local(stress, velocity_grad, velocity, metric, iteration_counts):
    padded = jnp.pad(metric, ((0, 0), (0, 0), (0, 1), (0, 0)))
    gathered = lax.all_gather(padded, PLANE)
    metrics = metric_fields(gathered)
    right, left, up, down = pack_faces(stress)
    ahead = [(c, c + 1) for c in range(15)]
    above = [(e, e + 1) for e in range(3)]
    faces = (
        lax.ppermute(right, FLOW, ahead),
        lax.ppermute(left, FLOW, [(b, a) for a, b in ahead]),
        lax.ppermute(up, CROSS, above),
        lax.ppermute(down, CROSS, [(b, a) for a, b in above]),
    )
    new_stress, parts = stress_step(stress, velocity_grad, velocity, faces)
    parts = lax.all_to_all(parts, ROWS, 0, 0, tiled=True)
    mine = jnp.sum(parts.reshape(4, 8, 7, 8, 128), axis=1)
    whole = lax.all_gather(mine, SPREAD)
    whole = whole.reshape(4, 4, 4, 7, 8, 128)
    answer = solve(iteration_counts, whole, metrics)
    answer = lax.all_to_all(answer, ROWS, 0, 0, tiled=True)
    return new_stress, pressure_planes(answer)


def solution(mesh):
    fine = Mesh(mesh.devices.reshape(SPLIT), PLANE + ("y",))
    field = P(None, "y", None, None, PLANE)
    return jax.shard_map(
        local,
        mesh=fine,
        in_specs=(field, field, field, P(None, None, None, PLANE), P()),
        out_specs=(field, P("y", None, None, PLANE)),
        check_vma=False,
    )
```

```python
import jax
import jax.numpy as jnp
import numpy as np
from jax import lax
from jax.experimental import pallas as pl
from jax.experimental.pallas import tpu as pltpu
from jax.sharding import Mesh
from jax.sharding import PartitionSpec as P

FLOW = ("z", "xh")
CROSS = ("xl", "core")
PLANE = ("z", "xh", "xl", "core")
SPREAD = ("z", "xl", "core")
ROWS = ("xh", "y")
SPLIT = (4, 4, 2, 2, 8)

EY = 16
NZ = 32
DT_STEP = 0.01
SPAN_UNIT = 0.5
MASS_SCALE = 0.25
MIB = 1 << 20


def node_tables():
    nodes = np.array(
        [-1.0, -0.830223896278567, -0.468848793470714, 0.0,
         0.468848793470714, 0.830223896278567, 1.0]
    )
    weights = np.array(
        [1.0 / 21.0, 0.276826047361566, 0.431745381209863, 0.487619047619048,
         0.431745381209863, 0.276826047361566, 1.0 / 21.0]
    )
    bary = np.array(
        [1.0 / np.prod([nodes[c] - nodes[o] for o in range(7) if o != c]) for c in range(7)]
    )
    deriv = np.zeros((7, 7))
    for row in range(7):
        for col in range(7):
            if row != col:
                deriv[row, col] = bary[col] / bary[row] / (nodes[row] - nodes[col])
        deriv[row, row] = -np.sum(deriv[row])
    return deriv, weights


DERIV, WEIGHTS = node_tables()
LIFT = 2.0 / WEIGHTS[0]


def span_tables():
    ids = np.arange(NZ)
    harmonic = np.where(ids == 1, NZ // 2, ids // 2)
    sine = (ids % 2 == 1) & (ids != 1)
    phase = 2.0 * np.pi / NZ * (harmonic[:, None] * ids[None, :] % NZ)
    basis = np.where(sine[:, None], np.sin(phase), np.cos(phase))
    basis = basis * np.where(ids < 2, 1.0 / np.sqrt(NZ), np.sqrt(2.0 / NZ))[:, None]
    wavenum = SPAN_UNIT * harmonic
    slope = np.where(ids < 2, 0.0, np.where(sine, -wavenum, wavenum))
    return basis, slope[:, None] * basis[ids ^ 1], wavenum


BASIS, SLOPE, WAVENUM = span_tables()
ROW_AT = np.array([4 * (q % 8) + q // 8 for q in range(NZ)])


def source_coefs():
    table = np.zeros((8, NZ, 3, 4))
    for y in range(8):
        cols = slice(4 * y, 4 * y + 4)
        table[y, :, 0] = BASIS[ROW_AT, cols]
        table[y, :, 1] = -(WAVENUM[ROW_AT] ** 2)[:, None] * BASIS[ROW_AT, cols]
        table[y, :, 2] = 2.0 * SLOPE[ROW_AT, cols]
    return table.astype(np.float32).reshape(-1)


def plane_coefs():
    table = np.stack([BASIS.T[4 * y : 4 * y + 4][:, ROW_AT] for y in range(8)])
    return table.astype(np.float32).reshape(-1)


def line_apply(mat, f):
    even = [f[m] + f[6 - m] for m in range(3)]
    odd = [f[m] - f[6 - m] for m in range(3)]
    out = [None] * 7
    for i in range(3):
        from_odd = float(0.5 * (mat[i, 0] - mat[i, 6])) * odd[0]
        from_even = float(mat[i, 3]) * f[3]
        for m in range(3):
            from_even = from_even + float(0.5 * (mat[i, m] + mat[i, 6 - m])) * even[m]
            if m:
                from_odd = from_odd + float(0.5 * (mat[i, m] - mat[i, 6 - m])) * odd[m]
        out[i] = from_odd + from_even
        out[6 - i] = from_odd - from_even
    out[3] = float(mat[3, 0]) * odd[0] + float(mat[3, 1]) * odd[1] + float(mat[3, 2]) * odd[2]
    return out


def tree_sum(terms):
    while len(terms) > 1:
        terms = [sum(terms[i : i + 2][1:], terms[i]) for i in range(0, len(terms), 2)]
    return terms[0]


def lanes():
    return lax.broadcasted_iota(jnp.int32, (8, 128), 1)


def pack_kernel(s_ref, right_ref, left_ref, up_ref, down_ref, t_ref):
    lane = lanes()
    block, inner = lane // 16, lane % 16

    def plane(z, carry):
        for c in range(6):
            for i in range(7):
                t_ref[c, i, 0:7, :] = s_ref[c, z, i]
        zero = jnp.zeros((8, 128), jnp.float32)
        right, left = zero, zero
        for c in range(6):
            right = jnp.where(block == c, pltpu.roll(t_ref[c, 6], (16 * (c + 1)) % 128, 1), right)
            left = jnp.where(block == c, pltpu.roll(t_ref[c, 0], 16 * c, 1), left)
        right_ref[z] = right
        left_ref[z] = left
        for i in range(7):
            up, down = zero, zero
            for c in range(6):
                up = jnp.where(inner == c, pltpu.roll(t_ref[c, i], (c - 15) % 128, 1), up)
                down = jnp.where(inner == c, pltpu.roll(t_ref[c, i], c, 1), down)
            up_ref[z, i : i + 1, :] = up[6:7, :]
            down_ref[z, i : i + 1, :] = down[0:1, :]
        up_ref[z, 7:8, :] = zero[0:1, :]
        down_ref[z, 7:8, :] = zero[0:1, :]
        return carry

    for c in range(6):
        for i in range(7):
            t_ref[c, i] = jnp.zeros((8, 128), jnp.float32)
    lax.fori_loop(0, 4, plane, 0)


def pack_faces(stress):
    return pl.pallas_call(
        pack_kernel,
        out_shape=[jax.ShapeDtypeStruct((4, 8, 128), jnp.float32)] * 4,
        in_specs=[pl.BlockSpec(memory_space=pltpu.VMEM)],
        out_specs=[pl.BlockSpec(memory_space=pltpu.VMEM)] * 4,
        scratch_shapes=[pltpu.VMEM((6, 7, 8, 128), jnp.float32)],
        compiler_params=pltpu.CompilerParams(vmem_limit_bytes=16 * MIB),
    )(stress)


def stress_kernel(
    coef_ref, s_ref, g_ref, v_ref, left_ref, right_ref, below_ref, above_ref, dcol_ref,
    new_ref, rows_ref, t_ref, d_ref, n_ref, f_ref, p_ref, lb_ref,
):
    lane = lanes()
    inner = lane % 16
    row = lax.broadcasted_iota(jnp.int32, (8, 128), 0)
    twice = 2.0 * DERIV
    y = lax.axis_index("y")

    def across(ref, *at):
        total = dcol_ref[0] * ref[(*at, pl.ds(0, 1), slice(None))]
        for m in range(1, 7):
            total = total + dcol_ref[m] * ref[(*at, pl.ds(m, 1), slice(None))]
        return total

    zero = jnp.zeros((8, 128), jnp.float32)
    for i in range(7):
        for c in range(6):
            t_ref[c, i] = zero
        for c in range(11):
            lb_ref[c, i] = zero

    def plane(z, carry):
        for i in range(7):
            for c in range(6):
                t_ref[c, i, 0:7, :] = s_ref[c, z, i]
            for c in range(9):
                lb_ref[c, i, 0:7, :] = g_ref[c, z, i]
            for c in range(2):
                lb_ref[9 + c, i, 0:7, :] = v_ref[c, z, i]
        for c in range(6):
            slope = line_apply(twice, [t_ref[c, i] for i in range(7)])
            for i in range(7):
                d_ref[c, i] = slope[i]
        for i in range(7):
            u, v = lb_ref[9, i], lb_ref[10, i]
            away = jnp.where(row == 0, -v, v)
            away = jnp.where((row == 0) | (row == 6), jnp.minimum(away, 0.0), 0.0) * float(-LIFT)
            if i == 0:
                along = jnp.minimum(-u, 0.0) * float(-LIFT)
            if i == 6:
                along = jnp.minimum(u, 0.0) * float(-LIFT)
            grad = [lb_ref[c, i] for c in range(9)]
            tau = [t_ref[c, i] for c in range(6)]
            xx, yy, zz = tau[0] + 0.5, tau[1] + 0.5, tau[2] + 0.5
            full = ((xx, tau[3], tau[4]), (tau[3], yy, tau[5]), (tau[4], tau[5], zz))
            prod = [
                [tree_sum([grad[3 * a + k] * full[k][b] for k in range(3)]) for b in range(3)]
                for a in range(3)
            ]
            pairs = ((0, 0), (1, 1), (2, 2), (0, 1), (0, 2), (1, 2))
            for c, (a, b) in enumerate(pairs):
                forcing = prod[a][b] + prod[b][a] - tau[c]
                advect = u * d_ref[c, i] + v * across(t_ref, c, i)
                low = jnp.broadcast_to(t_ref[c, i, 6:7, :], (8, 128))
                low = pltpu.roll(low, 1, 1)
                got = jnp.broadcast_to(below_ref[z, i : i + 1, :], (8, 128))
                low = jnp.where(inner == 0, pltpu.roll(got, (128 - c) % 128, 1), low)
                high = jnp.broadcast_to(t_ref[c, i, 0:1, :], (8, 128))
                high = pltpu.roll(high, 127, 1)
                got = jnp.broadcast_to(above_ref[z, i : i + 1, :], (8, 128))
                high = jnp.where(inner == 15, pltpu.roll(got, 15 - c, 1), high)
                advect = advect + away * (tau[c] - jnp.where(row == 0, low, high))
                if i == 0:
                    mine = pltpu.roll(t_ref[c, 6], 16, 1)
                    got = pltpu.roll(left_ref[z], (128 - 16 * c) % 128, 1)
                    advect = advect + along * (tau[c] - jnp.where(lane < 16, got, mine))
                if i == 6:
                    mine = pltpu.roll(t_ref[c, 0], 112, 1)
                    got = pltpu.roll(right_ref[z], 112 - 16 * c, 1)
                    advect = advect + along * (tau[c] - jnp.where(lane >= 112, got, mine))
                fresh = tau[c] + DT_STEP * (forcing - advect)
                n_ref[c, i] = fresh
                new_ref[c, z, i] = fresh[0:7, :]
        first = line_apply(twice, [n_ref[0, i] for i in range(7)])
        first = [first[i] + across(n_ref, 3, i) for i in range(7)]
        planar = line_apply(twice, first)
        second = line_apply(twice, [n_ref[3, i] for i in range(7)])
        for i in range(7):
            f_ref[i] = second[i] + across(n_ref, 1, i)
        crossed = line_apply(twice, [n_ref[4, i] for i in range(7)])
        for i in range(7):
            p_ref[0, z, i] = planar[i] + across(f_ref, i)
            p_ref[1, z, i] = n_ref[2, i]
            p_ref[2, z, i] = crossed[i] + across(n_ref, 5, i)
        return carry

    lax.fori_loop(0, 4, plane, 0)

    def one_row(q, carry):
        base = (y * NZ + q) * 12
        coefs = [coef_ref[base + k] for k in range(12)]
        for i in range(7):
            rows_ref[q, i] = tree_sum(
                [coefs[4 * s + z] * p_ref[s, z, i] for s in range(3) for z in range(4)]
            )
        return carry

    lax.fori_loop(0, NZ, one_row, 0)


def stress_step(stress, grad, velocity, faces):
    dcol = np.zeros((7, 8, 128))
    dcol[:, :7, :] = 2.0 * DERIV.T[:, :, None]
    vmem = pl.BlockSpec(memory_space=pltpu.VMEM)
    return pl.pallas_call(
        stress_kernel,
        out_shape=[
            jax.ShapeDtypeStruct((6, 4, 7, 7, 128), jnp.float32),
            jax.ShapeDtypeStruct((NZ, 7, 8, 128), jnp.float32),
        ],
        in_specs=[pl.BlockSpec(memory_space=pltpu.SMEM)] + [vmem] * 8,
        out_specs=[vmem] * 2,
        scratch_shapes=[
            pltpu.VMEM((6, 7, 8, 128), jnp.float32),
            pltpu.VMEM((6, 7, 8, 128), jnp.float32),
            pltpu.VMEM((6, 7, 8, 128), jnp.float32),
            pltpu.VMEM((7, 8, 128), jnp.float32),
            pltpu.VMEM((3, 4, 7, 8, 128), jnp.float32),
            pltpu.VMEM((11, 7, 8, 128), jnp.float32),
        ],
        compiler_params=pltpu.CompilerParams(vmem_limit_bytes=24 * MIB),
    )(
        jnp.asarray(source_coefs()), stress, grad, velocity, *faces,
        jnp.asarray(dcol, jnp.float32),
    )


def metric_kernel(m_ref, q_ref):
    def chunk(k, carry):
        here = pl.ds(pl.multiple_of(k * 8, 8), 8)
        source = [((k % 2) * 8 + s) * 4 + k // 2 for s in range(8)]
        for tile in range(19):
            block = jnp.stack([m_ref[at, 8 * tile : 8 * tile + 8, :] for at in source])
            block = jnp.swapaxes(block, 0, 1)
            for j in range(8):
                c, n = divmod(8 * tile + j, 49)
                if c < 3:
                    scale = WEIGHTS[n // 7] * WEIGHTS[n % 7] * (MASS_SCALE if c == 2 else 1.0)
                    q_ref[c, n, here, :] = float(scale) * block[j]
        return carry

    lax.fori_loop(0, 8, chunk, 0)


def metric_fields(gathered):
    vmem = pl.BlockSpec(memory_space=pltpu.VMEM)
    return pl.pallas_call(
        metric_kernel,
        out_shape=jax.ShapeDtypeStruct((3, 49, 64, 128), jnp.float32),
        in_specs=[vmem],
        out_specs=vmem,
        compiler_params=pltpu.CompilerParams(vmem_limit_bytes=24 * MIB),
    )(gathered)


def solve_kernel(
    count_ref, same_ref, other_ref, q_ref, out_ref, r_ref, d_ref, im_ref, mk_ref, x_ref, t_ref
):
    z, xh, y = lax.axis_index("z"), lax.axis_index("xh"), lax.axis_index("y")
    xl, core = lax.axis_index("xl"), lax.axis_index("core")
    e = xl * 2 + core
    row_id = 4 * y + xh
    harmonic = jnp.where(row_id == 1, NZ // 2, row_id // 2).astype(jnp.float32)
    wavesq = harmonic * harmonic * (SPAN_UNIT * SPAN_UNIT)
    own = pl.ds(pl.multiple_of((e * 2 + z // 2) * 8, 8), 8)
    flipped = DERIV.T
    zero = jnp.zeros((8, 128), jnp.float32)

    def here(k):
        return pl.ds(pl.multiple_of(k * 8, 8), 8)

    def chunk_in(quarter, carry):
        from_xl, half = quarter // 2, quarter % 2
        for ref, from_core in ((same_ref, core), (other_ref, 1 - core)):
            at = here((from_xl * 2 + from_core) * 2 + half)
            flip = (xl + from_xl) % 2
            back = [(z - half * 2 - s + 4) % 4 for s in range(2)]
            for i in range(7):
                block = jnp.stack([ref[flip, back[s // 4], s % 4, i] for s in range(8)])
                block = jnp.swapaxes(block, 0, 1)
                for j in range(7):
                    n = i * 7 + j
                    mass = q_ref[2, n, at, :]
                    im_ref[n, at, :] = mass * block[j]
                    mk_ref[n, at, :] = wavesq * mass
                    d_ref[n, at, :] = zero
        return carry

    lax.fori_loop(0, 4, chunk_in, 0)
    for n in range(49):
        x_ref[n] = zero

    lane = lax.broadcasted_iota(jnp.int32, (64, 128), 1)
    spot = lax.broadcasted_iota(jnp.int32, (64, 128), 0)
    inner, c_pos = lane % 16, spot % 16
    wall = (
        (c_pos == 0) & (lane < 16),
        (c_pos == 15) & (lane >= 112),
        (spot < 16) & (inner == 0),
        (spot >= 48) & (inner == 15),
    )

    def join():
        for j in range(7):
            low, high = im_ref[j], im_ref[42 + j]
            moved = pltpu.roll(high, 16, 1)
            moved = jnp.where(lane < 16, pltpu.roll(moved, 1, 0), moved)
            back = pltpu.roll(low, 112, 1)
            back = jnp.where(lane >= 112, pltpu.roll(back, 63, 0), back)
            im_ref[j] = jnp.where(wall[0], 0.0, low + moved)
            im_ref[42 + j] = jnp.where(wall[1], 0.0, high + back)
        for i in range(7):
            low, high = im_ref[7 * i], im_ref[7 * i + 6]
            other = pltpu.roll(pltpu.roll(high, 113, 1), 16, 0)
            moved = jnp.where(inner == 0, other, pltpu.roll(high, 1, 1))
            other = pltpu.roll(pltpu.roll(low, 15, 1), 48, 0)
            back = jnp.where(inner == 15, other, pltpu.roll(low, 127, 1))
            im_ref[7 * i] = jnp.where(wall[2], 0.0, low + moved)
            im_ref[7 * i + 6] = jnp.where(wall[3], 0.0, high + back)

    def total(acc):
        return jnp.broadcast_to(jnp.sum(acc, axis=(0, 1), keepdims=True), (8, 128))

    def square(line, ends):
        inside = tree_sum([line[m] * line[m] for m in range(1, 6)])
        return ends * (inside + 0.5 * (line[0] * line[0] + line[6] * line[6]))

    def set_residual(k, acc):
        for i in range(7):
            line = []
            for j in range(7):
                value = im_ref[i * 7 + j, here(k), :]
                r_ref[i * 7 + j, here(k), :] = value
                line.append(value)
            acc = acc + square(line, 0.5 if i in (0, 6) else 1.0)
        return acc

    join()
    rho = total(lax.fori_loop(0, 8, set_residual, zero))

    def sweep(t, state):
        rho, beta = state

        def image(k, acc):
            at = here(k)
            for j in range(7):
                line = []
                for i in range(7):
                    n = i * 7 + j
                    value = r_ref[n, at, :] + beta * d_ref[n, at, :]
                    d_ref[n, at, :] = value
                    line.append(value)
                flux = line_apply(DERIV, line)
                flux = [flux[i] * q_ref[0, i * 7 + j, at, :] for i in range(7)]
                part = line_apply(flipped, flux)
                for i in range(7):
                    n = i * 7 + j
                    part[i] = part[i] + mk_ref[n, at, :] * line[i]
                    im_ref[n, at, :] = part[i]
                acc = acc + tree_sum([part[i] * line[i] for i in range(7)])
            for i in range(7):
                line = [d_ref[i * 7 + j, at, :] for j in range(7)]
                flux = line_apply(DERIV, line)
                flux = [flux[j] * q_ref[1, i * 7 + j, at, :] for j in range(7)]
                part = line_apply(flipped, flux)
                for j in range(7):
                    n = i * 7 + j
                    im_ref[n, at, :] = im_ref[n, at, :] + part[j]
                acc = acc + tree_sum([part[j] * line[j] for j in range(7)])
            return acc

        step = rho / total(lax.fori_loop(0, 8, image, zero))
        join()
        for n in range(49):
            x_ref[n] = x_ref[n] + step * d_ref[n, own, :]

        def descend(k, acc):
            at = here(k)
            for i in range(7):
                line = []
                for j in range(7):
                    n = i * 7 + j
                    value = r_ref[n, at, :] - step * im_ref[n, at, :]
                    r_ref[n, at, :] = value
                    line.append(value)
                acc = acc + square(line, 0.5 if i in (0, 6) else 1.0)
            return acc

        fresh = total(lax.fori_loop(0, 8, descend, zero))
        return fresh, fresh / rho

    lax.fori_loop(0, count_ref[row_id], sweep, (rho, zero))

    for i in range(7):
        block = jnp.stack([x_ref[i * 7 + j] for j in range(7)] + [zero])
        block = jnp.swapaxes(block, 0, 1)
        for s in range(8):
            t_ref[s, i] = block[s]
    first = (z % 2) * 4
    for to in range(4):
        for i in range(7):
            value = t_ref[first + to, i]
            for copy in range(8):
                out_ref[to * 8 + copy, i] = value


def solve(counts, same, other, metrics):
    vmem = pl.BlockSpec(memory_space=pltpu.VMEM)
    field = pltpu.VMEM((49, 64, 128), jnp.float32)
    return pl.pallas_call(
        solve_kernel,
        out_shape=jax.ShapeDtypeStruct((NZ, 7, 8, 128), jnp.float32),
        in_specs=[pl.BlockSpec(memory_space=pltpu.SMEM)] + [vmem] * 3,
        out_specs=vmem,
        scratch_shapes=[
            field, field, field, field,
            pltpu.VMEM((49, 8, 128), jnp.float32),
            pltpu.VMEM((8, 7, 8, 128), jnp.float32),
        ],
        compiler_params=pltpu.CompilerParams(vmem_limit_bytes=40 * MIB),
    )(counts, same, other, metrics)


def pressure_kernel(coef_ref, rows_ref, out_ref):
    y = lax.axis_index("y")
    for zl in range(4):
        coefs = [coef_ref[(y * 4 + zl) * NZ + q] for q in range(NZ)]
        for i in range(7):
            value = tree_sum([coefs[q] * rows_ref[q, i] for q in range(NZ)])
            out_ref[zl, i] = value[0:7, :]


def pressure_planes(rows):
    vmem = pl.BlockSpec(memory_space=pltpu.VMEM)
    return pl.pallas_call(
        pressure_kernel,
        out_shape=jax.ShapeDtypeStruct((4, 7, 7, 128), jnp.float32),
        in_specs=[pl.BlockSpec(memory_space=pltpu.SMEM), vmem],
        out_specs=vmem,
        compiler_params=pltpu.CompilerParams(vmem_limit_bytes=16 * MIB),
    )(jnp.asarray(plane_coefs()), rows)


def gather_row(mine):
    swap = [(0, 1), (1, 0)]
    turns = [[(z, (z + back) % 4) for z in range(4)] for back in range(1, 4)]
    beside = lax.ppermute(mine, "xl", swap)
    pieces = [mine] + [lax.ppermute(mine, "z", turn) for turn in turns]
    pieces += [beside] + [lax.ppermute(beside, "z", turn) for turn in turns]
    same = jnp.stack(pieces).reshape(2, 4, 4, 7, 8, 128)
    return same, lax.ppermute(same, "core", swap)


def local(stress, velocity_grad, velocity, metric, iteration_counts):
    packed = jnp.pad(metric.reshape(147, 128), ((0, 5), (0, 0)))
    gathered = lax.all_gather(packed, PLANE)
    metrics = metric_fields(gathered)
    right, left, up, down = pack_faces(stress)
    ahead = [(c, c + 1) for c in range(15)]
    above = [(e, e + 1) for e in range(3)]
    faces = (
        lax.ppermute(right, FLOW, ahead),
        lax.ppermute(left, FLOW, [(b, a) for a, b in ahead]),
        lax.ppermute(up, CROSS, above),
        lax.ppermute(down, CROSS, [(b, a) for a, b in above]),
    )
    new_stress, parts = stress_step(stress, velocity_grad, velocity, faces)
    parts = lax.all_to_all(parts, ROWS, 0, 0, tiled=True)
    mine = jnp.sum(parts.reshape(4, 8, 7, 8, 128), axis=1)
    same, other = gather_row(mine)
    answer = solve(iteration_counts, same, other, metrics)
    answer = lax.all_to_all(answer, ROWS, 0, 0, tiled=True)
    return new_stress, pressure_planes(answer)


def solution(mesh):
    fine = Mesh(mesh.devices.reshape(SPLIT), PLANE + ("y",))
    field = P(None, "y", None, None, PLANE)
    return jax.shard_map(
        local,
        mesh=fine,
        in_specs=(field, field, field, P(None, None, None, PLANE), P()),
        out_specs=(field, P("y", None, None, PLANE)),
        check_vma=False,
    )
```

```python
import jax
import jax.numpy as jnp
import numpy as np
from jax import lax
from jax.experimental import pallas as pl
from jax.experimental.pallas import tpu as pltpu
from jax.sharding import Mesh
from jax.sharding import PartitionSpec as P

FLOW = ("z", "xh")
CROSS = ("xl", "core")
PLANE = ("z", "xh", "xl", "core")
ROWS = ("xh", "y")
SPLIT = (4, 4, 2, 2, 8)

EY = 16
NZ = 32
DT_STEP = 0.01
SPAN_UNIT = 0.5
MASS_SCALE = 0.25
MIB = 1 << 20


def node_tables():
    nodes = np.array(
        [-1.0, -0.830223896278567, -0.468848793470714, 0.0,
         0.468848793470714, 0.830223896278567, 1.0]
    )
    weights = np.array(
        [1.0 / 21.0, 0.276826047361566, 0.431745381209863, 0.487619047619048,
         0.431745381209863, 0.276826047361566, 1.0 / 21.0]
    )
    bary = np.array(
        [1.0 / np.prod([nodes[c] - nodes[o] for o in range(7) if o != c]) for c in range(7)]
    )
    deriv = np.zeros((7, 7))
    for row in range(7):
        for col in range(7):
            if row != col:
                deriv[row, col] = bary[col] / bary[row] / (nodes[row] - nodes[col])
        deriv[row, row] = -np.sum(deriv[row])
    return deriv, weights


DERIV, WEIGHTS = node_tables()
LIFT = 2.0 / WEIGHTS[0]


def span_tables():
    ids = np.arange(NZ)
    harmonic = np.where(ids == 1, NZ // 2, ids // 2)
    sine = (ids % 2 == 1) & (ids != 1)
    phase = 2.0 * np.pi / NZ * (harmonic[:, None] * ids[None, :] % NZ)
    basis = np.where(sine[:, None], np.sin(phase), np.cos(phase))
    basis = basis * np.where(ids < 2, 1.0 / np.sqrt(NZ), np.sqrt(2.0 / NZ))[:, None]
    wavenum = SPAN_UNIT * harmonic
    slope = np.where(ids < 2, 0.0, np.where(sine, -wavenum, wavenum))
    return basis, slope[:, None] * basis[ids ^ 1], wavenum


BASIS, SLOPE, WAVENUM = span_tables()
ROW_AT = np.array([4 * (q % 8) + q // 8 for q in range(NZ)])


def source_coefs():
    table = np.zeros((8, NZ, 3, 4))
    for y in range(8):
        cols = slice(4 * y, 4 * y + 4)
        table[y, :, 0] = BASIS[ROW_AT, cols]
        table[y, :, 1] = -(WAVENUM[ROW_AT] ** 2)[:, None] * BASIS[ROW_AT, cols]
        table[y, :, 2] = 2.0 * SLOPE[ROW_AT, cols]
    return table.astype(np.float32).reshape(-1)


def plane_coefs():
    table = np.stack([BASIS.T[4 * y : 4 * y + 4][:, ROW_AT] for y in range(8)])
    return table.astype(np.float32).reshape(-1)


def line_apply(mat, f):
    even = [f[m] + f[6 - m] for m in range(3)]
    odd = [f[m] - f[6 - m] for m in range(3)]
    out = [None] * 7
    for i in range(3):
        from_odd = float(0.5 * (mat[i, 0] - mat[i, 6])) * odd[0]
        from_even = float(mat[i, 3]) * f[3]
        for m in range(3):
            from_even = from_even + float(0.5 * (mat[i, m] + mat[i, 6 - m])) * even[m]
            if m:
                from_odd = from_odd + float(0.5 * (mat[i, m] - mat[i, 6 - m])) * odd[m]
        out[i] = from_odd + from_even
        out[6 - i] = from_odd - from_even
    out[3] = float(mat[3, 0]) * odd[0] + float(mat[3, 1]) * odd[1] + float(mat[3, 2]) * odd[2]
    return out


def tree_sum(terms):
    while len(terms) > 1:
        terms = [sum(terms[i : i + 2][1:], terms[i]) for i in range(0, len(terms), 2)]
    return terms[0]


def lanes():
    return lax.broadcasted_iota(jnp.int32, (8, 128), 1)


def pack_kernel(s_ref, right_ref, left_ref, up_ref, down_ref, t_ref):
    lane = lanes()
    block, inner = lane // 16, lane % 16

    def plane(z, carry):
        for c in range(6):
            for i in range(7):
                t_ref[c, i, 0:7, :] = s_ref[c, z, i]
        zero = jnp.zeros((8, 128), jnp.float32)
        right, left = zero, zero
        for c in range(6):
            right = jnp.where(block == c, pltpu.roll(t_ref[c, 6], (16 * (c + 1)) % 128, 1), right)
            left = jnp.where(block == c, pltpu.roll(t_ref[c, 0], 16 * c, 1), left)
        right_ref[z] = right
        left_ref[z] = left
        for i in range(7):
            up, down = zero, zero
            for c in range(6):
                up = jnp.where(inner == c, pltpu.roll(t_ref[c, i], (c - 15) % 128, 1), up)
                down = jnp.where(inner == c, pltpu.roll(t_ref[c, i], c, 1), down)
            up_ref[z, i : i + 1, :] = up[6:7, :]
            down_ref[z, i : i + 1, :] = down[0:1, :]
        up_ref[z, 7:8, :] = zero[0:1, :]
        down_ref[z, 7:8, :] = zero[0:1, :]
        return carry

    for c in range(6):
        for i in range(7):
            t_ref[c, i] = jnp.zeros((8, 128), jnp.float32)
    lax.fori_loop(0, 4, plane, 0)


def pack_faces(stress):
    return pl.pallas_call(
        pack_kernel,
        out_shape=[jax.ShapeDtypeStruct((4, 8, 128), jnp.float32)] * 4,
        in_specs=[pl.BlockSpec(memory_space=pltpu.VMEM)],
        out_specs=[pl.BlockSpec(memory_space=pltpu.VMEM)] * 4,
        scratch_shapes=[pltpu.VMEM((6, 7, 8, 128), jnp.float32)],
        compiler_params=pltpu.CompilerParams(vmem_limit_bytes=16 * MIB),
    )(stress)


def stress_kernel(
    coef_ref, s_ref, g_ref, v_ref, left_ref, right_ref, below_ref, above_ref, dcol_ref,
    new_ref, rows_ref, t_ref, d_ref, n_ref, f_ref, p_ref, lb_ref,
):
    lane = lanes()
    inner = lane % 16
    row = lax.broadcasted_iota(jnp.int32, (8, 128), 0)
    twice = 2.0 * DERIV
    y = lax.axis_index("y")

    def across(ref, *at):
        total = dcol_ref[0] * ref[(*at, pl.ds(0, 1), slice(None))]
        for m in range(1, 7):
            total = total + dcol_ref[m] * ref[(*at, pl.ds(m, 1), slice(None))]
        return total

    zero = jnp.zeros((8, 128), jnp.float32)
    for i in range(7):
        for c in range(6):
            t_ref[c, i] = zero
        for c in range(11):
            lb_ref[c, i] = zero

    def plane(z, carry):
        for i in range(7):
            for c in range(6):
                t_ref[c, i, 0:7, :] = s_ref[c, z, i]
            for c in range(9):
                lb_ref[c, i, 0:7, :] = g_ref[c, z, i]
            for c in range(2):
                lb_ref[9 + c, i, 0:7, :] = v_ref[c, z, i]
        for c in range(6):
            slope = line_apply(twice, [t_ref[c, i] for i in range(7)])
            for i in range(7):
                d_ref[c, i] = slope[i]
        for i in range(7):
            u, v = lb_ref[9, i], lb_ref[10, i]
            away = jnp.where(row == 0, -v, v)
            away = jnp.where((row == 0) | (row == 6), jnp.minimum(away, 0.0), 0.0) * float(-LIFT)
            if i == 0:
                along = jnp.minimum(-u, 0.0) * float(-LIFT)
            if i == 6:
                along = jnp.minimum(u, 0.0) * float(-LIFT)
            grad = [lb_ref[c, i] for c in range(9)]
            tau = [t_ref[c, i] for c in range(6)]
            xx, yy, zz = tau[0] + 0.5, tau[1] + 0.5, tau[2] + 0.5
            full = ((xx, tau[3], tau[4]), (tau[3], yy, tau[5]), (tau[4], tau[5], zz))
            prod = [
                [tree_sum([grad[3 * a + k] * full[k][b] for k in range(3)]) for b in range(3)]
                for a in range(3)
            ]
            pairs = ((0, 0), (1, 1), (2, 2), (0, 1), (0, 2), (1, 2))
            for c, (a, b) in enumerate(pairs):
                forcing = prod[a][b] + prod[b][a] - tau[c]
                advect = u * d_ref[c, i] + v * across(t_ref, c, i)
                low = jnp.broadcast_to(t_ref[c, i, 6:7, :], (8, 128))
                low = pltpu.roll(low, 1, 1)
                got = jnp.broadcast_to(below_ref[z, i : i + 1, :], (8, 128))
                low = jnp.where(inner == 0, pltpu.roll(got, (128 - c) % 128, 1), low)
                high = jnp.broadcast_to(t_ref[c, i, 0:1, :], (8, 128))
                high = pltpu.roll(high, 127, 1)
                got = jnp.broadcast_to(above_ref[z, i : i + 1, :], (8, 128))
                high = jnp.where(inner == 15, pltpu.roll(got, 15 - c, 1), high)
                advect = advect + away * (tau[c] - jnp.where(row == 0, low, high))
                if i == 0:
                    mine = pltpu.roll(t_ref[c, 6], 16, 1)
                    got = pltpu.roll(left_ref[z], (128 - 16 * c) % 128, 1)
                    advect = advect + along * (tau[c] - jnp.where(lane < 16, got, mine))
                if i == 6:
                    mine = pltpu.roll(t_ref[c, 0], 112, 1)
                    got = pltpu.roll(right_ref[z], 112 - 16 * c, 1)
                    advect = advect + along * (tau[c] - jnp.where(lane >= 112, got, mine))
                fresh = tau[c] + DT_STEP * (forcing - advect)
                n_ref[c, i] = fresh
                new_ref[c, z, i] = fresh[0:7, :]
        first = line_apply(twice, [n_ref[0, i] for i in range(7)])
        first = [first[i] + across(n_ref, 3, i) for i in range(7)]
        planar = line_apply(twice, first)
        second = line_apply(twice, [n_ref[3, i] for i in range(7)])
        for i in range(7):
            f_ref[i] = second[i] + across(n_ref, 1, i)
        crossed = line_apply(twice, [n_ref[4, i] for i in range(7)])
        for i in range(7):
            p_ref[0, z, i] = planar[i] + across(f_ref, i)
            p_ref[1, z, i] = n_ref[2, i]
            p_ref[2, z, i] = crossed[i] + across(n_ref, 5, i)
        return carry

    lax.fori_loop(0, 4, plane, 0)

    def one_row(q, carry):
        base = (y * NZ + q) * 12
        coefs = [coef_ref[base + k] for k in range(12)]
        for i in range(7):
            rows_ref[q, i] = tree_sum(
                [coefs[4 * s + z] * p_ref[s, z, i] for s in range(3) for z in range(4)]
            )
        return carry

    lax.fori_loop(0, NZ, one_row, 0)


def stress_step(stress, grad, velocity, faces):
    dcol = np.zeros((7, 8, 128))
    dcol[:, :7, :] = 2.0 * DERIV.T[:, :, None]
    vmem = pl.BlockSpec(memory_space=pltpu.VMEM)
    return pl.pallas_call(
        stress_kernel,
        out_shape=[
            jax.ShapeDtypeStruct((6, 4, 7, 7, 128), jnp.float32),
            jax.ShapeDtypeStruct((NZ, 7, 8, 128), jnp.float32),
        ],
        in_specs=[pl.BlockSpec(memory_space=pltpu.SMEM)] + [vmem] * 8,
        out_specs=[vmem] * 2,
        scratch_shapes=[
            pltpu.VMEM((6, 7, 8, 128), jnp.float32),
            pltpu.VMEM((6, 7, 8, 128), jnp.float32),
            pltpu.VMEM((6, 7, 8, 128), jnp.float32),
            pltpu.VMEM((7, 8, 128), jnp.float32),
            pltpu.VMEM((3, 4, 7, 8, 128), jnp.float32),
            pltpu.VMEM((11, 7, 8, 128), jnp.float32),
        ],
        compiler_params=pltpu.CompilerParams(vmem_limit_bytes=24 * MIB),
    )(
        jnp.asarray(source_coefs()), stress, grad, velocity, *faces,
        jnp.asarray(dcol, jnp.float32),
    )


def metric_kernel(same_ref, other_ref, q_ref):
    z, xh = lax.axis_index("z"), lax.axis_index("xh")
    xl, core = lax.axis_index("xl"), lax.axis_index("core")

    def chunk(quarter, carry):
        from_xl, half = quarter // 2, quarter % 2
        flip = (xl + from_xl) % 2
        back_z = [(z - half * 2 - s + 4) % 4 for s in range(2)]
        back_h = [(xh - s + 4) % 4 for s in range(4)]
        for ref, from_core in ((same_ref, core), (other_ref, 1 - core)):
            start = ((from_xl * 2 + from_core) * 2 + half) * 8
            here = pl.ds(pl.multiple_of(start, 8), 8)
            for tile in range(19):
                rows = slice(8 * tile, 8 * tile + 8)
                block = jnp.stack(
                    [ref[back_z[s // 4], back_h[s % 4], flip, rows, :] for s in range(8)]
                )
                block = jnp.swapaxes(block, 0, 1)
                for j in range(8):
                    c, n = divmod(8 * tile + j, 49)
                    if c < 3:
                        scale = WEIGHTS[n // 7] * WEIGHTS[n % 7] * (MASS_SCALE if c == 2 else 1.0)
                        q_ref[c, n, here, :] = float(scale) * block[j]
        return carry

    lax.fori_loop(0, 4, chunk, 0)


def metric_fields(same, other):
    vmem = pl.BlockSpec(memory_space=pltpu.VMEM)
    return pl.pallas_call(
        metric_kernel,
        out_shape=jax.ShapeDtypeStruct((3, 49, 64, 128), jnp.float32),
        in_specs=[vmem] * 2,
        out_specs=vmem,
        compiler_params=pltpu.CompilerParams(vmem_limit_bytes=24 * MIB),
    )(same, other)


def solve_kernel(
    count_ref, same_ref, other_ref, q_ref, out_ref, r_ref, d_ref, im_ref, mk_ref, x_ref, t_ref
):
    z, xh, y = lax.axis_index("z"), lax.axis_index("xh"), lax.axis_index("y")
    xl, core = lax.axis_index("xl"), lax.axis_index("core")
    e = xl * 2 + core
    row_id = 4 * y + xh
    harmonic = jnp.where(row_id == 1, NZ // 2, row_id // 2).astype(jnp.float32)
    wavesq = harmonic * harmonic * (SPAN_UNIT * SPAN_UNIT)
    own = pl.ds(pl.multiple_of((e * 2 + z // 2) * 8, 8), 8)
    flipped = DERIV.T
    zero = jnp.zeros((8, 128), jnp.float32)

    def here(k):
        return pl.ds(pl.multiple_of(k * 8, 8), 8)

    def chunk_in(quarter, carry):
        from_xl, half = quarter // 2, quarter % 2
        for ref, from_core in ((same_ref, core), (other_ref, 1 - core)):
            at = here((from_xl * 2 + from_core) * 2 + half)
            flip = (xl + from_xl) % 2
            back = [(z - half * 2 - s + 4) % 4 for s in range(2)]
            for i in range(7):
                block = jnp.stack([ref[flip, back[s // 4], s % 4, i] for s in range(8)])
                block = jnp.swapaxes(block, 0, 1)
                for j in range(7):
                    n = i * 7 + j
                    mass = q_ref[2, n, at, :]
                    im_ref[n, at, :] = mass * block[j]
                    mk_ref[n, at, :] = wavesq * mass
                    d_ref[n, at, :] = zero
        return carry

    lax.fori_loop(0, 4, chunk_in, 0)
    for n in range(49):
        x_ref[n] = zero

    lane = lax.broadcasted_iota(jnp.int32, (64, 128), 1)
    spot = lax.broadcasted_iota(jnp.int32, (64, 128), 0)
    inner, c_pos = lane % 16, spot % 16
    wall = (
        (c_pos == 0) & (lane < 16),
        (c_pos == 15) & (lane >= 112),
        (spot < 16) & (inner == 0),
        (spot >= 48) & (inner == 15),
    )

    def join():
        for j in range(7):
            low, high = im_ref[j], im_ref[42 + j]
            moved = pltpu.roll(high, 16, 1)
            moved = jnp.where(lane < 16, pltpu.roll(moved, 1, 0), moved)
            back = pltpu.roll(low, 112, 1)
            back = jnp.where(lane >= 112, pltpu.roll(back, 63, 0), back)
            im_ref[j] = jnp.where(wall[0], 0.0, low + moved)
            im_ref[42 + j] = jnp.where(wall[1], 0.0, high + back)
        for i in range(7):
            low, high = im_ref[7 * i], im_ref[7 * i + 6]
            other = pltpu.roll(pltpu.roll(high, 113, 1), 16, 0)
            moved = jnp.where(inner == 0, other, pltpu.roll(high, 1, 1))
            other = pltpu.roll(pltpu.roll(low, 15, 1), 48, 0)
            back = jnp.where(inner == 15, other, pltpu.roll(low, 127, 1))
            im_ref[7 * i] = jnp.where(wall[2], 0.0, low + moved)
            im_ref[7 * i + 6] = jnp.where(wall[3], 0.0, high + back)

    def total(acc):
        return jnp.broadcast_to(jnp.sum(acc, axis=(0, 1), keepdims=True), (8, 128))

    def square(line, ends):
        inside = tree_sum([line[m] * line[m] for m in range(1, 6)])
        return ends * (inside + 0.5 * (line[0] * line[0] + line[6] * line[6]))

    def set_residual(k, acc):
        for i in range(7):
            line = []
            for j in range(7):
                value = im_ref[i * 7 + j, here(k), :]
                r_ref[i * 7 + j, here(k), :] = value
                line.append(value)
            acc = acc + square(line, 0.5 if i in (0, 6) else 1.0)
        return acc

    join()
    rho = total(lax.fori_loop(0, 8, set_residual, zero))

    def sweep(t, state):
        rho, beta = state

        def image(k, acc):
            at = here(k)
            for j in range(7):
                line = []
                for i in range(7):
                    n = i * 7 + j
                    value = r_ref[n, at, :] + beta * d_ref[n, at, :]
                    d_ref[n, at, :] = value
                    line.append(value)
                flux = line_apply(DERIV, line)
                flux = [flux[i] * q_ref[0, i * 7 + j, at, :] for i in range(7)]
                part = line_apply(flipped, flux)
                for i in range(7):
                    n = i * 7 + j
                    part[i] = part[i] + mk_ref[n, at, :] * line[i]
                    im_ref[n, at, :] = part[i]
                acc = acc + tree_sum([part[i] * line[i] for i in range(7)])
            for i in range(7):
                line = [d_ref[i * 7 + j, at, :] for j in range(7)]
                flux = line_apply(DERIV, line)
                flux = [flux[j] * q_ref[1, i * 7 + j, at, :] for j in range(7)]
                part = line_apply(flipped, flux)
                for j in range(7):
                    n = i * 7 + j
                    im_ref[n, at, :] = im_ref[n, at, :] + part[j]
                acc = acc + tree_sum([part[j] * line[j] for j in range(7)])
            return acc

        step = rho / total(lax.fori_loop(0, 8, image, zero))
        join()
        for n in range(49):
            x_ref[n] = x_ref[n] + step * d_ref[n, own, :]

        def descend(k, acc):
            at = here(k)
            for i in range(7):
                line = []
                for j in range(7):
                    n = i * 7 + j
                    value = r_ref[n, at, :] - step * im_ref[n, at, :]
                    r_ref[n, at, :] = value
                    line.append(value)
                acc = acc + square(line, 0.5 if i in (0, 6) else 1.0)
            return acc

        fresh = total(lax.fori_loop(0, 8, descend, zero))
        return fresh, fresh / rho

    lax.fori_loop(0, count_ref[row_id], sweep, (rho, zero))

    for i in range(7):
        block = jnp.stack([x_ref[i * 7 + j] for j in range(7)] + [zero])
        block = jnp.swapaxes(block, 0, 1)
        for s in range(8):
            t_ref[s, i] = block[s]
    first = (z % 2) * 4
    for to in range(4):
        for i in range(7):
            value = t_ref[first + to, i]
            for copy in range(8):
                out_ref[to * 8 + copy, i] = value


def solve(counts, same, other, metrics):
    vmem = pl.BlockSpec(memory_space=pltpu.VMEM)
    field = pltpu.VMEM((49, 64, 128), jnp.float32)
    return pl.pallas_call(
        solve_kernel,
        out_shape=jax.ShapeDtypeStruct((NZ, 7, 8, 128), jnp.float32),
        in_specs=[pl.BlockSpec(memory_space=pltpu.SMEM)] + [vmem] * 3,
        out_specs=vmem,
        scratch_shapes=[
            field, field, field, field,
            pltpu.VMEM((49, 8, 128), jnp.float32),
            pltpu.VMEM((8, 7, 8, 128), jnp.float32),
        ],
        compiler_params=pltpu.CompilerParams(vmem_limit_bytes=40 * MIB),
    )(counts, same, other, metrics)


def pressure_kernel(coef_ref, rows_ref, out_ref):
    y = lax.axis_index("y")
    for zl in range(4):
        coefs = [coef_ref[(y * 4 + zl) * NZ + q] for q in range(NZ)]
        for i in range(7):
            value = tree_sum([coefs[q] * rows_ref[q, i] for q in range(NZ)])
            out_ref[zl, i] = value[0:7, :]


def pressure_planes(rows):
    vmem = pl.BlockSpec(memory_space=pltpu.VMEM)
    return pl.pallas_call(
        pressure_kernel,
        out_shape=jax.ShapeDtypeStruct((4, 7, 7, 128), jnp.float32),
        in_specs=[pl.BlockSpec(memory_space=pltpu.SMEM), vmem],
        out_specs=vmem,
        compiler_params=pltpu.CompilerParams(vmem_limit_bytes=16 * MIB),
    )(jnp.asarray(plane_coefs()), rows)


SWAP = [(0, 1), (1, 0)]
TURNS = [[(at, (at + back) % 4) for at in range(4)] for back in range(1, 4)]


def gather_row(mine):
    beside = lax.ppermute(mine, "xl", SWAP)
    pieces = [mine] + [lax.ppermute(mine, "z", turn) for turn in TURNS]
    pieces += [beside] + [lax.ppermute(beside, "z", turn) for turn in TURNS]
    same = jnp.stack(pieces).reshape(2, 4, 4, 7, 8, 128)
    return same, lax.ppermute(same, "core", SWAP)


def gather_metric(mine):
    pair = jnp.stack([mine, lax.ppermute(mine, "xl", SWAP)])
    ring = jnp.stack([pair] + [lax.ppermute(pair, "xh", turn) for turn in TURNS])
    same = jnp.stack([ring] + [lax.ppermute(ring, "z", turn) for turn in TURNS])
    return same, lax.ppermute(same, "core", SWAP)


def local(stress, velocity_grad, velocity, metric, iteration_counts):
    packed = jnp.pad(metric.reshape(147, 128), ((0, 5), (0, 0)))
    metrics = metric_fields(*gather_metric(packed))
    right, left, up, down = pack_faces(stress)
    ahead = [(c, c + 1) for c in range(15)]
    above = [(e, e + 1) for e in range(3)]
    faces = (
        lax.ppermute(right, FLOW, ahead),
        lax.ppermute(left, FLOW, [(b, a) for a, b in ahead]),
        lax.ppermute(up, CROSS, above),
        lax.ppermute(down, CROSS, [(b, a) for a, b in above]),
    )
    new_stress, parts = stress_step(stress, velocity_grad, velocity, faces)
    parts = lax.all_to_all(parts, ROWS, 0, 0, tiled=True)
    mine = jnp.sum(parts.reshape(4, 8, 7, 8, 128), axis=1)
    same, other = gather_row(mine)
    answer = solve(iteration_counts, same, other, metrics)
    answer = lax.all_to_all(answer, ROWS, 0, 0, tiled=True)
    return new_stress, pressure_planes(answer)


def solution(mesh):
    fine = Mesh(mesh.devices.reshape(SPLIT), PLANE + ("y",))
    field = P(None, "y", None, None, PLANE)
    return jax.shard_map(
        local,
        mesh=fine,
        in_specs=(field, field, field, P(None, None, None, PLANE), P()),
        out_specs=(field, P("y", None, None, PLANE)),
        check_vma=False,
    )
```

```python
import jax
import jax.numpy as jnp
import numpy as np
from jax import lax
from jax.experimental import pallas as pl
from jax.experimental.pallas import tpu as pltpu
from jax.sharding import Mesh
from jax.sharding import PartitionSpec as P

FLOW = ("z", "xh")
CROSS = ("xl", "core")
PLANE = ("z", "xh", "xl", "core")
ROWS = ("xh", "y")
SPLIT = (4, 4, 2, 2, 8)

EY = 16
NZ = 32
DT_STEP = 0.01
SPAN_UNIT = 0.5
MASS_SCALE = 0.25
MIB = 1 << 20


def node_tables():
    nodes = np.array(
        [-1.0, -0.830223896278567, -0.468848793470714, 0.0,
         0.468848793470714, 0.830223896278567, 1.0]
    )
    weights = np.array(
        [1.0 / 21.0, 0.276826047361566, 0.431745381209863, 0.487619047619048,
         0.431745381209863, 0.276826047361566, 1.0 / 21.0]
    )
    bary = np.array(
        [1.0 / np.prod([nodes[c] - nodes[o] for o in range(7) if o != c]) for c in range(7)]
    )
    deriv = np.zeros((7, 7))
    for row in range(7):
        for col in range(7):
            if row != col:
                deriv[row, col] = bary[col] / bary[row] / (nodes[row] - nodes[col])
        deriv[row, row] = -np.sum(deriv[row])
    return deriv, weights


DERIV, WEIGHTS = node_tables()
LIFT = 2.0 / WEIGHTS[0]


def span_tables():
    ids = np.arange(NZ)
    harmonic = np.where(ids == 1, NZ // 2, ids // 2)
    sine = (ids % 2 == 1) & (ids != 1)
    phase = 2.0 * np.pi / NZ * (harmonic[:, None] * ids[None, :] % NZ)
    basis = np.where(sine[:, None], np.sin(phase), np.cos(phase))
    basis = basis * np.where(ids < 2, 1.0 / np.sqrt(NZ), np.sqrt(2.0 / NZ))[:, None]
    wavenum = SPAN_UNIT * harmonic
    slope = np.where(ids < 2, 0.0, np.where(sine, -wavenum, wavenum))
    return basis, slope[:, None] * basis[ids ^ 1], wavenum


BASIS, SLOPE, WAVENUM = span_tables()
ROW_AT = np.array([4 * (q % 8) + q // 8 for q in range(NZ)])


def source_coefs():
    table = np.zeros((8, NZ, 3, 4))
    for y in range(8):
        cols = slice(4 * y, 4 * y + 4)
        table[y, :, 0] = BASIS[ROW_AT, cols]
        table[y, :, 1] = -(WAVENUM[ROW_AT] ** 2)[:, None] * BASIS[ROW_AT, cols]
        table[y, :, 2] = 2.0 * SLOPE[ROW_AT, cols]
    return table.astype(np.float32).reshape(-1)


def plane_coefs():
    table = np.stack([BASIS.T[4 * y : 4 * y + 4][:, ROW_AT] for y in range(8)])
    return table.astype(np.float32).reshape(-1)


def line_apply(mat, f):
    even = [f[m] + f[6 - m] for m in range(3)]
    odd = [f[m] - f[6 - m] for m in range(3)]
    out = [None] * 7
    for i in range(3):
        from_odd = float(0.5 * (mat[i, 0] - mat[i, 6])) * odd[0]
        from_even = float(mat[i, 3]) * f[3]
        for m in range(3):
            from_even = from_even + float(0.5 * (mat[i, m] + mat[i, 6 - m])) * even[m]
            if m:
                from_odd = from_odd + float(0.5 * (mat[i, m] - mat[i, 6 - m])) * odd[m]
        out[i] = from_odd + from_even
        out[6 - i] = from_odd - from_even
    out[3] = float(mat[3, 0]) * odd[0] + float(mat[3, 1]) * odd[1] + float(mat[3, 2]) * odd[2]
    return out


def tree_sum(terms):
    while len(terms) > 1:
        terms = [sum(terms[i : i + 2][1:], terms[i]) for i in range(0, len(terms), 2)]
    return terms[0]


def lanes():
    return lax.broadcasted_iota(jnp.int32, (8, 128), 1)


def pack_kernel(s_ref, right_ref, left_ref, up_ref, down_ref, t_ref):
    lane = lanes()
    block, inner = lane // 16, lane % 16

    def plane(z, carry):
        for c in range(6):
            for i in range(7):
                t_ref[c, i, 0:7, :] = s_ref[c, z, i]
        zero = jnp.zeros((8, 128), jnp.float32)
        right, left = zero, zero
        for c in range(6):
            right = jnp.where(block == c, pltpu.roll(t_ref[c, 6], (16 * (c + 1)) % 128, 1), right)
            left = jnp.where(block == c, pltpu.roll(t_ref[c, 0], 16 * c, 1), left)
        right_ref[z] = right
        left_ref[z] = left
        for i in range(7):
            up, down = zero, zero
            for c in range(6):
                up = jnp.where(inner == c, pltpu.roll(t_ref[c, i], (c - 15) % 128, 1), up)
                down = jnp.where(inner == c, pltpu.roll(t_ref[c, i], c, 1), down)
            up_ref[z, i : i + 1, :] = up[6:7, :]
            down_ref[z, i : i + 1, :] = down[0:1, :]
        up_ref[z, 7:8, :] = zero[0:1, :]
        down_ref[z, 7:8, :] = zero[0:1, :]
        return carry

    for c in range(6):
        for i in range(7):
            t_ref[c, i] = jnp.zeros((8, 128), jnp.float32)
    lax.fori_loop(0, 4, plane, 0)


def pack_faces(stress):
    return pl.pallas_call(
        pack_kernel,
        out_shape=[jax.ShapeDtypeStruct((4, 8, 128), jnp.float32)] * 4,
        in_specs=[pl.BlockSpec(memory_space=pltpu.VMEM)],
        out_specs=[pl.BlockSpec(memory_space=pltpu.VMEM)] * 4,
        scratch_shapes=[pltpu.VMEM((6, 7, 8, 128), jnp.float32)],
        compiler_params=pltpu.CompilerParams(vmem_limit_bytes=16 * MIB),
    )(stress)


def stress_kernel(
    coef_ref, s_ref, g_ref, v_ref, left_ref, right_ref, below_ref, above_ref, dcol_ref,
    new_ref, rows_ref, t_ref, d_ref, n_ref, f_ref, p_ref, lb_ref,
):
    lane = lanes()
    inner = lane % 16
    row = lax.broadcasted_iota(jnp.int32, (8, 128), 0)
    twice = 2.0 * DERIV
    y = lax.axis_index("y")

    def across(ref, *at):
        total = dcol_ref[0] * ref[(*at, pl.ds(0, 1), slice(None))]
        for m in range(1, 7):
            total = total + dcol_ref[m] * ref[(*at, pl.ds(m, 1), slice(None))]
        return total

    zero = jnp.zeros((8, 128), jnp.float32)
    for i in range(7):
        for c in range(6):
            t_ref[c, i] = zero
        for c in range(11):
            lb_ref[c, i] = zero

    def plane(z, carry):
        for i in range(7):
            for c in range(6):
                t_ref[c, i, 0:7, :] = s_ref[c, z, i]
            for c in range(9):
                lb_ref[c, i, 0:7, :] = g_ref[c, z, i]
            for c in range(2):
                lb_ref[9 + c, i, 0:7, :] = v_ref[c, z, i]
        for c in range(6):
            slope = line_apply(twice, [t_ref[c, i] for i in range(7)])
            for i in range(7):
                d_ref[c, i] = slope[i]
        for i in range(7):
            u, v = lb_ref[9, i], lb_ref[10, i]
            away = jnp.where(row == 0, -v, v)
            away = jnp.where((row == 0) | (row == 6), jnp.minimum(away, 0.0), 0.0) * float(-LIFT)
            if i == 0:
                along = jnp.minimum(-u, 0.0) * float(-LIFT)
            if i == 6:
                along = jnp.minimum(u, 0.0) * float(-LIFT)
            grad = [lb_ref[c, i] for c in range(9)]
            tau = [t_ref[c, i] for c in range(6)]
            xx, yy, zz = tau[0] + 0.5, tau[1] + 0.5, tau[2] + 0.5
            full = ((xx, tau[3], tau[4]), (tau[3], yy, tau[5]), (tau[4], tau[5], zz))
            prod = [
                [tree_sum([grad[3 * a + k] * full[k][b] for k in range(3)]) for b in range(3)]
                for a in range(3)
            ]
            pairs = ((0, 0), (1, 1), (2, 2), (0, 1), (0, 2), (1, 2))
            for c, (a, b) in enumerate(pairs):
                forcing = prod[a][b] + prod[b][a] - tau[c]
                advect = u * d_ref[c, i] + v * across(t_ref, c, i)
                low = jnp.broadcast_to(t_ref[c, i, 6:7, :], (8, 128))
                low = pltpu.roll(low, 1, 1)
                got = jnp.broadcast_to(below_ref[z, i : i + 1, :], (8, 128))
                low = jnp.where(inner == 0, pltpu.roll(got, (128 - c) % 128, 1), low)
                high = jnp.broadcast_to(t_ref[c, i, 0:1, :], (8, 128))
                high = pltpu.roll(high, 127, 1)
                got = jnp.broadcast_to(above_ref[z, i : i + 1, :], (8, 128))
                high = jnp.where(inner == 15, pltpu.roll(got, 15 - c, 1), high)
                advect = advect + away * (tau[c] - jnp.where(row == 0, low, high))
                if i == 0:
                    mine = pltpu.roll(t_ref[c, 6], 16, 1)
                    got = pltpu.roll(left_ref[z], (128 - 16 * c) % 128, 1)
                    advect = advect + along * (tau[c] - jnp.where(lane < 16, got, mine))
                if i == 6:
                    mine = pltpu.roll(t_ref[c, 0], 112, 1)
                    got = pltpu.roll(right_ref[z], 112 - 16 * c, 1)
                    advect = advect + along * (tau[c] - jnp.where(lane >= 112, got, mine))
                fresh = tau[c] + DT_STEP * (forcing - advect)
                n_ref[c, i] = fresh
                new_ref[c, z, i] = fresh[0:7, :]
        first = line_apply(twice, [n_ref[0, i] for i in range(7)])
        first = [first[i] + across(n_ref, 3, i) for i in range(7)]
        planar = line_apply(twice, first)
        second = line_apply(twice, [n_ref[3, i] for i in range(7)])
        for i in range(7):
            f_ref[i] = second[i] + across(n_ref, 1, i)
        crossed = line_apply(twice, [n_ref[4, i] for i in range(7)])
        for i in range(7):
            p_ref[0, z, i] = planar[i] + across(f_ref, i)
            p_ref[1, z, i] = n_ref[2, i]
            p_ref[2, z, i] = crossed[i] + across(n_ref, 5, i)
        return carry

    lax.fori_loop(0, 4, plane, 0)

    def one_row(q, carry):
        base = (y * NZ + q) * 12
        coefs = [coef_ref[base + k] for k in range(12)]
        for i in range(7):
            rows_ref[q, i] = tree_sum(
                [coefs[4 * s + z] * p_ref[s, z, i] for s in range(3) for z in range(4)]
            )
        return carry

    lax.fori_loop(0, NZ, one_row, 0)


def stress_step(stress, grad, velocity, faces):
    dcol = np.zeros((7, 8, 128))
    dcol[:, :7, :] = 2.0 * DERIV.T[:, :, None]
    vmem = pl.BlockSpec(memory_space=pltpu.VMEM)
    return pl.pallas_call(
        stress_kernel,
        out_shape=[
            jax.ShapeDtypeStruct((6, 4, 7, 7, 128), jnp.float32),
            jax.ShapeDtypeStruct((NZ, 7, 8, 128), jnp.float32),
        ],
        in_specs=[pl.BlockSpec(memory_space=pltpu.SMEM)] + [vmem] * 8,
        out_specs=[vmem] * 2,
        scratch_shapes=[
            pltpu.VMEM((6, 7, 8, 128), jnp.float32),
            pltpu.VMEM((6, 7, 8, 128), jnp.float32),
            pltpu.VMEM((6, 7, 8, 128), jnp.float32),
            pltpu.VMEM((7, 8, 128), jnp.float32),
            pltpu.VMEM((3, 4, 7, 8, 128), jnp.float32),
            pltpu.VMEM((11, 7, 8, 128), jnp.float32),
        ],
        compiler_params=pltpu.CompilerParams(vmem_limit_bytes=24 * MIB),
    )(
        jnp.asarray(source_coefs()), stress, grad, velocity, *faces,
        jnp.asarray(dcol, jnp.float32),
    )


def metric_kernel(same_ref, other_ref, q_ref):
    z, xh = lax.axis_index("z"), lax.axis_index("xh")
    xl, core = lax.axis_index("xl"), lax.axis_index("core")

    def chunk(quarter, carry):
        from_xl, half = quarter // 2, quarter % 2
        flip = (xl + from_xl) % 2
        back_z = [(z - half * 2 - s + 4) % 4 for s in range(2)]
        back_h = [(xh - s + 4) % 4 for s in range(4)]
        for ref, from_core in ((same_ref, core), (other_ref, 1 - core)):
            start = ((from_xl * 2 + from_core) * 2 + half) * 8
            here = pl.ds(pl.multiple_of(start, 8), 8)
            for tile in range(19):
                rows = slice(8 * tile, 8 * tile + 8)
                block = jnp.stack(
                    [ref[back_z[s // 4], back_h[s % 4], flip, rows, :] for s in range(8)]
                )
                block = jnp.swapaxes(block, 0, 1)
                for j in range(8):
                    c, n = divmod(8 * tile + j, 49)
                    if c < 3:
                        scale = WEIGHTS[n // 7] * WEIGHTS[n % 7] * (MASS_SCALE if c == 2 else 1.0)
                        q_ref[c, n, here, :] = float(scale) * block[j]
        return carry

    lax.fori_loop(0, 4, chunk, 0)


def metric_fields(same, other):
    vmem = pl.BlockSpec(memory_space=pltpu.VMEM)
    return pl.pallas_call(
        metric_kernel,
        out_shape=jax.ShapeDtypeStruct((3, 49, 64, 128), jnp.float32),
        in_specs=[vmem] * 2,
        out_specs=vmem,
        compiler_params=pltpu.CompilerParams(vmem_limit_bytes=24 * MIB),
    )(same, other)


def solve_kernel(
    count_ref, same_ref, other_ref, q_ref, out_ref, r_ref, d_ref, im_ref, mk_ref, x_ref, t_ref
):
    z, xh, y = lax.axis_index("z"), lax.axis_index("xh"), lax.axis_index("y")
    xl, core = lax.axis_index("xl"), lax.axis_index("core")
    e = xl * 2 + core
    row_id = 4 * y + xh
    harmonic = jnp.where(row_id == 1, NZ // 2, row_id // 2).astype(jnp.float32)
    wavesq = harmonic * harmonic * (SPAN_UNIT * SPAN_UNIT)
    own = pl.ds(pl.multiple_of((e * 2 + z // 2) * 8, 8), 8)
    flipped = DERIV.T
    zero = jnp.zeros((8, 128), jnp.float32)

    def here(k):
        return pl.ds(pl.multiple_of(k * 8, 8), 8)

    def chunk_in(quarter, carry):
        from_xl, half = quarter // 2, quarter % 2
        for ref, from_core in ((same_ref, core), (other_ref, 1 - core)):
            at = here((from_xl * 2 + from_core) * 2 + half)
            flip = (xl + from_xl) % 2
            back = [(z - half * 2 - s + 4) % 4 for s in range(2)]
            for i in range(7):
                block = jnp.stack([ref[back[s // 4], flip, s % 4, i] for s in range(8)])
                block = jnp.swapaxes(block, 0, 1)
                for j in range(7):
                    n = i * 7 + j
                    mass = q_ref[2, n, at, :]
                    im_ref[n, at, :] = mass * block[j]
                    mk_ref[n, at, :] = wavesq * mass
                    d_ref[n, at, :] = zero
        return carry

    lax.fori_loop(0, 4, chunk_in, 0)
    for n in range(49):
        x_ref[n] = zero

    lane = lax.broadcasted_iota(jnp.int32, (64, 128), 1)
    spot = lax.broadcasted_iota(jnp.int32, (64, 128), 0)
    inner, c_pos = lane % 16, spot % 16
    wall = (
        (c_pos == 0) & (lane < 16),
        (c_pos == 15) & (lane >= 112),
        (spot < 16) & (inner == 0),
        (spot >= 48) & (inner == 15),
    )

    def join():
        for j in range(7):
            low, high = im_ref[j], im_ref[42 + j]
            moved = pltpu.roll(high, 16, 1)
            moved = jnp.where(lane < 16, pltpu.roll(moved, 1, 0), moved)
            back = pltpu.roll(low, 112, 1)
            back = jnp.where(lane >= 112, pltpu.roll(back, 63, 0), back)
            im_ref[j] = jnp.where(wall[0], 0.0, low + moved)
            im_ref[42 + j] = jnp.where(wall[1], 0.0, high + back)
        for i in range(7):
            low, high = im_ref[7 * i], im_ref[7 * i + 6]
            other = pltpu.roll(pltpu.roll(high, 113, 1), 16, 0)
            moved = jnp.where(inner == 0, other, pltpu.roll(high, 1, 1))
            other = pltpu.roll(pltpu.roll(low, 15, 1), 48, 0)
            back = jnp.where(inner == 15, other, pltpu.roll(low, 127, 1))
            im_ref[7 * i] = jnp.where(wall[2], 0.0, low + moved)
            im_ref[7 * i + 6] = jnp.where(wall[3], 0.0, high + back)

    def total(acc):
        return jnp.broadcast_to(jnp.sum(acc, axis=(0, 1), keepdims=True), (8, 128))

    def square(line, ends):
        inside = tree_sum([line[m] * line[m] for m in range(1, 6)])
        return ends * (inside + 0.5 * (line[0] * line[0] + line[6] * line[6]))

    def set_residual(k, acc):
        for i in range(7):
            line = []
            for j in range(7):
                value = im_ref[i * 7 + j, here(k), :]
                r_ref[i * 7 + j, here(k), :] = value
                line.append(value)
            acc = acc + square(line, 0.5 if i in (0, 6) else 1.0)
        return acc

    join()
    rho = total(lax.fori_loop(0, 8, set_residual, zero))

    def sweep(t, state):
        rho, beta = state

        def image(k, acc):
            at = here(k)
            for j in range(7):
                line = []
                for i in range(7):
                    n = i * 7 + j
                    value = r_ref[n, at, :] + beta * d_ref[n, at, :]
                    d_ref[n, at, :] = value
                    line.append(value)
                flux = line_apply(DERIV, line)
                flux = [flux[i] * q_ref[0, i * 7 + j, at, :] for i in range(7)]
                part = line_apply(flipped, flux)
                for i in range(7):
                    n = i * 7 + j
                    part[i] = part[i] + mk_ref[n, at, :] * line[i]
                    im_ref[n, at, :] = part[i]
                acc = acc + tree_sum([part[i] * line[i] for i in range(7)])
            for i in range(7):
                line = [d_ref[i * 7 + j, at, :] for j in range(7)]
                flux = line_apply(DERIV, line)
                flux = [flux[j] * q_ref[1, i * 7 + j, at, :] for j in range(7)]
                part = line_apply(flipped, flux)
                for j in range(7):
                    n = i * 7 + j
                    im_ref[n, at, :] = im_ref[n, at, :] + part[j]
                acc = acc + tree_sum([part[j] * line[j] for j in range(7)])
            return acc

        step = rho / total(lax.fori_loop(0, 8, image, zero))
        join()
        for n in range(49):
            x_ref[n] = x_ref[n] + step * d_ref[n, own, :]

        def descend(k, acc):
            at = here(k)
            for i in range(7):
                line = []
                for j in range(7):
                    n = i * 7 + j
                    value = r_ref[n, at, :] - step * im_ref[n, at, :]
                    r_ref[n, at, :] = value
                    line.append(value)
                acc = acc + square(line, 0.5 if i in (0, 6) else 1.0)
            return acc

        fresh = total(lax.fori_loop(0, 8, descend, zero))
        return fresh, fresh / rho

    lax.fori_loop(0, count_ref[row_id], sweep, (rho, zero))

    for i in range(7):
        block = jnp.stack([x_ref[i * 7 + j] for j in range(7)] + [zero])
        block = jnp.swapaxes(block, 0, 1)
        for s in range(8):
            t_ref[s, i] = block[s]
    first = (z % 2) * 4
    for to in range(4):
        for i in range(7):
            value = t_ref[first + to, i]
            for copy in range(8):
                out_ref[to * 8 + copy, i] = value


def solve(counts, same, other, metrics):
    vmem = pl.BlockSpec(memory_space=pltpu.VMEM)
    field = pltpu.VMEM((49, 64, 128), jnp.float32)
    return pl.pallas_call(
        solve_kernel,
        out_shape=jax.ShapeDtypeStruct((NZ, 7, 8, 128), jnp.float32),
        in_specs=[pl.BlockSpec(memory_space=pltpu.SMEM)] + [vmem] * 3,
        out_specs=vmem,
        scratch_shapes=[
            field, field, field, field,
            pltpu.VMEM((49, 8, 128), jnp.float32),
            pltpu.VMEM((8, 7, 8, 128), jnp.float32),
        ],
        compiler_params=pltpu.CompilerParams(vmem_limit_bytes=40 * MIB),
    )(counts, same, other, metrics)


def pressure_kernel(coef_ref, rows_ref, out_ref):
    y = lax.axis_index("y")
    for zl in range(4):
        coefs = [coef_ref[(y * 4 + zl) * NZ + q] for q in range(NZ)]
        for i in range(7):
            value = tree_sum([coefs[q] * rows_ref[q, i] for q in range(NZ)])
            out_ref[zl, i] = value[0:7, :]


def pressure_planes(rows):
    vmem = pl.BlockSpec(memory_space=pltpu.VMEM)
    return pl.pallas_call(
        pressure_kernel,
        out_shape=jax.ShapeDtypeStruct((4, 7, 7, 128), jnp.float32),
        in_specs=[pl.BlockSpec(memory_space=pltpu.SMEM), vmem],
        out_specs=vmem,
        compiler_params=pltpu.CompilerParams(vmem_limit_bytes=16 * MIB),
    )(jnp.asarray(plane_coefs()), rows)


SWAP = [(0, 1), (1, 0)]
TURNS = [[(at, (at + back) % 4) for at in range(4)] for back in range(1, 4)]


def around(mine):
    behind = lax.ppermute(mine, "z", TURNS[0])
    before = lax.ppermute(mine, "z", TURNS[2])
    half = mine.shape[0] // 2
    far = [
        lax.ppermute(behind[:half], "z", TURNS[0]),
        lax.ppermute(before[half:], "z", TURNS[2]),
    ]
    return behind, far, before


def gather_row(mine):
    pair = jnp.stack([mine, lax.ppermute(mine, "xl", SWAP)])
    behind, far, before = around(pair)
    same = jnp.concatenate([pair, behind, *far, before]).reshape(4, 2, 4, 7, 8, 128)
    return same, lax.ppermute(same, "core", SWAP)


def after(value, other):
    return lax.optimization_barrier((value, other))[0]


def local(stress, velocity_grad, velocity, metric, iteration_counts):
    packed = jnp.pad(metric.reshape(147, 128), ((0, 5), (0, 0)))
    beside = lax.ppermute(packed, "xl", SWAP)
    right, left, up, down = pack_faces(stress)
    pair = jnp.stack([after(packed, right), beside])
    ahead = [(c, c + 1) for c in range(15)]
    above = [(e, e + 1) for e in range(3)]
    faces = (
        lax.ppermute(right, FLOW, ahead),
        lax.ppermute(left, FLOW, [(b, a) for a, b in ahead]),
        lax.ppermute(up, CROSS, above),
        lax.ppermute(down, CROSS, [(b, a) for a, b in above]),
    )
    faces = after(faces, pair)
    new_stress, parts = stress_step(stress, velocity_grad, velocity, faces)
    ring = jnp.stack([pair] + [lax.ppermute(pair, "xh", turn) for turn in TURNS])
    parts = after(parts, ring)
    behind, far, before = around(ring)
    parts = lax.all_to_all(parts, ROWS, 0, 0, tiled=True)
    mine = jnp.sum(parts.reshape(4, 8, 7, 8, 128), axis=1)
    ring = after(ring, mine)
    plane = jnp.concatenate([ring, behind, *far, before]).reshape(4, 4, 2, 152, 128)
    metrics = metric_fields(plane, lax.ppermute(plane, "core", SWAP))
    same, other = gather_row(mine)
    answer = solve(iteration_counts, same, other, metrics)
    answer = lax.all_to_all(answer, ROWS, 0, 0, tiled=True)
    return new_stress, pressure_planes(answer)


def solution(mesh):
    fine = Mesh(mesh.devices.reshape(SPLIT), PLANE + ("y",))
    field = P(None, "y", None, None, PLANE)
    return jax.shard_map(
        local,
        mesh=fine,
        in_specs=(field, field, field, P(None, None, None, PLANE), P()),
        out_specs=(field, P("y", None, None, PLANE)),
        check_vma=False,
    )
```

```python
import jax
import jax.numpy as jnp
import numpy as np
from jax import lax
from jax.experimental import pallas as pl
from jax.experimental.pallas import tpu as pltpu
from jax.sharding import Mesh
from jax.sharding import PartitionSpec as P

FLOW = ("zh", "zl", "xh")
CROSS = ("xl", "core")
PLANE = ("zh", "zl", "xh", "xl", "core")
RING_X = ("xh", "xl")
ROWS = ("zh", "y")
SPLIT = (4, 2, 2, 2, 2, 8)

EY = 16
NZ = 32
DT_STEP = 0.01
SPAN_UNIT = 0.5
MASS_SCALE = 0.25
MIB = 1 << 20


def node_tables():
    nodes = np.array(
        [-1.0, -0.830223896278567, -0.468848793470714, 0.0,
         0.468848793470714, 0.830223896278567, 1.0]
    )
    weights = np.array(
        [1.0 / 21.0, 0.276826047361566, 0.431745381209863, 0.487619047619048,
         0.431745381209863, 0.276826047361566, 1.0 / 21.0]
    )
    bary = np.array(
        [1.0 / np.prod([nodes[c] - nodes[o] for o in range(7) if o != c]) for c in range(7)]
    )
    deriv = np.zeros((7, 7))
    for row in range(7):
        for col in range(7):
            if row != col:
                deriv[row, col] = bary[col] / bary[row] / (nodes[row] - nodes[col])
        deriv[row, row] = -np.sum(deriv[row])
    return deriv, weights


DERIV, WEIGHTS = node_tables()
LIFT = 2.0 / WEIGHTS[0]


def span_tables():
    ids = np.arange(NZ)
    harmonic = np.where(ids == 1, NZ // 2, ids // 2)
    sine = (ids % 2 == 1) & (ids != 1)
    phase = 2.0 * np.pi / NZ * (harmonic[:, None] * ids[None, :] % NZ)
    basis = np.where(sine[:, None], np.sin(phase), np.cos(phase))
    basis = basis * np.where(ids < 2, 1.0 / np.sqrt(NZ), np.sqrt(2.0 / NZ))[:, None]
    wavenum = SPAN_UNIT * harmonic
    slope = np.where(ids < 2, 0.0, np.where(sine, -wavenum, wavenum))
    return basis, slope[:, None] * basis[ids ^ 1], wavenum


BASIS, SLOPE, WAVENUM = span_tables()
ROW_AT = np.array([4 * (q % 8) + q // 8 for q in range(NZ)])


def source_coefs():
    table = np.zeros((8, NZ, 3, 4))
    for y in range(8):
        cols = slice(4 * y, 4 * y + 4)
        table[y, :, 0] = BASIS[ROW_AT, cols]
        table[y, :, 1] = -(WAVENUM[ROW_AT] ** 2)[:, None] * BASIS[ROW_AT, cols]
        table[y, :, 2] = 2.0 * SLOPE[ROW_AT, cols]
    return table.astype(np.float32).reshape(-1)


def plane_coefs():
    table = np.stack([BASIS.T[4 * y : 4 * y + 4][:, ROW_AT] for y in range(8)])
    return table.astype(np.float32).reshape(-1)


def line_apply(mat, f):
    even = [f[m] + f[6 - m] for m in range(3)]
    odd = [f[m] - f[6 - m] for m in range(3)]
    out = [None] * 7
    for i in range(3):
        from_odd = float(0.5 * (mat[i, 0] - mat[i, 6])) * odd[0]
        from_even = float(mat[i, 3]) * f[3]
        for m in range(3):
            from_even = from_even + float(0.5 * (mat[i, m] + mat[i, 6 - m])) * even[m]
            if m:
                from_odd = from_odd + float(0.5 * (mat[i, m] - mat[i, 6 - m])) * odd[m]
        out[i] = from_odd + from_even
        out[6 - i] = from_odd - from_even
    out[3] = float(mat[3, 0]) * odd[0] + float(mat[3, 1]) * odd[1] + float(mat[3, 2]) * odd[2]
    return out


def tree_sum(terms):
    while len(terms) > 1:
        terms = [sum(terms[i : i + 2][1:], terms[i]) for i in range(0, len(terms), 2)]
    return terms[0]


def lanes():
    return lax.broadcasted_iota(jnp.int32, (8, 128), 1)


def pack_kernel(s_ref, right_ref, left_ref, up_ref, down_ref, t_ref):
    lane = lanes()
    block, inner = lane // 16, lane % 16

    def plane(z, carry):
        for c in range(6):
            for i in range(7):
                t_ref[c, i, 0:7, :] = s_ref[c, z, i]
        zero = jnp.zeros((8, 128), jnp.float32)
        right, left = zero, zero
        for c in range(6):
            right = jnp.where(block == c, pltpu.roll(t_ref[c, 6], (16 * (c + 1)) % 128, 1), right)
            left = jnp.where(block == c, pltpu.roll(t_ref[c, 0], 16 * c, 1), left)
        right_ref[z] = right
        left_ref[z] = left
        for i in range(7):
            up, down = zero, zero
            for c in range(6):
                up = jnp.where(inner == c, pltpu.roll(t_ref[c, i], (c - 15) % 128, 1), up)
                down = jnp.where(inner == c, pltpu.roll(t_ref[c, i], c, 1), down)
            up_ref[z, i : i + 1, :] = up[6:7, :]
            down_ref[z, i : i + 1, :] = down[0:1, :]
        up_ref[z, 7:8, :] = zero[0:1, :]
        down_ref[z, 7:8, :] = zero[0:1, :]
        return carry

    for c in range(6):
        for i in range(7):
            t_ref[c, i] = jnp.zeros((8, 128), jnp.float32)
    lax.fori_loop(0, 4, plane, 0)


def pack_faces(stress):
    return pl.pallas_call(
        pack_kernel,
        out_shape=[jax.ShapeDtypeStruct((4, 8, 128), jnp.float32)] * 4,
        in_specs=[pl.BlockSpec(memory_space=pltpu.VMEM)],
        out_specs=[pl.BlockSpec(memory_space=pltpu.VMEM)] * 4,
        scratch_shapes=[pltpu.VMEM((6, 7, 8, 128), jnp.float32)],
        compiler_params=pltpu.CompilerParams(vmem_limit_bytes=16 * MIB),
    )(stress)


def stress_kernel(
    coef_ref, s_ref, g_ref, v_ref, left_ref, right_ref, below_ref, above_ref, dcol_ref,
    new_ref, rows_ref, t_ref, d_ref, n_ref, f_ref, p_ref, lb_ref,
):
    lane = lanes()
    inner = lane % 16
    row = lax.broadcasted_iota(jnp.int32, (8, 128), 0)
    twice = 2.0 * DERIV
    y = lax.axis_index("y")

    def across(ref, *at):
        total = dcol_ref[0] * ref[(*at, pl.ds(0, 1), slice(None))]
        for m in range(1, 7):
            total = total + dcol_ref[m] * ref[(*at, pl.ds(m, 1), slice(None))]
        return total

    zero = jnp.zeros((8, 128), jnp.float32)
    for i in range(7):
        for c in range(6):
            t_ref[c, i] = zero
        for c in range(11):
            lb_ref[c, i] = zero

    def plane(z, carry):
        for i in range(7):
            for c in range(6):
                t_ref[c, i, 0:7, :] = s_ref[c, z, i]
            for c in range(9):
                lb_ref[c, i, 0:7, :] = g_ref[c, z, i]
            for c in range(2):
                lb_ref[9 + c, i, 0:7, :] = v_ref[c, z, i]
        for c in range(6):
            slope = line_apply(twice, [t_ref[c, i] for i in range(7)])
            for i in range(7):
                d_ref[c, i] = slope[i]
        for i in range(7):
            u, v = lb_ref[9, i], lb_ref[10, i]
            away = jnp.where(row == 0, -v, v)
            away = jnp.where((row == 0) | (row == 6), jnp.minimum(away, 0.0), 0.0) * float(-LIFT)
            if i == 0:
                along = jnp.minimum(-u, 0.0) * float(-LIFT)
            if i == 6:
                along = jnp.minimum(u, 0.0) * float(-LIFT)
            grad = [lb_ref[c, i] for c in range(9)]
            tau = [t_ref[c, i] for c in range(6)]
            xx, yy, zz = tau[0] + 0.5, tau[1] + 0.5, tau[2] + 0.5
            full = ((xx, tau[3], tau[4]), (tau[3], yy, tau[5]), (tau[4], tau[5], zz))
            prod = [
                [tree_sum([grad[3 * a + k] * full[k][b] for k in range(3)]) for b in range(3)]
                for a in range(3)
            ]
            pairs = ((0, 0), (1, 1), (2, 2), (0, 1), (0, 2), (1, 2))
            for c, (a, b) in enumerate(pairs):
                forcing = prod[a][b] + prod[b][a] - tau[c]
                advect = u * d_ref[c, i] + v * across(t_ref, c, i)
                low = jnp.broadcast_to(t_ref[c, i, 6:7, :], (8, 128))
                low = pltpu.roll(low, 1, 1)
                got = jnp.broadcast_to(below_ref[z, i : i + 1, :], (8, 128))
                low = jnp.where(inner == 0, pltpu.roll(got, (128 - c) % 128, 1), low)
                high = jnp.broadcast_to(t_ref[c, i, 0:1, :], (8, 128))
                high = pltpu.roll(high, 127, 1)
                got = jnp.broadcast_to(above_ref[z, i : i + 1, :], (8, 128))
                high = jnp.where(inner == 15, pltpu.roll(got, 15 - c, 1), high)
                advect = advect + away * (tau[c] - jnp.where(row == 0, low, high))
                if i == 0:
                    mine = pltpu.roll(t_ref[c, 6], 16, 1)
                    got = pltpu.roll(left_ref[z], (128 - 16 * c) % 128, 1)
                    advect = advect + along * (tau[c] - jnp.where(lane < 16, got, mine))
                if i == 6:
                    mine = pltpu.roll(t_ref[c, 0], 112, 1)
                    got = pltpu.roll(right_ref[z], 112 - 16 * c, 1)
                    advect = advect + along * (tau[c] - jnp.where(lane >= 112, got, mine))
                fresh = tau[c] + DT_STEP * (forcing - advect)
                n_ref[c, i] = fresh
                new_ref[c, z, i] = fresh[0:7, :]
        first = line_apply(twice, [n_ref[0, i] for i in range(7)])
        first = [first[i] + across(n_ref, 3, i) for i in range(7)]
        planar = line_apply(twice, first)
        second = line_apply(twice, [n_ref[3, i] for i in range(7)])
        for i in range(7):
            f_ref[i] = second[i] + across(n_ref, 1, i)
        crossed = line_apply(twice, [n_ref[4, i] for i in range(7)])
        for i in range(7):
            p_ref[0, z, i] = planar[i] + across(f_ref, i)
            p_ref[1, z, i] = n_ref[2, i]
            p_ref[2, z, i] = crossed[i] + across(n_ref, 5, i)
        return carry

    lax.fori_loop(0, 4, plane, 0)

    def one_row(q, carry):
        base = (y * NZ + q) * 12
        coefs = [coef_ref[base + k] for k in range(12)]
        for i in range(7):
            rows_ref[q, i] = tree_sum(
                [coefs[4 * s + z] * p_ref[s, z, i] for s in range(3) for z in range(4)]
            )
        return carry

    lax.fori_loop(0, NZ, one_row, 0)


def stress_step(stress, grad, velocity, faces):
    dcol = np.zeros((7, 8, 128))
    dcol[:, :7, :] = 2.0 * DERIV.T[:, :, None]
    vmem = pl.BlockSpec(memory_space=pltpu.VMEM)
    return pl.pallas_call(
        stress_kernel,
        out_shape=[
            jax.ShapeDtypeStruct((6, 4, 7, 7, 128), jnp.float32),
            jax.ShapeDtypeStruct((NZ, 7, 8, 128), jnp.float32),
        ],
        in_specs=[pl.BlockSpec(memory_space=pltpu.SMEM)] + [vmem] * 8,
        out_specs=[vmem] * 2,
        scratch_shapes=[
            pltpu.VMEM((6, 7, 8, 128), jnp.float32),
            pltpu.VMEM((6, 7, 8, 128), jnp.float32),
            pltpu.VMEM((6, 7, 8, 128), jnp.float32),
            pltpu.VMEM((7, 8, 128), jnp.float32),
            pltpu.VMEM((3, 4, 7, 8, 128), jnp.float32),
            pltpu.VMEM((11, 7, 8, 128), jnp.float32),
        ],
        compiler_params=pltpu.CompilerParams(vmem_limit_bytes=24 * MIB),
    )(
        jnp.asarray(source_coefs()), stress, grad, velocity, *faces,
        jnp.asarray(dcol, jnp.float32),
    )


def places():
    zh, zl = lax.axis_index("zh"), lax.axis_index("zl")
    xh, xl = lax.axis_index("xh"), lax.axis_index("xl")
    return zh, zl, xh, xl, lax.axis_index("core")


def metric_kernel(same_ref, other_ref, q_ref):
    zh, zl, xh, xl, core = places()
    flip = [zl, 1 - zl]

    def chunk(quarter, carry):
        from_xl, half = quarter // 2, quarter % 2
        back_x = [(2 * xh + xl - 2 * s - from_xl + 4) % 4 for s in range(2)]
        back_z = [(zh - half * 2 - s + 4) % 4 for s in range(2)]
        for ref, from_core in ((same_ref, core), (other_ref, 1 - core)):
            start = ((from_xl * 2 + from_core) * 2 + half) * 8
            here = pl.ds(pl.multiple_of(start, 8), 8)
            for tile in range(19):
                rows = slice(8 * tile, 8 * tile + 8)
                block = jnp.stack(
                    [
                        ref[back_x[s % 2], back_z[s // 4], flip[s // 2 % 2], rows, :]
                        for s in range(8)
                    ]
                )
                block = jnp.swapaxes(block, 0, 1)
                for j in range(8):
                    c, n = divmod(8 * tile + j, 49)
                    if c < 3:
                        scale = WEIGHTS[n // 7] * WEIGHTS[n % 7] * (MASS_SCALE if c == 2 else 1.0)
                        q_ref[c, n, here, :] = float(scale) * block[j]
        return carry

    lax.fori_loop(0, 4, chunk, 0)


def metric_fields(same, other):
    vmem = pl.BlockSpec(memory_space=pltpu.VMEM)
    return pl.pallas_call(
        metric_kernel,
        out_shape=jax.ShapeDtypeStruct((3, 49, 64, 128), jnp.float32),
        in_specs=[vmem] * 2,
        out_specs=vmem,
        compiler_params=pltpu.CompilerParams(vmem_limit_bytes=24 * MIB),
    )(same, other)


def solve_kernel(
    count_ref, same_ref, other_ref, q_ref, out_ref, r_ref, d_ref, im_ref, mk_ref, x_ref, t_ref
):
    zh, zl, xh, xl, core = places()
    e = xl * 2 + core
    row_id = 4 * lax.axis_index("y") + zh
    harmonic = jnp.where(row_id == 1, NZ // 2, row_id // 2).astype(jnp.float32)
    wavesq = harmonic * harmonic * (SPAN_UNIT * SPAN_UNIT)
    own = pl.ds(pl.multiple_of(e * 16, 16), 16)
    flipped = DERIV.T
    zero = jnp.zeros((8, 128), jnp.float32)

    def here(k):
        return pl.ds(pl.multiple_of(k * 8, 8), 8)

    flip = [zl, 1 - zl]

    def chunk_in(quarter, carry):
        from_xl, half = quarter // 2, quarter % 2
        back = [(2 * xh + xl - 2 * s - from_xl + 4) % 4 for s in range(2)]
        for ref, from_core in ((same_ref, core), (other_ref, 1 - core)):
            at = here((from_xl * 2 + from_core) * 2 + half)
            for i in range(7):
                block = jnp.stack(
                    [ref[back[s % 2], flip[s // 2 % 2], half * 2 + s // 4, i] for s in range(8)]
                )
                block = jnp.swapaxes(block, 0, 1)
                for j in range(7):
                    n = i * 7 + j
                    mass = q_ref[2, n, at, :]
                    im_ref[n, at, :] = mass * block[j]
                    mk_ref[n, at, :] = wavesq * mass
                    d_ref[n, at, :] = zero
        return carry

    lax.fori_loop(0, 4, chunk_in, 0)
    for n in range(49):
        x_ref[n] = jnp.zeros((16, 128), jnp.float32)

    lane = lax.broadcasted_iota(jnp.int32, (64, 128), 1)
    spot = lax.broadcasted_iota(jnp.int32, (64, 128), 0)
    inner, c_pos = lane % 16, spot % 16
    wall = (
        (c_pos == 0) & (lane < 16),
        (c_pos == 15) & (lane >= 112),
        (spot < 16) & (inner == 0),
        (spot >= 48) & (inner == 15),
    )

    def join():
        for j in range(7):
            low, high = im_ref[j], im_ref[42 + j]
            moved = pltpu.roll(high, 16, 1)
            moved = jnp.where(lane < 16, pltpu.roll(moved, 1, 0), moved)
            back = pltpu.roll(low, 112, 1)
            back = jnp.where(lane >= 112, pltpu.roll(back, 63, 0), back)
            im_ref[j] = jnp.where(wall[0], 0.0, low + moved)
            im_ref[42 + j] = jnp.where(wall[1], 0.0, high + back)
        for i in range(7):
            low, high = im_ref[7 * i], im_ref[7 * i + 6]
            other = pltpu.roll(pltpu.roll(high, 113, 1), 16, 0)
            moved = jnp.where(inner == 0, other, pltpu.roll(high, 1, 1))
            other = pltpu.roll(pltpu.roll(low, 15, 1), 48, 0)
            back = jnp.where(inner == 15, other, pltpu.roll(low, 127, 1))
            im_ref[7 * i] = jnp.where(wall[2], 0.0, low + moved)
            im_ref[7 * i + 6] = jnp.where(wall[3], 0.0, high + back)

    def total(acc):
        return jnp.broadcast_to(jnp.sum(acc, axis=(0, 1), keepdims=True), (8, 128))

    def square(line, ends):
        inside = tree_sum([line[m] * line[m] for m in range(1, 6)])
        return ends * (inside + 0.5 * (line[0] * line[0] + line[6] * line[6]))

    def set_residual(k, acc):
        for i in range(7):
            line = []
            for j in range(7):
                value = im_ref[i * 7 + j, here(k), :]
                r_ref[i * 7 + j, here(k), :] = value
                line.append(value)
            acc = acc + square(line, 0.5 if i in (0, 6) else 1.0)
        return acc

    join()
    rho = total(lax.fori_loop(0, 8, set_residual, zero))

    def sweep(t, state):
        rho, beta = state

        def image(k, acc):
            at = here(k)
            for j in range(7):
                line = []
                for i in range(7):
                    n = i * 7 + j
                    value = r_ref[n, at, :] + beta * d_ref[n, at, :]
                    d_ref[n, at, :] = value
                    line.append(value)
                flux = line_apply(DERIV, line)
                flux = [flux[i] * q_ref[0, i * 7 + j, at, :] for i in range(7)]
                part = line_apply(flipped, flux)
                for i in range(7):
                    n = i * 7 + j
                    part[i] = part[i] + mk_ref[n, at, :] * line[i]
                    im_ref[n, at, :] = part[i]
                acc = acc + tree_sum([part[i] * line[i] for i in range(7)])
            for i in range(7):
                line = [d_ref[i * 7 + j, at, :] for j in range(7)]
                flux = line_apply(DERIV, line)
                flux = [flux[j] * q_ref[1, i * 7 + j, at, :] for j in range(7)]
                part = line_apply(flipped, flux)
                for j in range(7):
                    n = i * 7 + j
                    im_ref[n, at, :] = im_ref[n, at, :] + part[j]
                acc = acc + tree_sum([part[j] * line[j] for j in range(7)])
            return acc

        step = rho / total(lax.fori_loop(0, 8, image, zero))
        join()
        for n in range(49):
            x_ref[n] = x_ref[n] + step[0:1] * d_ref[n, own, :]

        def descend(k, acc):
            at = here(k)
            for i in range(7):
                line = []
                for j in range(7):
                    n = i * 7 + j
                    value = r_ref[n, at, :] - step * im_ref[n, at, :]
                    r_ref[n, at, :] = value
                    line.append(value)
                acc = acc + square(line, 0.5 if i in (0, 6) else 1.0)
            return acc

        fresh = total(lax.fori_loop(0, 8, descend, zero))
        return fresh, fresh / rho

    lax.fori_loop(0, count_ref[row_id], sweep, (rho, zero))

    for i in range(7):
        for half in range(2):
            rows = slice(8 * half, 8 * half + 8)
            block = jnp.stack([x_ref[i * 7 + j, rows, :] for j in range(7)] + [zero])
            block = jnp.swapaxes(block, 0, 1)
            for s in range(8):
                t_ref[8 * half + s, i] = block[s]
    for to in range(4):
        for i in range(7):
            value = t_ref[4 * to + 2 * zl + xh, i]
            for copy in range(8):
                out_ref[to * 8 + copy, i] = value


def solve(counts, same, other, metrics):
    vmem = pl.BlockSpec(memory_space=pltpu.VMEM)
    field = pltpu.VMEM((49, 64, 128), jnp.float32)
    return pl.pallas_call(
        solve_kernel,
        out_shape=jax.ShapeDtypeStruct((NZ, 7, 8, 128), jnp.float32),
        in_specs=[pl.BlockSpec(memory_space=pltpu.SMEM)] + [vmem] * 3,
        out_specs=vmem,
        scratch_shapes=[
            field, field, field, field,
            pltpu.VMEM((49, 16, 128), jnp.float32),
            pltpu.VMEM((16, 7, 8, 128), jnp.float32),
        ],
        compiler_params=pltpu.CompilerParams(vmem_limit_bytes=40 * MIB),
    )(counts, same, other, metrics)


def pressure_kernel(coef_ref, rows_ref, out_ref):
    y = lax.axis_index("y")
    for zl in range(4):
        coefs = [coef_ref[(y * 4 + zl) * NZ + q] for q in range(NZ)]
        for i in range(7):
            value = tree_sum([coefs[q] * rows_ref[q, i] for q in range(NZ)])
            out_ref[zl, i] = value[0:7, :]


def pressure_planes(rows):
    vmem = pl.BlockSpec(memory_space=pltpu.VMEM)
    return pl.pallas_call(
        pressure_kernel,
        out_shape=jax.ShapeDtypeStruct((4, 7, 7, 128), jnp.float32),
        in_specs=[pl.BlockSpec(memory_space=pltpu.SMEM), vmem],
        out_specs=vmem,
        compiler_params=pltpu.CompilerParams(vmem_limit_bytes=16 * MIB),
    )(jnp.asarray(plane_coefs()), rows)


SWAP = [(0, 1), (1, 0)]
TURNS = [[(at, (at + back) % 4) for at in range(4)] for back in range(1, 4)]


def around(mine, axis):
    behind = lax.ppermute(mine, axis, TURNS[0])
    before = lax.ppermute(mine, axis, TURNS[2])
    half = mine.shape[0] // 2
    far = [
        lax.ppermute(behind[:half], axis, TURNS[0]),
        lax.ppermute(before[half:], axis, TURNS[2]),
    ]
    return behind, far, before


def gather_row(mine):
    pair = jnp.stack([mine, lax.ppermute(mine, "zl", SWAP)])
    behind, far, before = around(pair, RING_X)
    same = jnp.concatenate([pair, behind, *far, before]).reshape(4, 2, 4, 7, 8, 128)
    return same, lax.ppermute(same, "core", SWAP)


def after(value, other):
    return lax.optimization_barrier((value, other))[0]


def local(stress, velocity_grad, velocity, metric, iteration_counts):
    packed = jnp.pad(metric.reshape(147, 128), ((0, 5), (0, 0)))
    beside = lax.ppermute(packed, "zl", SWAP)
    right, left, up, down = pack_faces(stress)
    ahead = [(c, c + 1) for c in range(15)]
    above = [(e, e + 1) for e in range(3)]
    faces = (
        lax.ppermute(right, FLOW, ahead),
        lax.ppermute(left, FLOW, [(b, a) for a, b in ahead]),
        lax.ppermute(up, CROSS, above),
        lax.ppermute(down, CROSS, [(b, a) for a, b in above]),
    )
    pair = jnp.stack([after(packed, faces), beside])
    behind, far, before = around(pair, "zh")
    faces = after(faces, pair)
    new_stress, parts = stress_step(stress, velocity_grad, velocity, faces)
    parts = after(parts, (behind, before))
    ring = jnp.concatenate([pair, behind, *far, before])
    behind, far, before = around(ring, RING_X)
    parts = lax.all_to_all(parts, ROWS, 0, 0, tiled=True)
    mine = jnp.sum(parts.reshape(4, 8, 7, 8, 128), axis=1)
    ring = after(ring.reshape(4, 2, 152, 128), mine)
    plane = [part.reshape(-1, 2, 152, 128) for part in (behind, *far, before)]
    plane = jnp.concatenate([ring, *plane]).reshape(4, 4, 2, 152, 128)
    metrics = metric_fields(plane, lax.ppermute(plane, "core", SWAP))
    same, other = gather_row(mine)
    answer = solve(iteration_counts, same, other, metrics)
    answer = lax.all_to_all(answer, ROWS, 0, 0, tiled=True)
    return new_stress, pressure_planes(answer)


def solution(mesh):
    fine = Mesh(mesh.devices.reshape(SPLIT), PLANE + ("y",))
    field = P(None, "y", None, None, PLANE)
    return jax.shard_map(
        local,
        mesh=fine,
        in_specs=(field, field, field, P(None, None, None, PLANE), P()),
        out_specs=(field, P("y", None, None, PLANE)),
        check_vma=False,
    )
```

```python
import jax
import jax.numpy as jnp
import numpy as np
from jax import lax
from jax.experimental import pallas as pl
from jax.experimental.pallas import tpu as pltpu
from jax.sharding import Mesh
from jax.sharding import PartitionSpec as P

FLOW = ("z", "xh")
CROSS = ("xl", "core")
PLANE = ("z", "xh", "xl", "core")
RING_X = ("xh", "xl")
ROWS = ("xh", "xl", "y")
SPLIT = (8, 2, 2, 2, 8)

EY = 16
NZ = 32
DT_STEP = 0.01
SPAN_UNIT = 0.5
MASS_SCALE = 0.25
MIB = 1 << 20


def node_tables():
    nodes = np.array(
        [-1.0, -0.830223896278567, -0.468848793470714, 0.0,
         0.468848793470714, 0.830223896278567, 1.0]
    )
    weights = np.array(
        [1.0 / 21.0, 0.276826047361566, 0.431745381209863, 0.487619047619048,
         0.431745381209863, 0.276826047361566, 1.0 / 21.0]
    )
    bary = np.array(
        [1.0 / np.prod([nodes[c] - nodes[o] for o in range(7) if o != c]) for c in range(7)]
    )
    deriv = np.zeros((7, 7))
    for row in range(7):
        for col in range(7):
            if row != col:
                deriv[row, col] = bary[col] / bary[row] / (nodes[row] - nodes[col])
        deriv[row, row] = -np.sum(deriv[row])
    return deriv, weights


DERIV, WEIGHTS = node_tables()
LIFT = 2.0 / WEIGHTS[0]


def span_tables():
    ids = np.arange(NZ)
    harmonic = np.where(ids == 1, NZ // 2, ids // 2)
    sine = (ids % 2 == 1) & (ids != 1)
    phase = 2.0 * np.pi / NZ * (harmonic[:, None] * ids[None, :] % NZ)
    basis = np.where(sine[:, None], np.sin(phase), np.cos(phase))
    basis = basis * np.where(ids < 2, 1.0 / np.sqrt(NZ), np.sqrt(2.0 / NZ))[:, None]
    wavenum = SPAN_UNIT * harmonic
    slope = np.where(ids < 2, 0.0, np.where(sine, -wavenum, wavenum))
    return basis, slope[:, None] * basis[ids ^ 1], wavenum


BASIS, SLOPE, WAVENUM = span_tables()
ROW_AT = np.array([4 * (q % 8) + q // 8 for q in range(NZ)])


def source_coefs():
    table = np.zeros((8, NZ, 3, 4))
    for y in range(8):
        cols = slice(4 * y, 4 * y + 4)
        table[y, :, 0] = BASIS[ROW_AT, cols]
        table[y, :, 1] = -(WAVENUM[ROW_AT] ** 2)[:, None] * BASIS[ROW_AT, cols]
        table[y, :, 2] = 2.0 * SLOPE[ROW_AT, cols]
    return table.astype(np.float32).reshape(-1)


def plane_coefs():
    table = np.stack([BASIS.T[4 * y : 4 * y + 4][:, ROW_AT] for y in range(8)])
    return table.astype(np.float32).reshape(-1)


def line_apply(mat, f):
    even = [f[m] + f[6 - m] for m in range(3)]
    odd = [f[m] - f[6 - m] for m in range(3)]
    out = [None] * 7
    for i in range(3):
        from_odd = float(0.5 * (mat[i, 0] - mat[i, 6])) * odd[0]
        from_even = float(mat[i, 3]) * f[3]
        for m in range(3):
            from_even = from_even + float(0.5 * (mat[i, m] + mat[i, 6 - m])) * even[m]
            if m:
                from_odd = from_odd + float(0.5 * (mat[i, m] - mat[i, 6 - m])) * odd[m]
        out[i] = from_odd + from_even
        out[6 - i] = from_odd - from_even
    out[3] = float(mat[3, 0]) * odd[0] + float(mat[3, 1]) * odd[1] + float(mat[3, 2]) * odd[2]
    return out


def tree_sum(terms):
    while len(terms) > 1:
        terms = [sum(terms[i : i + 2][1:], terms[i]) for i in range(0, len(terms), 2)]
    return terms[0]


def lanes():
    return lax.broadcasted_iota(jnp.int32, (8, 128), 1)


def pack_kernel(s_ref, right_ref, left_ref, up_ref, down_ref, t_ref):
    lane = lanes()
    block, inner = lane // 16, lane % 16

    def plane(z, carry):
        for c in range(6):
            for i in range(7):
                t_ref[c, i, 0:7, :] = s_ref[c, z, i]
        zero = jnp.zeros((8, 128), jnp.float32)
        right, left = zero, zero
        for c in range(6):
            right = jnp.where(block == c, pltpu.roll(t_ref[c, 6], (16 * (c + 1)) % 128, 1), right)
            left = jnp.where(block == c, pltpu.roll(t_ref[c, 0], 16 * c, 1), left)
        right_ref[z] = right
        left_ref[z] = left
        for i in range(7):
            up, down = zero, zero
            for c in range(6):
                up = jnp.where(inner == c, pltpu.roll(t_ref[c, i], (c - 15) % 128, 1), up)
                down = jnp.where(inner == c, pltpu.roll(t_ref[c, i], c, 1), down)
            up_ref[z, i : i + 1, :] = up[6:7, :]
            down_ref[z, i : i + 1, :] = down[0:1, :]
        up_ref[z, 7:8, :] = zero[0:1, :]
        down_ref[z, 7:8, :] = zero[0:1, :]
        return carry

    for c in range(6):
        for i in range(7):
            t_ref[c, i] = jnp.zeros((8, 128), jnp.float32)
    lax.fori_loop(0, 4, plane, 0)


def pack_faces(stress):
    return pl.pallas_call(
        pack_kernel,
        out_shape=[jax.ShapeDtypeStruct((4, 8, 128), jnp.float32)] * 4,
        in_specs=[pl.BlockSpec(memory_space=pltpu.VMEM)],
        out_specs=[pl.BlockSpec(memory_space=pltpu.VMEM)] * 4,
        scratch_shapes=[pltpu.VMEM((6, 7, 8, 128), jnp.float32)],
        compiler_params=pltpu.CompilerParams(vmem_limit_bytes=16 * MIB),
    )(stress)


def stress_kernel(
    coef_ref, s_ref, g_ref, v_ref, left_ref, right_ref, below_ref, above_ref, dcol_ref,
    new_ref, rows_ref, t_ref, d_ref, n_ref, f_ref, p_ref, lb_ref,
):
    lane = lanes()
    inner = lane % 16
    row = lax.broadcasted_iota(jnp.int32, (8, 128), 0)
    twice = 2.0 * DERIV
    y = lax.axis_index("y")

    def across(ref, *at):
        total = dcol_ref[0] * ref[(*at, pl.ds(0, 1), slice(None))]
        for m in range(1, 7):
            total = total + dcol_ref[m] * ref[(*at, pl.ds(m, 1), slice(None))]
        return total

    zero = jnp.zeros((8, 128), jnp.float32)
    for i in range(7):
        for c in range(6):
            t_ref[c, i] = zero
        for c in range(11):
            lb_ref[c, i] = zero

    def plane(z, carry):
        for i in range(7):
            for c in range(6):
                t_ref[c, i, 0:7, :] = s_ref[c, z, i]
            for c in range(9):
                lb_ref[c, i, 0:7, :] = g_ref[c, z, i]
            for c in range(2):
                lb_ref[9 + c, i, 0:7, :] = v_ref[c, z, i]
        for c in range(6):
            slope = line_apply(twice, [t_ref[c, i] for i in range(7)])
            for i in range(7):
                d_ref[c, i] = slope[i]
        for i in range(7):
            u, v = lb_ref[9, i], lb_ref[10, i]
            away = jnp.where(row == 0, -v, v)
            away = jnp.where((row == 0) | (row == 6), jnp.minimum(away, 0.0), 0.0) * float(-LIFT)
            if i == 0:
                along = jnp.minimum(-u, 0.0) * float(-LIFT)
            if i == 6:
                along = jnp.minimum(u, 0.0) * float(-LIFT)
            grad = [lb_ref[c, i] for c in range(9)]
            tau = [t_ref[c, i] for c in range(6)]
            xx, yy, zz = tau[0] + 0.5, tau[1] + 0.5, tau[2] + 0.5
            full = ((xx, tau[3], tau[4]), (tau[3], yy, tau[5]), (tau[4], tau[5], zz))
            prod = [
                [tree_sum([grad[3 * a + k] * full[k][b] for k in range(3)]) for b in range(3)]
                for a in range(3)
            ]
            pairs = ((0, 0), (1, 1), (2, 2), (0, 1), (0, 2), (1, 2))
            for c, (a, b) in enumerate(pairs):
                forcing = prod[a][b] + prod[b][a] - tau[c]
                advect = u * d_ref[c, i] + v * across(t_ref, c, i)
                low = jnp.broadcast_to(t_ref[c, i, 6:7, :], (8, 128))
                low = pltpu.roll(low, 1, 1)
                got = jnp.broadcast_to(below_ref[z, i : i + 1, :], (8, 128))
                low = jnp.where(inner == 0, pltpu.roll(got, (128 - c) % 128, 1), low)
                high = jnp.broadcast_to(t_ref[c, i, 0:1, :], (8, 128))
                high = pltpu.roll(high, 127, 1)
                got = jnp.broadcast_to(above_ref[z, i : i + 1, :], (8, 128))
                high = jnp.where(inner == 15, pltpu.roll(got, 15 - c, 1), high)
                advect = advect + away * (tau[c] - jnp.where(row == 0, low, high))
                if i == 0:
                    mine = pltpu.roll(t_ref[c, 6], 16, 1)
                    got = pltpu.roll(left_ref[z], (128 - 16 * c) % 128, 1)
                    advect = advect + along * (tau[c] - jnp.where(lane < 16, got, mine))
                if i == 6:
                    mine = pltpu.roll(t_ref[c, 0], 112, 1)
                    got = pltpu.roll(right_ref[z], 112 - 16 * c, 1)
                    advect = advect + along * (tau[c] - jnp.where(lane >= 112, got, mine))
                fresh = tau[c] + DT_STEP * (forcing - advect)
                n_ref[c, i] = fresh
                new_ref[c, z, i] = fresh[0:7, :]
        first = line_apply(twice, [n_ref[0, i] for i in range(7)])
        first = [first[i] + across(n_ref, 3, i) for i in range(7)]
        planar = line_apply(twice, first)
        second = line_apply(twice, [n_ref[3, i] for i in range(7)])
        for i in range(7):
            f_ref[i] = second[i] + across(n_ref, 1, i)
        crossed = line_apply(twice, [n_ref[4, i] for i in range(7)])
        for i in range(7):
            p_ref[0, z, i] = planar[i] + across(f_ref, i)
            p_ref[1, z, i] = n_ref[2, i]
            p_ref[2, z, i] = crossed[i] + across(n_ref, 5, i)
        return carry

    lax.fori_loop(0, 4, plane, 0)

    def one_row(q, carry):
        base = (y * NZ + q) * 12
        coefs = [coef_ref[base + k] for k in range(12)]
        for i in range(7):
            rows_ref[q, i] = tree_sum(
                [coefs[4 * s + z] * p_ref[s, z, i] for s in range(3) for z in range(4)]
            )
        return carry

    lax.fori_loop(0, NZ, one_row, 0)


def stress_step(stress, grad, velocity, faces):
    dcol = np.zeros((7, 8, 128))
    dcol[:, :7, :] = 2.0 * DERIV.T[:, :, None]
    vmem = pl.BlockSpec(memory_space=pltpu.VMEM)
    return pl.pallas_call(
        stress_kernel,
        out_shape=[
            jax.ShapeDtypeStruct((6, 4, 7, 7, 128), jnp.float32),
            jax.ShapeDtypeStruct((NZ, 7, 8, 128), jnp.float32),
        ],
        in_specs=[pl.BlockSpec(memory_space=pltpu.SMEM)] + [vmem] * 8,
        out_specs=[vmem] * 2,
        scratch_shapes=[
            pltpu.VMEM((6, 7, 8, 128), jnp.float32),
            pltpu.VMEM((6, 7, 8, 128), jnp.float32),
            pltpu.VMEM((6, 7, 8, 128), jnp.float32),
            pltpu.VMEM((7, 8, 128), jnp.float32),
            pltpu.VMEM((3, 4, 7, 8, 128), jnp.float32),
            pltpu.VMEM((11, 7, 8, 128), jnp.float32),
        ],
        compiler_params=pltpu.CompilerParams(vmem_limit_bytes=24 * MIB),
    )(
        jnp.asarray(source_coefs()), stress, grad, velocity, *faces,
        jnp.asarray(dcol, jnp.float32),
    )


def metric_kernel(m_ref, q_ref):
    x = 2 * lax.axis_index("xh") + lax.axis_index("xl")

    def chunk(k, carry):
        from_xl, from_core, half = k // 4, k // 2 % 2, k % 2
        here = pl.ds(pl.multiple_of(k * 8, 8), 8)
        back = [(x - 2 * s - from_xl + 4) % 4 for s in range(2)]
        for tile in range(19):
            rows = slice(8 * tile, 8 * tile + 8)
            block = jnp.stack(
                [m_ref[(half * 4 + s // 2) * 2 + from_core, back[s % 2], rows, :] for s in range(8)]
            )
            block = jnp.swapaxes(block, 0, 1)
            for j in range(8):
                c, n = divmod(8 * tile + j, 49)
                if c < 3:
                    scale = WEIGHTS[n // 7] * WEIGHTS[n % 7] * (MASS_SCALE if c == 2 else 1.0)
                    q_ref[c, n, here, :] = float(scale) * block[j]
        return carry

    lax.fori_loop(0, 8, chunk, 0)


def metric_fields(gathered):
    vmem = pl.BlockSpec(memory_space=pltpu.VMEM)
    return pl.pallas_call(
        metric_kernel,
        out_shape=jax.ShapeDtypeStruct((3, 49, 64, 128), jnp.float32),
        in_specs=[vmem],
        out_specs=vmem,
        compiler_params=pltpu.CompilerParams(vmem_limit_bytes=24 * MIB),
    )(gathered)


def solve_kernel(
    count_ref, same_ref, other_ref, q_ref, out_ref, r_ref, d_ref, im_ref, mk_ref, x_ref, t_ref
):
    z, core = lax.axis_index("z"), lax.axis_index("core")
    row_id = 4 * lax.axis_index("y") + 2 * lax.axis_index("xh") + lax.axis_index("xl")
    harmonic = jnp.where(row_id == 1, NZ // 2, row_id // 2).astype(jnp.float32)
    wavesq = harmonic * harmonic * (SPAN_UNIT * SPAN_UNIT)
    own = [pl.ds(pl.multiple_of(((2 * to + core) * 2 + z // 4) * 8, 8), 8) for to in range(2)]
    flipped = DERIV.T
    zero = jnp.zeros((8, 128), jnp.float32)

    def here(k):
        return pl.ds(pl.multiple_of(k * 8, 8), 8)

    def chunk_in(quarter, carry):
        from_xl, half = quarter // 2, quarter % 2
        for ref, from_core in ((same_ref, core), (other_ref, 1 - core)):
            at = here((from_xl * 2 + from_core) * 2 + half)
            for i in range(7):
                block = jnp.stack(
                    [ref[half * 4 + s // 2, 2 * (s % 2) + from_xl, i] for s in range(8)]
                )
                block = jnp.swapaxes(block, 0, 1)
                for j in range(7):
                    n = i * 7 + j
                    mass = q_ref[2, n, at, :]
                    im_ref[n, at, :] = mass * block[j]
                    mk_ref[n, at, :] = wavesq * mass
                    d_ref[n, at, :] = zero
        return carry

    lax.fori_loop(0, 4, chunk_in, 0)
    for n in range(49):
        x_ref[0, n] = zero
        x_ref[1, n] = zero

    lane = lax.broadcasted_iota(jnp.int32, (64, 128), 1)
    spot = lax.broadcasted_iota(jnp.int32, (64, 128), 0)
    inner, c_pos = lane % 16, spot % 16
    wall = (
        (c_pos == 0) & (lane < 16),
        (c_pos == 15) & (lane >= 112),
        (spot < 16) & (inner == 0),
        (spot >= 48) & (inner == 15),
    )

    def join():
        for j in range(7):
            low, high = im_ref[j], im_ref[42 + j]
            moved = pltpu.roll(high, 16, 1)
            moved = jnp.where(lane < 16, pltpu.roll(moved, 1, 0), moved)
            back = pltpu.roll(low, 112, 1)
            back = jnp.where(lane >= 112, pltpu.roll(back, 63, 0), back)
            im_ref[j] = jnp.where(wall[0], 0.0, low + moved)
            im_ref[42 + j] = jnp.where(wall[1], 0.0, high + back)
        for i in range(7):
            low, high = im_ref[7 * i], im_ref[7 * i + 6]
            other = pltpu.roll(pltpu.roll(high, 113, 1), 16, 0)
            moved = jnp.where(inner == 0, other, pltpu.roll(high, 1, 1))
            other = pltpu.roll(pltpu.roll(low, 15, 1), 48, 0)
            back = jnp.where(inner == 15, other, pltpu.roll(low, 127, 1))
            im_ref[7 * i] = jnp.where(wall[2], 0.0, low + moved)
            im_ref[7 * i + 6] = jnp.where(wall[3], 0.0, high + back)

    def total(acc):
        return jnp.broadcast_to(jnp.sum(acc, axis=(0, 1), keepdims=True), (8, 128))

    def square(line, ends):
        inside = tree_sum([line[m] * line[m] for m in range(1, 6)])
        return ends * (inside + 0.5 * (line[0] * line[0] + line[6] * line[6]))

    def set_residual(k, acc):
        for i in range(7):
            line = []
            for j in range(7):
                value = im_ref[i * 7 + j, here(k), :]
                r_ref[i * 7 + j, here(k), :] = value
                line.append(value)
            acc = acc + square(line, 0.5 if i in (0, 6) else 1.0)
        return acc

    join()
    rho = total(lax.fori_loop(0, 8, set_residual, zero))

    def sweep(t, state):
        rho, beta = state

        def image(k, acc):
            at = here(k)
            for j in range(7):
                line = []
                for i in range(7):
                    n = i * 7 + j
                    value = r_ref[n, at, :] + beta * d_ref[n, at, :]
                    d_ref[n, at, :] = value
                    line.append(value)
                flux = line_apply(DERIV, line)
                flux = [flux[i] * q_ref[0, i * 7 + j, at, :] for i in range(7)]
                part = line_apply(flipped, flux)
                for i in range(7):
                    n = i * 7 + j
                    part[i] = part[i] + mk_ref[n, at, :] * line[i]
                    im_ref[n, at, :] = part[i]
                acc = acc + tree_sum([part[i] * line[i] for i in range(7)])
            for i in range(7):
                line = [d_ref[i * 7 + j, at, :] for j in range(7)]
                flux = line_apply(DERIV, line)
                flux = [flux[j] * q_ref[1, i * 7 + j, at, :] for j in range(7)]
                part = line_apply(flipped, flux)
                for j in range(7):
                    n = i * 7 + j
                    im_ref[n, at, :] = im_ref[n, at, :] + part[j]
                acc = acc + tree_sum([part[j] * line[j] for j in range(7)])
            return acc

        step = rho / total(lax.fori_loop(0, 8, image, zero))
        join()
        for n in range(49):
            for to in range(2):
                x_ref[to, n] = x_ref[to, n] + step * d_ref[n, own[to], :]

        def descend(k, acc):
            at = here(k)
            for i in range(7):
                line = []
                for j in range(7):
                    n = i * 7 + j
                    value = r_ref[n, at, :] - step * im_ref[n, at, :]
                    r_ref[n, at, :] = value
                    line.append(value)
                acc = acc + square(line, 0.5 if i in (0, 6) else 1.0)
            return acc

        fresh = total(lax.fori_loop(0, 8, descend, zero))
        return fresh, fresh / rho

    lax.fori_loop(0, count_ref[row_id], sweep, (rho, zero))

    for i in range(7):
        for to in range(2):
            block = jnp.stack([x_ref[to, i * 7 + j] for j in range(7)] + [zero])
            block = jnp.swapaxes(block, 0, 1)
            for s in range(8):
                t_ref[to, s, i] = block[s]
    for to in range(4):
        for i in range(7):
            value = t_ref[to % 2, z % 4 * 2 + to // 2, i]
            for copy in range(8):
                out_ref[to * 8 + copy, i] = value


def solve(counts, same, other, metrics):
    vmem = pl.BlockSpec(memory_space=pltpu.VMEM)
    field = pltpu.VMEM((49, 64, 128), jnp.float32)
    return pl.pallas_call(
        solve_kernel,
        out_shape=jax.ShapeDtypeStruct((NZ, 7, 8, 128), jnp.float32),
        in_specs=[pl.BlockSpec(memory_space=pltpu.SMEM)] + [vmem] * 3,
        out_specs=vmem,
        scratch_shapes=[
            field, field, field, field,
            pltpu.VMEM((2, 49, 8, 128), jnp.float32),
            pltpu.VMEM((2, 8, 7, 8, 128), jnp.float32),
        ],
        compiler_params=pltpu.CompilerParams(vmem_limit_bytes=40 * MIB),
    )(counts, same, other, metrics)


def pressure_kernel(coef_ref, rows_ref, out_ref):
    y = lax.axis_index("y")
    for zl in range(4):
        coefs = [coef_ref[(y * 4 + zl) * NZ + q] for q in range(NZ)]
        for i in range(7):
            value = tree_sum([coefs[q] * rows_ref[q, i] for q in range(NZ)])
            out_ref[zl, i] = value[0:7, :]


def pressure_planes(rows):
    vmem = pl.BlockSpec(memory_space=pltpu.VMEM)
    return pl.pallas_call(
        pressure_kernel,
        out_shape=jax.ShapeDtypeStruct((4, 7, 7, 128), jnp.float32),
        in_specs=[pl.BlockSpec(memory_space=pltpu.SMEM), vmem],
        out_specs=vmem,
        compiler_params=pltpu.CompilerParams(vmem_limit_bytes=16 * MIB),
    )(jnp.asarray(plane_coefs()), rows)


SWAP = [(0, 1), (1, 0)]
TURNS = [[(at, (at + back) % 4) for at in range(4)] for back in range(1, 4)]


def after(value, other):
    return lax.optimization_barrier((value, other))[0]


def local(stress, velocity_grad, velocity, metric, iteration_counts):
    packed = jnp.pad(metric.reshape(147, 128), ((0, 5), (0, 0)))
    turned = [lax.ppermute(packed, RING_X, turn) for turn in TURNS]
    right, left, up, down = pack_faces(stress)
    ahead = [(c, c + 1) for c in range(15)]
    above = [(e, e + 1) for e in range(3)]
    faces = (
        lax.ppermute(right, FLOW, ahead),
        lax.ppermute(left, FLOW, [(b, a) for a, b in ahead]),
        lax.ppermute(up, CROSS, above),
        lax.ppermute(down, CROSS, [(b, a) for a, b in above]),
    )
    ring = jnp.stack([after(packed, right)] + turned)
    faces = after(faces, ring)
    metrics = metric_fields(lax.all_gather(ring, ("z", "core")))
    new_stress, parts = stress_step(stress, velocity_grad, velocity, faces)
    parts = lax.all_to_all(parts, ROWS, 0, 0, tiled=True)
    mine = jnp.sum(parts.reshape(4, 8, 7, 8, 128), axis=1)
    same = lax.all_gather(mine, "z")
    other = lax.ppermute(same, "core", SWAP)
    answer = solve(iteration_counts, same, other, metrics)
    answer = lax.all_to_all(answer, ROWS, 0, 0, tiled=True)
    return new_stress, pressure_planes(answer)


def solution(mesh):
    fine = Mesh(mesh.devices.reshape(SPLIT), PLANE + ("y",))
    field = P(None, "y", None, None, PLANE)
    return jax.shard_map(
        local,
        mesh=fine,
        in_specs=(field, field, field, P(None, None, None, PLANE), P()),
        out_specs=(field, P("y", None, None, PLANE)),
        check_vma=False,
    )
```

```python
import jax
import jax.numpy as jnp
import numpy as np
from jax import lax
from jax.experimental import pallas as pl
from jax.experimental.pallas import tpu as pltpu
from jax.sharding import Mesh
from jax.sharding import PartitionSpec as P

FLOW = ("zh", "zl", "xh")
CROSS = ("xl", "core")
PLANE = ("zh", "zl", "xh", "xl", "core")
RING_X = ("xh", "xl")
ROWS = ("xh", "xl", "y")
SPLIT = (4, 2, 2, 2, 2, 8)

EY = 16
NZ = 32
DT_STEP = 0.01
SPAN_UNIT = 0.5
MASS_SCALE = 0.25
MIB = 1 << 20


def node_tables():
    nodes = np.array(
        [-1.0, -0.830223896278567, -0.468848793470714, 0.0,
         0.468848793470714, 0.830223896278567, 1.0]
    )
    weights = np.array(
        [1.0 / 21.0, 0.276826047361566, 0.431745381209863, 0.487619047619048,
         0.431745381209863, 0.276826047361566, 1.0 / 21.0]
    )
    bary = np.array(
        [1.0 / np.prod([nodes[c] - nodes[o] for o in range(7) if o != c]) for c in range(7)]
    )
    deriv = np.zeros((7, 7))
    for row in range(7):
        for col in range(7):
            if row != col:
                deriv[row, col] = bary[col] / bary[row] / (nodes[row] - nodes[col])
        deriv[row, row] = -np.sum(deriv[row])
    return deriv, weights


DERIV, WEIGHTS = node_tables()
LIFT = 2.0 / WEIGHTS[0]


def span_tables():
    ids = np.arange(NZ)
    harmonic = np.where(ids == 1, NZ // 2, ids // 2)
    sine = (ids % 2 == 1) & (ids != 1)
    phase = 2.0 * np.pi / NZ * (harmonic[:, None] * ids[None, :] % NZ)
    basis = np.where(sine[:, None], np.sin(phase), np.cos(phase))
    basis = basis * np.where(ids < 2, 1.0 / np.sqrt(NZ), np.sqrt(2.0 / NZ))[:, None]
    wavenum = SPAN_UNIT * harmonic
    slope = np.where(ids < 2, 0.0, np.where(sine, -wavenum, wavenum))
    return basis, slope[:, None] * basis[ids ^ 1], wavenum


BASIS, SLOPE, WAVENUM = span_tables()
ROW_AT = np.array([4 * (q % 8) + q // 8 for q in range(NZ)])


def source_coefs():
    table = np.zeros((8, NZ, 3, 4))
    for y in range(8):
        cols = slice(4 * y, 4 * y + 4)
        table[y, :, 0] = BASIS[ROW_AT, cols]
        table[y, :, 1] = -(WAVENUM[ROW_AT] ** 2)[:, None] * BASIS[ROW_AT, cols]
        table[y, :, 2] = 2.0 * SLOPE[ROW_AT, cols]
    return table.astype(np.float32).reshape(-1)


def plane_coefs():
    table = np.stack([BASIS.T[4 * y : 4 * y + 4][:, ROW_AT] for y in range(8)])
    return table.astype(np.float32).reshape(-1)


def line_apply(mat, f):
    even = [f[m] + f[6 - m] for m in range(3)]
    odd = [f[m] - f[6 - m] for m in range(3)]
    out = [None] * 7
    for i in range(3):
        from_odd = float(0.5 * (mat[i, 0] - mat[i, 6])) * odd[0]
        from_even = float(mat[i, 3]) * f[3]
        for m in range(3):
            from_even = from_even + float(0.5 * (mat[i, m] + mat[i, 6 - m])) * even[m]
            if m:
                from_odd = from_odd + float(0.5 * (mat[i, m] - mat[i, 6 - m])) * odd[m]
        out[i] = from_odd + from_even
        out[6 - i] = from_odd - from_even
    out[3] = float(mat[3, 0]) * odd[0] + float(mat[3, 1]) * odd[1] + float(mat[3, 2]) * odd[2]
    return out


def tree_sum(terms):
    while len(terms) > 1:
        terms = [sum(terms[i : i + 2][1:], terms[i]) for i in range(0, len(terms), 2)]
    return terms[0]


def lanes():
    return lax.broadcasted_iota(jnp.int32, (8, 128), 1)


def pack_kernel(s_ref, right_ref, left_ref, up_ref, down_ref, t_ref):
    lane = lanes()
    block, inner = lane // 16, lane % 16

    def plane(z, carry):
        for c in range(6):
            for i in range(7):
                t_ref[c, i, 0:7, :] = s_ref[c, z, i]
        zero = jnp.zeros((8, 128), jnp.float32)
        right, left = zero, zero
        for c in range(6):
            right = jnp.where(block == c, pltpu.roll(t_ref[c, 6], (16 * (c + 1)) % 128, 1), right)
            left = jnp.where(block == c, pltpu.roll(t_ref[c, 0], 16 * c, 1), left)
        right_ref[z] = right
        left_ref[z] = left
        for i in range(7):
            up, down = zero, zero
            for c in range(6):
                up = jnp.where(inner == c, pltpu.roll(t_ref[c, i], (c - 15) % 128, 1), up)
                down = jnp.where(inner == c, pltpu.roll(t_ref[c, i], c, 1), down)
            up_ref[z, i : i + 1, :] = up[6:7, :]
            down_ref[z, i : i + 1, :] = down[0:1, :]
        up_ref[z, 7:8, :] = zero[0:1, :]
        down_ref[z, 7:8, :] = zero[0:1, :]
        return carry

    for c in range(6):
        for i in range(7):
            t_ref[c, i] = jnp.zeros((8, 128), jnp.float32)
    lax.fori_loop(0, 4, plane, 0)


def pack_faces(stress):
    return pl.pallas_call(
        pack_kernel,
        out_shape=[jax.ShapeDtypeStruct((4, 8, 128), jnp.float32)] * 4,
        in_specs=[pl.BlockSpec(memory_space=pltpu.VMEM)],
        out_specs=[pl.BlockSpec(memory_space=pltpu.VMEM)] * 4,
        scratch_shapes=[pltpu.VMEM((6, 7, 8, 128), jnp.float32)],
        compiler_params=pltpu.CompilerParams(vmem_limit_bytes=16 * MIB),
    )(stress)


def stress_kernel(
    coef_ref, s_ref, g_ref, v_ref, left_ref, right_ref, below_ref, above_ref, dcol_ref,
    new_ref, rows_ref, t_ref, d_ref, n_ref, f_ref, p_ref, lb_ref,
):
    lane = lanes()
    inner = lane % 16
    row = lax.broadcasted_iota(jnp.int32, (8, 128), 0)
    twice = 2.0 * DERIV
    y = lax.axis_index("y")

    def across(ref, *at):
        total = dcol_ref[0] * ref[(*at, pl.ds(0, 1), slice(None))]
        for m in range(1, 7):
            total = total + dcol_ref[m] * ref[(*at, pl.ds(m, 1), slice(None))]
        return total

    zero = jnp.zeros((8, 128), jnp.float32)
    for i in range(7):
        for c in range(6):
            t_ref[c, i] = zero
        for c in range(11):
            lb_ref[c, i] = zero

    def plane(z, carry):
        for i in range(7):
            for c in range(6):
                t_ref[c, i, 0:7, :] = s_ref[c, z, i]
            for c in range(9):
                lb_ref[c, i, 0:7, :] = g_ref[c, z, i]
            for c in range(2):
                lb_ref[9 + c, i, 0:7, :] = v_ref[c, z, i]
        for c in range(6):
            slope = line_apply(twice, [t_ref[c, i] for i in range(7)])
            for i in range(7):
                d_ref[c, i] = slope[i]
        for i in range(7):
            u, v = lb_ref[9, i], lb_ref[10, i]
            away = jnp.where(row == 0, -v, v)
            away = jnp.where((row == 0) | (row == 6), jnp.minimum(away, 0.0), 0.0) * float(-LIFT)
            if i == 0:
                along = jnp.minimum(-u, 0.0) * float(-LIFT)
            if i == 6:
                along = jnp.minimum(u, 0.0) * float(-LIFT)
            grad = [lb_ref[c, i] for c in range(9)]
            tau = [t_ref[c, i] for c in range(6)]
            xx, yy, zz = tau[0] + 0.5, tau[1] + 0.5, tau[2] + 0.5
            full = ((xx, tau[3], tau[4]), (tau[3], yy, tau[5]), (tau[4], tau[5], zz))
            prod = [
                [tree_sum([grad[3 * a + k] * full[k][b] for k in range(3)]) for b in range(3)]
                for a in range(3)
            ]
            pairs = ((0, 0), (1, 1), (2, 2), (0, 1), (0, 2), (1, 2))
            for c, (a, b) in enumerate(pairs):
                forcing = prod[a][b] + prod[b][a] - tau[c]
                advect = u * d_ref[c, i] + v * across(t_ref, c, i)
                low = jnp.broadcast_to(t_ref[c, i, 6:7, :], (8, 128))
                low = pltpu.roll(low, 1, 1)
                got = jnp.broadcast_to(below_ref[z, i : i + 1, :], (8, 128))
                low = jnp.where(inner == 0, pltpu.roll(got, (128 - c) % 128, 1), low)
                high = jnp.broadcast_to(t_ref[c, i, 0:1, :], (8, 128))
                high = pltpu.roll(high, 127, 1)
                got = jnp.broadcast_to(above_ref[z, i : i + 1, :], (8, 128))
                high = jnp.where(inner == 15, pltpu.roll(got, 15 - c, 1), high)
                advect = advect + away * (tau[c] - jnp.where(row == 0, low, high))
                if i == 0:
                    mine = pltpu.roll(t_ref[c, 6], 16, 1)
                    got = pltpu.roll(left_ref[z], (128 - 16 * c) % 128, 1)
                    advect = advect + along * (tau[c] - jnp.where(lane < 16, got, mine))
                if i == 6:
                    mine = pltpu.roll(t_ref[c, 0], 112, 1)
                    got = pltpu.roll(right_ref[z], 112 - 16 * c, 1)
                    advect = advect + along * (tau[c] - jnp.where(lane >= 112, got, mine))
                fresh = tau[c] + DT_STEP * (forcing - advect)
                n_ref[c, i] = fresh
                new_ref[c, z, i] = fresh[0:7, :]
        first = line_apply(twice, [n_ref[0, i] for i in range(7)])
        first = [first[i] + across(n_ref, 3, i) for i in range(7)]
        planar = line_apply(twice, first)
        second = line_apply(twice, [n_ref[3, i] for i in range(7)])
        for i in range(7):
            f_ref[i] = second[i] + across(n_ref, 1, i)
        crossed = line_apply(twice, [n_ref[4, i] for i in range(7)])
        for i in range(7):
            p_ref[0, z, i] = planar[i] + across(f_ref, i)
            p_ref[1, z, i] = n_ref[2, i]
            p_ref[2, z, i] = crossed[i] + across(n_ref, 5, i)
        return carry

    lax.fori_loop(0, 4, plane, 0)

    def one_row(q, carry):
        base = (y * NZ + q) * 12
        coefs = [coef_ref[base + k] for k in range(12)]
        for i in range(7):
            rows_ref[q, i] = tree_sum(
                [coefs[4 * s + z] * p_ref[s, z, i] for s in range(3) for z in range(4)]
            )
        return carry

    lax.fori_loop(0, NZ, one_row, 0)


def stress_step(stress, grad, velocity, faces):
    dcol = np.zeros((7, 8, 128))
    dcol[:, :7, :] = 2.0 * DERIV.T[:, :, None]
    vmem = pl.BlockSpec(memory_space=pltpu.VMEM)
    return pl.pallas_call(
        stress_kernel,
        out_shape=[
            jax.ShapeDtypeStruct((6, 4, 7, 7, 128), jnp.float32),
            jax.ShapeDtypeStruct((NZ, 7, 8, 128), jnp.float32),
        ],
        in_specs=[pl.BlockSpec(memory_space=pltpu.SMEM)] + [vmem] * 8,
        out_specs=[vmem] * 2,
        scratch_shapes=[
            pltpu.VMEM((6, 7, 8, 128), jnp.float32),
            pltpu.VMEM((6, 7, 8, 128), jnp.float32),
            pltpu.VMEM((6, 7, 8, 128), jnp.float32),
            pltpu.VMEM((7, 8, 128), jnp.float32),
            pltpu.VMEM((3, 4, 7, 8, 128), jnp.float32),
            pltpu.VMEM((11, 7, 8, 128), jnp.float32),
        ],
        compiler_params=pltpu.CompilerParams(vmem_limit_bytes=24 * MIB),
    )(
        jnp.asarray(source_coefs()), stress, grad, velocity, *faces,
        jnp.asarray(dcol, jnp.float32),
    )


def metric_kernel(m_ref, q_ref):
    x = 2 * lax.axis_index("xh") + lax.axis_index("xl")

    def chunk(k, carry):
        from_xl, from_core, half = k // 4, k // 2 % 2, k % 2
        here = pl.ds(pl.multiple_of(k * 8, 8), 8)
        back = [(x - 2 * s - from_xl + 4) % 4 for s in range(2)]
        for tile in range(19):
            rows = slice(8 * tile, 8 * tile + 8)
            block = jnp.stack(
                [m_ref[(half * 4 + s // 2) * 2 + from_core, back[s % 2], rows, :] for s in range(8)]
            )
            block = jnp.swapaxes(block, 0, 1)
            for j in range(8):
                c, n = divmod(8 * tile + j, 49)
                if c < 3:
                    scale = WEIGHTS[n // 7] * WEIGHTS[n % 7] * (MASS_SCALE if c == 2 else 1.0)
                    q_ref[c, n, here, :] = float(scale) * block[j]
        return carry

    lax.fori_loop(0, 8, chunk, 0)


def metric_fields(gathered):
    vmem = pl.BlockSpec(memory_space=pltpu.VMEM)
    return pl.pallas_call(
        metric_kernel,
        out_shape=jax.ShapeDtypeStruct((3, 49, 64, 128), jnp.float32),
        in_specs=[vmem],
        out_specs=vmem,
        compiler_params=pltpu.CompilerParams(vmem_limit_bytes=24 * MIB),
    )(gathered)


def solve_kernel(
    count_ref, same_ref, other_ref, q_ref, out_ref, r_ref, d_ref, im_ref, mk_ref, x_ref, t_ref
):
    zl, core = lax.axis_index("zl"), lax.axis_index("core")
    z = 2 * lax.axis_index("zh") + zl
    flip = [zl, 1 - zl]
    row_id = 4 * lax.axis_index("y") + 2 * lax.axis_index("xh") + lax.axis_index("xl")
    harmonic = jnp.where(row_id == 1, NZ // 2, row_id // 2).astype(jnp.float32)
    wavesq = harmonic * harmonic * (SPAN_UNIT * SPAN_UNIT)
    own = [pl.ds(pl.multiple_of(((2 * to + core) * 2 + z // 4) * 8, 8), 8) for to in range(2)]
    flipped = DERIV.T
    zero = jnp.zeros((8, 128), jnp.float32)

    def here(k):
        return pl.ds(pl.multiple_of(k * 8, 8), 8)

    def chunk_in(quarter, carry):
        from_xl, half = quarter // 2, quarter % 2
        for ref, from_core in ((same_ref, core), (other_ref, 1 - core)):
            at = here((from_xl * 2 + from_core) * 2 + half)
            for i in range(7):
                block = jnp.stack(
                    [
                        ref[half * 2 + s // 4, flip[s // 2 % 2], 2 * (s % 2) + from_xl, i]
                        for s in range(8)
                    ]
                )
                block = jnp.swapaxes(block, 0, 1)
                for j in range(7):
                    n = i * 7 + j
                    mass = q_ref[2, n, at, :]
                    im_ref[n, at, :] = mass * block[j]
                    mk_ref[n, at, :] = wavesq * mass
                    d_ref[n, at, :] = zero
        return carry

    lax.fori_loop(0, 4, chunk_in, 0)
    for n in range(49):
        x_ref[0, n] = zero
        x_ref[1, n] = zero

    lane = lax.broadcasted_iota(jnp.int32, (64, 128), 1)
    spot = lax.broadcasted_iota(jnp.int32, (64, 128), 0)
    inner, c_pos = lane % 16, spot % 16
    wall = (
        (c_pos == 0) & (lane < 16),
        (c_pos == 15) & (lane >= 112),
        (spot < 16) & (inner == 0),
        (spot >= 48) & (inner == 15),
    )

    def join():
        for j in range(7):
            low, high = im_ref[j], im_ref[42 + j]
            moved = pltpu.roll(high, 16, 1)
            moved = jnp.where(lane < 16, pltpu.roll(moved, 1, 0), moved)
            back = pltpu.roll(low, 112, 1)
            back = jnp.where(lane >= 112, pltpu.roll(back, 63, 0), back)
            im_ref[j] = jnp.where(wall[0], 0.0, low + moved)
            im_ref[42 + j] = jnp.where(wall[1], 0.0, high + back)
        for i in range(7):
            low, high = im_ref[7 * i], im_ref[7 * i + 6]
            other = pltpu.roll(pltpu.roll(high, 113, 1), 16, 0)
            moved = jnp.where(inner == 0, other, pltpu.roll(high, 1, 1))
            other = pltpu.roll(pltpu.roll(low, 15, 1), 48, 0)
            back = jnp.where(inner == 15, other, pltpu.roll(low, 127, 1))
            im_ref[7 * i] = jnp.where(wall[2], 0.0, low + moved)
            im_ref[7 * i + 6] = jnp.where(wall[3], 0.0, high + back)

    def total(acc):
        return jnp.broadcast_to(jnp.sum(acc, axis=(0, 1), keepdims=True), (8, 128))

    def square(line, ends):
        inside = tree_sum([line[m] * line[m] for m in range(1, 6)])
        return ends * (inside + 0.5 * (line[0] * line[0] + line[6] * line[6]))

    def set_residual(k, acc):
        for i in range(7):
            line = []
            for j in range(7):
                value = im_ref[i * 7 + j, here(k), :]
                r_ref[i * 7 + j, here(k), :] = value
                line.append(value)
            acc = acc + square(line, 0.5 if i in (0, 6) else 1.0)
        return acc

    join()
    rho = total(lax.fori_loop(0, 8, set_residual, zero))

    def sweep(t, state):
        rho, beta = state

        def image(k, acc):
            at = here(k)
            for j in range(7):
                line = []
                for i in range(7):
                    n = i * 7 + j
                    value = r_ref[n, at, :] + beta * d_ref[n, at, :]
                    d_ref[n, at, :] = value
                    line.append(value)
                flux = line_apply(DERIV, line)
                flux = [flux[i] * q_ref[0, i * 7 + j, at, :] for i in range(7)]
                part = line_apply(flipped, flux)
                for i in range(7):
                    n = i * 7 + j
                    part[i] = part[i] + mk_ref[n, at, :] * line[i]
                    im_ref[n, at, :] = part[i]
                acc = acc + tree_sum([part[i] * line[i] for i in range(7)])
            for i in range(7):
                line = [d_ref[i * 7 + j, at, :] for j in range(7)]
                flux = line_apply(DERIV, line)
                flux = [flux[j] * q_ref[1, i * 7 + j, at, :] for j in range(7)]
                part = line_apply(flipped, flux)
                for j in range(7):
                    n = i * 7 + j
                    im_ref[n, at, :] = im_ref[n, at, :] + part[j]
                acc = acc + tree_sum([part[j] * line[j] for j in range(7)])
            return acc

        step = rho / total(lax.fori_loop(0, 8, image, zero))
        join()
        for n in range(49):
            for to in range(2):
                x_ref[to, n] = x_ref[to, n] + step * d_ref[n, own[to], :]

        def descend(k, acc):
            at = here(k)
            for i in range(7):
                line = []
                for j in range(7):
                    n = i * 7 + j
                    value = r_ref[n, at, :] - step * im_ref[n, at, :]
                    r_ref[n, at, :] = value
                    line.append(value)
                acc = acc + square(line, 0.5 if i in (0, 6) else 1.0)
            return acc

        fresh = total(lax.fori_loop(0, 8, descend, zero))
        return fresh, fresh / rho

    lax.fori_loop(0, count_ref[row_id], sweep, (rho, zero))

    for i in range(7):
        for to in range(2):
            block = jnp.stack([x_ref[to, i * 7 + j] for j in range(7)] + [zero])
            block = jnp.swapaxes(block, 0, 1)
            for s in range(8):
                t_ref[to, s, i] = block[s]
    for to in range(4):
        for i in range(7):
            value = t_ref[to % 2, z % 4 * 2 + to // 2, i]
            for copy in range(8):
                out_ref[to * 8 + copy, i] = value


def solve(counts, same, other, metrics):
    vmem = pl.BlockSpec(memory_space=pltpu.VMEM)
    field = pltpu.VMEM((49, 64, 128), jnp.float32)
    return pl.pallas_call(
        solve_kernel,
        out_shape=jax.ShapeDtypeStruct((NZ, 7, 8, 128), jnp.float32),
        in_specs=[pl.BlockSpec(memory_space=pltpu.SMEM)] + [vmem] * 3,
        out_specs=vmem,
        scratch_shapes=[
            field, field, field, field,
            pltpu.VMEM((2, 49, 8, 128), jnp.float32),
            pltpu.VMEM((2, 8, 7, 8, 128), jnp.float32),
        ],
        compiler_params=pltpu.CompilerParams(vmem_limit_bytes=40 * MIB),
    )(counts, same, other, metrics)


def pressure_kernel(coef_ref, rows_ref, out_ref):
    y = lax.axis_index("y")
    for zl in range(4):
        coefs = [coef_ref[(y * 4 + zl) * NZ + q] for q in range(NZ)]
        for i in range(7):
            value = tree_sum([coefs[q] * rows_ref[q, i] for q in range(NZ)])
            out_ref[zl, i] = value[0:7, :]


def pressure_planes(rows):
    vmem = pl.BlockSpec(memory_space=pltpu.VMEM)
    return pl.pallas_call(
        pressure_kernel,
        out_shape=jax.ShapeDtypeStruct((4, 7, 7, 128), jnp.float32),
        in_specs=[pl.BlockSpec(memory_space=pltpu.SMEM), vmem],
        out_specs=vmem,
        compiler_params=pltpu.CompilerParams(vmem_limit_bytes=16 * MIB),
    )(jnp.asarray(plane_coefs()), rows)


SWAP = [(0, 1), (1, 0)]
TURNS = [[(at, (at + back) % 4) for at in range(4)] for back in range(1, 4)]


def after(value, other):
    return lax.optimization_barrier((value, other))[0]


def local(stress, velocity_grad, velocity, metric, iteration_counts):
    packed = jnp.pad(metric.reshape(147, 128), ((0, 5), (0, 0)))
    right, left, up, down = pack_faces(stress)
    ahead = [(c, c + 1) for c in range(15)]
    above = [(e, e + 1) for e in range(3)]
    faces = (
        lax.ppermute(right, FLOW, ahead),
        lax.ppermute(left, FLOW, [(b, a) for a, b in ahead]),
        lax.ppermute(up, CROSS, above),
        lax.ppermute(down, CROSS, [(b, a) for a, b in above]),
    )
    packed = after(packed, faces)
    turned = [lax.ppermute(packed, RING_X, turn) for turn in TURNS]
    new_stress, parts = stress_step(stress, velocity_grad, velocity, faces)
    ring = jnp.stack([after(packed, parts)] + turned)
    metrics = metric_fields(lax.all_gather(ring, ("zh", "zl", "core")))
    parts = lax.all_to_all(after(parts, ring), ROWS, 0, 0, tiled=True)
    mine = jnp.sum(parts.reshape(4, 8, 7, 8, 128), axis=1)
    pair = jnp.stack([mine, lax.ppermute(mine, "zl", SWAP)])
    same = lax.all_gather(pair, "zh")
    other = lax.ppermute(same, "core", SWAP)
    answer = solve(iteration_counts, same, other, metrics)
    answer = lax.all_to_all(answer, ROWS, 0, 0, tiled=True)
    return new_stress, pressure_planes(answer)


def solution(mesh):
    fine = Mesh(mesh.devices.reshape(SPLIT), PLANE + ("y",))
    field = P(None, "y", None, None, PLANE)
    return jax.shard_map(
        local,
        mesh=fine,
        in_specs=(field, field, field, P(None, None, None, PLANE), P()),
        out_specs=(field, P("y", None, None, PLANE)),
        check_vma=False,
    )
```

```python
import jax
import jax.numpy as jnp
import numpy as np
from jax import lax
from jax.experimental import pallas as pl
from jax.experimental.pallas import tpu as pltpu
from jax.sharding import Mesh
from jax.sharding import PartitionSpec as P

FLOW = ("zh", "zl", "xh")
CROSS = ("xl", "core")
PLANE = ("zh", "zl", "xh", "xl", "core")
RING_X = ("xh", "xl")
ROWS = ("zh", "y")
SPLIT = (4, 2, 2, 2, 2, 8)

EY = 16
NZ = 32
DT_STEP = 0.01
SPAN_UNIT = 0.5
MASS_SCALE = 0.25
MIB = 1 << 20


def node_tables():
    nodes = np.array(
        [-1.0, -0.830223896278567, -0.468848793470714, 0.0,
         0.468848793470714, 0.830223896278567, 1.0]
    )
    weights = np.array(
        [1.0 / 21.0, 0.276826047361566, 0.431745381209863, 0.487619047619048,
         0.431745381209863, 0.276826047361566, 1.0 / 21.0]
    )
    bary = np.array(
        [1.0 / np.prod([nodes[c] - nodes[o] for o in range(7) if o != c]) for c in range(7)]
    )
    deriv = np.zeros((7, 7))
    for row in range(7):
        for col in range(7):
            if row != col:
                deriv[row, col] = bary[col] / bary[row] / (nodes[row] - nodes[col])
        deriv[row, row] = -np.sum(deriv[row])
    return deriv, weights


DERIV, WEIGHTS = node_tables()
LIFT = 2.0 / WEIGHTS[0]


def span_tables():
    ids = np.arange(NZ)
    harmonic = np.where(ids == 1, NZ // 2, ids // 2)
    sine = (ids % 2 == 1) & (ids != 1)
    phase = 2.0 * np.pi / NZ * (harmonic[:, None] * ids[None, :] % NZ)
    basis = np.where(sine[:, None], np.sin(phase), np.cos(phase))
    basis = basis * np.where(ids < 2, 1.0 / np.sqrt(NZ), np.sqrt(2.0 / NZ))[:, None]
    wavenum = SPAN_UNIT * harmonic
    slope = np.where(ids < 2, 0.0, np.where(sine, -wavenum, wavenum))
    return basis, slope[:, None] * basis[ids ^ 1], wavenum


BASIS, SLOPE, WAVENUM = span_tables()
ROW_AT = np.array([4 * (q % 8) + q // 8 for q in range(NZ)])


def source_coefs():
    table = np.zeros((8, NZ, 3, 4))
    for y in range(8):
        cols = slice(4 * y, 4 * y + 4)
        table[y, :, 0] = BASIS[ROW_AT, cols]
        table[y, :, 1] = -(WAVENUM[ROW_AT] ** 2)[:, None] * BASIS[ROW_AT, cols]
        table[y, :, 2] = 2.0 * SLOPE[ROW_AT, cols]
    return table.astype(np.float32).reshape(-1)


def plane_coefs():
    table = np.stack([BASIS.T[4 * y : 4 * y + 4][:, ROW_AT] for y in range(8)])
    return table.astype(np.float32).reshape(-1)


def line_apply(mat, f):
    even = [f[m] + f[6 - m] for m in range(3)]
    odd = [f[m] - f[6 - m] for m in range(3)]
    out = [None] * 7
    for i in range(3):
        from_odd = float(0.5 * (mat[i, 0] - mat[i, 6])) * odd[0]
        from_even = float(mat[i, 3]) * f[3]
        for m in range(3):
            from_even = from_even + float(0.5 * (mat[i, m] + mat[i, 6 - m])) * even[m]
            if m:
                from_odd = from_odd + float(0.5 * (mat[i, m] - mat[i, 6 - m])) * odd[m]
        out[i] = from_odd + from_even
        out[6 - i] = from_odd - from_even
    out[3] = float(mat[3, 0]) * odd[0] + float(mat[3, 1]) * odd[1] + float(mat[3, 2]) * odd[2]
    return out


def tree_sum(terms):
    while len(terms) > 1:
        terms = [sum(terms[i : i + 2][1:], terms[i]) for i in range(0, len(terms), 2)]
    return terms[0]


def lanes():
    return lax.broadcasted_iota(jnp.int32, (8, 128), 1)


def pack_kernel(s_ref, right_ref, left_ref, up_ref, down_ref, t_ref):
    lane = lanes()
    block, inner = lane // 16, lane % 16

    def plane(z, carry):
        for c in range(6):
            for i in range(7):
                t_ref[c, i, 0:7, :] = s_ref[c, z, i]
        zero = jnp.zeros((8, 128), jnp.float32)
        right, left = zero, zero
        for c in range(6):
            right = jnp.where(block == c, pltpu.roll(t_ref[c, 6], (16 * (c + 1)) % 128, 1), right)
            left = jnp.where(block == c, pltpu.roll(t_ref[c, 0], 16 * c, 1), left)
        right_ref[z] = right
        left_ref[z] = left
        for i in range(7):
            up, down = zero, zero
            for c in range(6):
                up = jnp.where(inner == c, pltpu.roll(t_ref[c, i], (c - 15) % 128, 1), up)
                down = jnp.where(inner == c, pltpu.roll(t_ref[c, i], c, 1), down)
            up_ref[z, i : i + 1, :] = up[6:7, :]
            down_ref[z, i : i + 1, :] = down[0:1, :]
        up_ref[z, 7:8, :] = zero[0:1, :]
        down_ref[z, 7:8, :] = zero[0:1, :]
        return carry

    for c in range(6):
        for i in range(7):
            t_ref[c, i] = jnp.zeros((8, 128), jnp.float32)
    lax.fori_loop(0, 4, plane, 0)


def pack_faces(stress):
    return pl.pallas_call(
        pack_kernel,
        out_shape=[jax.ShapeDtypeStruct((4, 8, 128), jnp.float32)] * 4,
        in_specs=[pl.BlockSpec(memory_space=pltpu.VMEM)],
        out_specs=[pl.BlockSpec(memory_space=pltpu.VMEM)] * 4,
        scratch_shapes=[pltpu.VMEM((6, 7, 8, 128), jnp.float32)],
        compiler_params=pltpu.CompilerParams(vmem_limit_bytes=16 * MIB),
    )(stress)


def stress_kernel(
    coef_ref, s_ref, g_ref, v_ref, left_ref, right_ref, below_ref, above_ref, dcol_ref,
    new_ref, rows_ref, t_ref, d_ref, n_ref, f_ref, p_ref, lb_ref,
):
    lane = lanes()
    inner = lane % 16
    row = lax.broadcasted_iota(jnp.int32, (8, 128), 0)
    twice = 2.0 * DERIV
    y = lax.axis_index("y")

    def across(ref, *at):
        total = dcol_ref[0] * ref[(*at, pl.ds(0, 1), slice(None))]
        for m in range(1, 7):
            total = total + dcol_ref[m] * ref[(*at, pl.ds(m, 1), slice(None))]
        return total

    zero = jnp.zeros((8, 128), jnp.float32)
    for i in range(7):
        for c in range(6):
            t_ref[c, i] = zero
        for c in range(11):
            lb_ref[c, i] = zero

    def plane(z, carry):
        for i in range(7):
            for c in range(6):
                t_ref[c, i, 0:7, :] = s_ref[c, z, i]
            for c in range(9):
                lb_ref[c, i, 0:7, :] = g_ref[c, z, i]
            for c in range(2):
                lb_ref[9 + c, i, 0:7, :] = v_ref[c, z, i]
        for c in range(6):
            slope = line_apply(twice, [t_ref[c, i] for i in range(7)])
            for i in range(7):
                d_ref[c, i] = slope[i]
        for i in range(7):
            u, v = lb_ref[9, i], lb_ref[10, i]
            away = jnp.where(row == 0, -v, v)
            away = jnp.where((row == 0) | (row == 6), jnp.minimum(away, 0.0), 0.0) * float(-LIFT)
            if i == 0:
                along = jnp.minimum(-u, 0.0) * float(-LIFT)
            if i == 6:
                along = jnp.minimum(u, 0.0) * float(-LIFT)
            grad = [lb_ref[c, i] for c in range(9)]
            tau = [t_ref[c, i] for c in range(6)]
            xx, yy, zz = tau[0] + 0.5, tau[1] + 0.5, tau[2] + 0.5
            full = ((xx, tau[3], tau[4]), (tau[3], yy, tau[5]), (tau[4], tau[5], zz))
            prod = [
                [tree_sum([grad[3 * a + k] * full[k][b] for k in range(3)]) for b in range(3)]
                for a in range(3)
            ]
            pairs = ((0, 0), (1, 1), (2, 2), (0, 1), (0, 2), (1, 2))
            for c, (a, b) in enumerate(pairs):
                forcing = prod[a][b] + prod[b][a] - tau[c]
                advect = u * d_ref[c, i] + v * across(t_ref, c, i)
                low = jnp.broadcast_to(t_ref[c, i, 6:7, :], (8, 128))
                low = pltpu.roll(low, 1, 1)
                got = jnp.broadcast_to(below_ref[z, i : i + 1, :], (8, 128))
                low = jnp.where(inner == 0, pltpu.roll(got, (128 - c) % 128, 1), low)
                high = jnp.broadcast_to(t_ref[c, i, 0:1, :], (8, 128))
                high = pltpu.roll(high, 127, 1)
                got = jnp.broadcast_to(above_ref[z, i : i + 1, :], (8, 128))
                high = jnp.where(inner == 15, pltpu.roll(got, 15 - c, 1), high)
                advect = advect + away * (tau[c] - jnp.where(row == 0, low, high))
                if i == 0:
                    mine = pltpu.roll(t_ref[c, 6], 16, 1)
                    got = pltpu.roll(left_ref[z], (128 - 16 * c) % 128, 1)
                    advect = advect + along * (tau[c] - jnp.where(lane < 16, got, mine))
                if i == 6:
                    mine = pltpu.roll(t_ref[c, 0], 112, 1)
                    got = pltpu.roll(right_ref[z], 112 - 16 * c, 1)
                    advect = advect + along * (tau[c] - jnp.where(lane >= 112, got, mine))
                fresh = tau[c] + DT_STEP * (forcing - advect)
                n_ref[c, i] = fresh
                new_ref[c, z, i] = fresh[0:7, :]
        first = line_apply(twice, [n_ref[0, i] for i in range(7)])
        first = [first[i] + across(n_ref, 3, i) for i in range(7)]
        planar = line_apply(twice, first)
        second = line_apply(twice, [n_ref[3, i] for i in range(7)])
        for i in range(7):
            f_ref[i] = second[i] + across(n_ref, 1, i)
        crossed = line_apply(twice, [n_ref[4, i] for i in range(7)])
        for i in range(7):
            p_ref[0, z, i] = planar[i] + across(f_ref, i)
            p_ref[1, z, i] = n_ref[2, i]
            p_ref[2, z, i] = crossed[i] + across(n_ref, 5, i)
        return carry

    lax.fori_loop(0, 4, plane, 0)

    def one_row(q, carry):
        base = (y * NZ + q) * 12
        coefs = [coef_ref[base + k] for k in range(12)]
        for i in range(7):
            rows_ref[q, i] = tree_sum(
                [coefs[4 * s + z] * p_ref[s, z, i] for s in range(3) for z in range(4)]
            )
        return carry

    lax.fori_loop(0, NZ, one_row, 0)


def stress_step(stress, grad, velocity, faces):
    dcol = np.zeros((7, 8, 128))
    dcol[:, :7, :] = 2.0 * DERIV.T[:, :, None]
    vmem = pl.BlockSpec(memory_space=pltpu.VMEM)
    return pl.pallas_call(
        stress_kernel,
        out_shape=[
            jax.ShapeDtypeStruct((6, 4, 7, 7, 128), jnp.float32),
            jax.ShapeDtypeStruct((NZ, 7, 8, 128), jnp.float32),
        ],
        in_specs=[pl.BlockSpec(memory_space=pltpu.SMEM)] + [vmem] * 8,
        out_specs=[vmem] * 2,
        scratch_shapes=[
            pltpu.VMEM((6, 7, 8, 128), jnp.float32),
            pltpu.VMEM((6, 7, 8, 128), jnp.float32),
            pltpu.VMEM((6, 7, 8, 128), jnp.float32),
            pltpu.VMEM((7, 8, 128), jnp.float32),
            pltpu.VMEM((3, 4, 7, 8, 128), jnp.float32),
            pltpu.VMEM((11, 7, 8, 128), jnp.float32),
        ],
        compiler_params=pltpu.CompilerParams(vmem_limit_bytes=24 * MIB),
    )(
        jnp.asarray(source_coefs()), stress, grad, velocity, *faces,
        jnp.asarray(dcol, jnp.float32),
    )


def metric_kernel(m_ref, q_ref):
    x = 2 * lax.axis_index("xh") + lax.axis_index("xl")

    def chunk(k, carry):
        from_xl, from_core, half = k // 4, k // 2 % 2, k % 2
        here = pl.ds(pl.multiple_of(k * 8, 8), 8)
        back = [(x - 2 * s - from_xl + 4) % 4 for s in range(2)]
        for tile in range(19):
            rows = slice(8 * tile, 8 * tile + 8)
            block = jnp.stack(
                [m_ref[(half * 4 + s // 2) * 2 + from_core, back[s % 2], rows, :] for s in range(8)]
            )
            block = jnp.swapaxes(block, 0, 1)
            for j in range(8):
                c, n = divmod(8 * tile + j, 49)
                if c < 3:
                    scale = WEIGHTS[n // 7] * WEIGHTS[n % 7] * (MASS_SCALE if c == 2 else 1.0)
                    q_ref[c, n, here, :] = float(scale) * block[j]
        return carry

    lax.fori_loop(0, 8, chunk, 0)


def metric_fields(gathered):
    vmem = pl.BlockSpec(memory_space=pltpu.VMEM)
    return pl.pallas_call(
        metric_kernel,
        out_shape=jax.ShapeDtypeStruct((3, 49, 64, 128), jnp.float32),
        in_specs=[vmem],
        out_specs=vmem,
        compiler_params=pltpu.CompilerParams(vmem_limit_bytes=24 * MIB),
    )(gathered)


def solve_kernel(
    count_ref, same_ref, other_ref, q_ref, out_ref, r_ref, d_ref, im_ref, mk_ref, x_ref, t_ref
):
    zh, zl = lax.axis_index("zh"), lax.axis_index("zl")
    xh, xl, core = lax.axis_index("xh"), lax.axis_index("xl"), lax.axis_index("core")
    e = xl * 2 + core
    row_id = 4 * lax.axis_index("y") + zh
    harmonic = jnp.where(row_id == 1, NZ // 2, row_id // 2).astype(jnp.float32)
    wavesq = harmonic * harmonic * (SPAN_UNIT * SPAN_UNIT)
    own = pl.ds(pl.multiple_of(e * 16, 16), 16)
    flipped = DERIV.T
    zero = jnp.zeros((8, 128), jnp.float32)

    def here(k):
        return pl.ds(pl.multiple_of(k * 8, 8), 8)

    flip = [zl, 1 - zl]

    def chunk_in(quarter, carry):
        from_xl, half = quarter // 2, quarter % 2
        for ref, from_core in ((same_ref, core), (other_ref, 1 - core)):
            at = here((from_xl * 2 + from_core) * 2 + half)
            for i in range(7):
                block = jnp.stack(
                    [
                        ref[2 * (s % 2) + from_xl, flip[s // 2 % 2], half * 2 + s // 4, i]
                        for s in range(8)
                    ]
                )
                block = jnp.swapaxes(block, 0, 1)
                for j in range(7):
                    n = i * 7 + j
                    mass = q_ref[2, n, at, :]
                    im_ref[n, at, :] = mass * block[j]
                    mk_ref[n, at, :] = wavesq * mass
                    d_ref[n, at, :] = zero
        return carry

    lax.fori_loop(0, 4, chunk_in, 0)
    for n in range(49):
        x_ref[n] = jnp.zeros((16, 128), jnp.float32)

    lane = lax.broadcasted_iota(jnp.int32, (64, 128), 1)
    spot = lax.broadcasted_iota(jnp.int32, (64, 128), 0)
    inner, c_pos = lane % 16, spot % 16
    wall = (
        (c_pos == 0) & (lane < 16),
        (c_pos == 15) & (lane >= 112),
        (spot < 16) & (inner == 0),
        (spot >= 48) & (inner == 15),
    )

    def join():
        for j in range(7):
            low, high = im_ref[j], im_ref[42 + j]
            moved = pltpu.roll(high, 16, 1)
            moved = jnp.where(lane < 16, pltpu.roll(moved, 1, 0), moved)
            back = pltpu.roll(low, 112, 1)
            back = jnp.where(lane >= 112, pltpu.roll(back, 63, 0), back)
            im_ref[j] = jnp.where(wall[0], 0.0, low + moved)
            im_ref[42 + j] = jnp.where(wall[1], 0.0, high + back)
        for i in range(7):
            low, high = im_ref[7 * i], im_ref[7 * i + 6]
            other = pltpu.roll(pltpu.roll(high, 113, 1), 16, 0)
            moved = jnp.where(inner == 0, other, pltpu.roll(high, 1, 1))
            other = pltpu.roll(pltpu.roll(low, 15, 1), 48, 0)
            back = jnp.where(inner == 15, other, pltpu.roll(low, 127, 1))
            im_ref[7 * i] = jnp.where(wall[2], 0.0, low + moved)
            im_ref[7 * i + 6] = jnp.where(wall[3], 0.0, high + back)

    def total(acc):
        return jnp.broadcast_to(jnp.sum(acc, axis=(0, 1), keepdims=True), (8, 128))

    def square(line, ends):
        inside = tree_sum([line[m] * line[m] for m in range(1, 6)])
        return ends * (inside + 0.5 * (line[0] * line[0] + line[6] * line[6]))

    def set_residual(k, acc):
        for i in range(7):
            line = []
            for j in range(7):
                value = im_ref[i * 7 + j, here(k), :]
                r_ref[i * 7 + j, here(k), :] = value
                line.append(value)
            acc = acc + square(line, 0.5 if i in (0, 6) else 1.0)
        return acc

    join()
    rho = total(lax.fori_loop(0, 8, set_residual, zero))

    def sweep(t, state):
        rho, beta = state

        def image(k, acc):
            at = here(k)
            for j in range(7):
                line = []
                for i in range(7):
                    n = i * 7 + j
                    value = r_ref[n, at, :] + beta * d_ref[n, at, :]
                    d_ref[n, at, :] = value
                    line.append(value)
                flux = line_apply(DERIV, line)
                flux = [flux[i] * q_ref[0, i * 7 + j, at, :] for i in range(7)]
                part = line_apply(flipped, flux)
                for i in range(7):
                    n = i * 7 + j
                    part[i] = part[i] + mk_ref[n, at, :] * line[i]
                    im_ref[n, at, :] = part[i]
                acc = acc + tree_sum([part[i] * line[i] for i in range(7)])
            for i in range(7):
                line = [d_ref[i * 7 + j, at, :] for j in range(7)]
                flux = line_apply(DERIV, line)
                flux = [flux[j] * q_ref[1, i * 7 + j, at, :] for j in range(7)]
                part = line_apply(flipped, flux)
                for j in range(7):
                    n = i * 7 + j
                    im_ref[n, at, :] = im_ref[n, at, :] + part[j]
                acc = acc + tree_sum([part[j] * line[j] for j in range(7)])
            return acc

        step = rho / total(lax.fori_loop(0, 8, image, zero))
        join()
        for n in range(49):
            x_ref[n] = x_ref[n] + step[0:1] * d_ref[n, own, :]

        def descend(k, acc):
            at = here(k)
            for i in range(7):
                line = []
                for j in range(7):
                    n = i * 7 + j
                    value = r_ref[n, at, :] - step * im_ref[n, at, :]
                    r_ref[n, at, :] = value
                    line.append(value)
                acc = acc + square(line, 0.5 if i in (0, 6) else 1.0)
            return acc

        fresh = total(lax.fori_loop(0, 8, descend, zero))
        return fresh, fresh / rho

    lax.fori_loop(0, count_ref[row_id], sweep, (rho, zero))

    for i in range(7):
        for half in range(2):
            rows = slice(8 * half, 8 * half + 8)
            block = jnp.stack([x_ref[i * 7 + j, rows, :] for j in range(7)] + [zero])
            block = jnp.swapaxes(block, 0, 1)
            for s in range(8):
                t_ref[8 * half + s, i] = block[s]
    for to in range(4):
        for i in range(7):
            value = t_ref[4 * to + 2 * zl + xh, i]
            for copy in range(8):
                out_ref[to * 8 + copy, i] = value


def solve(counts, same, other, metrics):
    vmem = pl.BlockSpec(memory_space=pltpu.VMEM)
    field = pltpu.VMEM((49, 64, 128), jnp.float32)
    return pl.pallas_call(
        solve_kernel,
        out_shape=jax.ShapeDtypeStruct((NZ, 7, 8, 128), jnp.float32),
        in_specs=[pl.BlockSpec(memory_space=pltpu.SMEM)] + [vmem] * 3,
        out_specs=vmem,
        scratch_shapes=[
            field, field, field, field,
            pltpu.VMEM((49, 16, 128), jnp.float32),
            pltpu.VMEM((16, 7, 8, 128), jnp.float32),
        ],
        compiler_params=pltpu.CompilerParams(vmem_limit_bytes=40 * MIB),
    )(counts, same, other, metrics)


def pressure_kernel(coef_ref, rows_ref, out_ref):
    y = lax.axis_index("y")
    for zl in range(4):
        coefs = [coef_ref[(y * 4 + zl) * NZ + q] for q in range(NZ)]
        for i in range(7):
            value = tree_sum([coefs[q] * rows_ref[q, i] for q in range(NZ)])
            out_ref[zl, i] = value[0:7, :]


def pressure_planes(rows):
    vmem = pl.BlockSpec(memory_space=pltpu.VMEM)
    return pl.pallas_call(
        pressure_kernel,
        out_shape=jax.ShapeDtypeStruct((4, 7, 7, 128), jnp.float32),
        in_specs=[pl.BlockSpec(memory_space=pltpu.SMEM), vmem],
        out_specs=vmem,
        compiler_params=pltpu.CompilerParams(vmem_limit_bytes=16 * MIB),
    )(jnp.asarray(plane_coefs()), rows)


SWAP = [(0, 1), (1, 0)]
TURNS = [[(at, (at + back) % 4) for at in range(4)] for back in range(1, 4)]


def after(value, other):
    return lax.optimization_barrier((value, other))[0]


def local(stress, velocity_grad, velocity, metric, iteration_counts):
    packed = jnp.pad(metric.reshape(147, 128), ((0, 5), (0, 0)))
    right, left, up, down = pack_faces(stress)
    ahead = [(c, c + 1) for c in range(15)]
    above = [(e, e + 1) for e in range(3)]
    faces = (
        lax.ppermute(right, FLOW, ahead),
        lax.ppermute(left, FLOW, [(b, a) for a, b in ahead]),
        lax.ppermute(up, CROSS, above),
        lax.ppermute(down, CROSS, [(b, a) for a, b in above]),
    )
    new_stress, parts = stress_step(stress, velocity_grad, velocity, faces)
    packed = after(packed, parts)
    ring = jnp.stack([packed] + [lax.ppermute(packed, RING_X, turn) for turn in TURNS])
    metrics = metric_fields(lax.all_gather(ring, ("zh", "zl", "core")))
    parts = lax.all_to_all(parts, ROWS, 0, 0, tiled=True)
    mine = jnp.sum(parts.reshape(4, 8, 7, 8, 128), axis=1)
    pair = jnp.stack([mine, lax.ppermute(mine, "zl", SWAP)])
    same = lax.all_gather(pair, RING_X)
    other = lax.ppermute(same, "core", SWAP)
    answer = solve(iteration_counts, same, other, metrics)
    answer = lax.all_to_all(answer, ROWS, 0, 0, tiled=True)
    return new_stress, pressure_planes(answer)


def solution(mesh):
    fine = Mesh(mesh.devices.reshape(SPLIT), PLANE + ("y",))
    field = P(None, "y", None, None, PLANE)
    return jax.shard_map(
        local,
        mesh=fine,
        in_specs=(field, field, field, P(None, None, None, PLANE), P()),
        out_specs=(field, P("y", None, None, PLANE)),
        check_vma=False,
    )
```

```python
import jax
import jax.numpy as jnp
import numpy as np
from jax import lax
from jax.experimental import pallas as pl
from jax.experimental.pallas import tpu as pltpu
from jax.sharding import Mesh
from jax.sharding import PartitionSpec as P

FLOW = ("zh", "zl", "xh")
CROSS = ("xl", "core")
PLANE = ("zh", "zl", "xh", "xl", "core")
RING_X = ("xh", "xl")
ROWS = ("xh", "xl", "y")
SPLIT = (4, 2, 2, 2, 2, 8)

EY = 16
NZ = 32
DT_STEP = 0.01
SPAN_UNIT = 0.5
MASS_SCALE = 0.25
MIB = 1 << 20


def node_tables():
    nodes = np.array(
        [-1.0, -0.830223896278567, -0.468848793470714, 0.0,
         0.468848793470714, 0.830223896278567, 1.0]
    )
    weights = np.array(
        [1.0 / 21.0, 0.276826047361566, 0.431745381209863, 0.487619047619048,
         0.431745381209863, 0.276826047361566, 1.0 / 21.0]
    )
    bary = np.array(
        [1.0 / np.prod([nodes[c] - nodes[o] for o in range(7) if o != c]) for c in range(7)]
    )
    deriv = np.zeros((7, 7))
    for row in range(7):
        for col in range(7):
            if row != col:
                deriv[row, col] = bary[col] / bary[row] / (nodes[row] - nodes[col])
        deriv[row, row] = -np.sum(deriv[row])
    return deriv, weights


DERIV, WEIGHTS = node_tables()
LIFT = 2.0 / WEIGHTS[0]


def span_tables():
    ids = np.arange(NZ)
    harmonic = np.where(ids == 1, NZ // 2, ids // 2)
    sine = (ids % 2 == 1) & (ids != 1)
    phase = 2.0 * np.pi / NZ * (harmonic[:, None] * ids[None, :] % NZ)
    basis = np.where(sine[:, None], np.sin(phase), np.cos(phase))
    basis = basis * np.where(ids < 2, 1.0 / np.sqrt(NZ), np.sqrt(2.0 / NZ))[:, None]
    wavenum = SPAN_UNIT * harmonic
    slope = np.where(ids < 2, 0.0, np.where(sine, -wavenum, wavenum))
    return basis, slope[:, None] * basis[ids ^ 1], wavenum


BASIS, SLOPE, WAVENUM = span_tables()
ROW_AT = np.array([4 * (q % 8) + q // 8 for q in range(NZ)])


def source_coefs():
    table = np.zeros((8, NZ, 3, 4))
    for y in range(8):
        cols = slice(4 * y, 4 * y + 4)
        table[y, :, 0] = BASIS[ROW_AT, cols]
        table[y, :, 1] = -(WAVENUM[ROW_AT] ** 2)[:, None] * BASIS[ROW_AT, cols]
        table[y, :, 2] = 2.0 * SLOPE[ROW_AT, cols]
    return table.astype(np.float32).reshape(-1)


def plane_coefs():
    table = np.stack([BASIS.T[4 * y : 4 * y + 4][:, ROW_AT] for y in range(8)])
    return table.astype(np.float32).reshape(-1)


def line_apply(mat, f):
    even = [f[m] + f[6 - m] for m in range(3)]
    odd = [f[m] - f[6 - m] for m in range(3)]
    out = [None] * 7
    for i in range(3):
        from_odd = float(0.5 * (mat[i, 0] - mat[i, 6])) * odd[0]
        from_even = float(mat[i, 3]) * f[3]
        for m in range(3):
            from_even = from_even + float(0.5 * (mat[i, m] + mat[i, 6 - m])) * even[m]
            if m:
                from_odd = from_odd + float(0.5 * (mat[i, m] - mat[i, 6 - m])) * odd[m]
        out[i] = from_odd + from_even
        out[6 - i] = from_odd - from_even
    out[3] = float(mat[3, 0]) * odd[0] + float(mat[3, 1]) * odd[1] + float(mat[3, 2]) * odd[2]
    return out


def tree_sum(terms):
    while len(terms) > 1:
        terms = [sum(terms[i : i + 2][1:], terms[i]) for i in range(0, len(terms), 2)]
    return terms[0]


def lanes():
    return lax.broadcasted_iota(jnp.int32, (8, 128), 1)


def pack_kernel(s_ref, right_ref, left_ref, up_ref, down_ref, t_ref):
    lane = lanes()
    block, inner = lane // 16, lane % 16

    def plane(z, carry):
        for c in range(6):
            for i in range(7):
                t_ref[c, i, 0:7, :] = s_ref[c, z, i]
        zero = jnp.zeros((8, 128), jnp.float32)
        right, left = zero, zero
        for c in range(6):
            right = jnp.where(block == c, pltpu.roll(t_ref[c, 6], (16 * (c + 1)) % 128, 1), right)
            left = jnp.where(block == c, pltpu.roll(t_ref[c, 0], 16 * c, 1), left)
        right_ref[z] = right
        left_ref[z] = left
        for i in range(7):
            up, down = zero, zero
            for c in range(6):
                up = jnp.where(inner == c, pltpu.roll(t_ref[c, i], (c - 15) % 128, 1), up)
                down = jnp.where(inner == c, pltpu.roll(t_ref[c, i], c, 1), down)
            up_ref[z, i : i + 1, :] = up[6:7, :]
            down_ref[z, i : i + 1, :] = down[0:1, :]
        up_ref[z, 7:8, :] = zero[0:1, :]
        down_ref[z, 7:8, :] = zero[0:1, :]
        return carry

    for c in range(6):
        for i in range(7):
            t_ref[c, i] = jnp.zeros((8, 128), jnp.float32)
    lax.fori_loop(0, 4, plane, 0)


def pack_faces(stress):
    return pl.pallas_call(
        pack_kernel,
        out_shape=[jax.ShapeDtypeStruct((4, 8, 128), jnp.float32)] * 4,
        in_specs=[pl.BlockSpec(memory_space=pltpu.VMEM)],
        out_specs=[pl.BlockSpec(memory_space=pltpu.VMEM)] * 4,
        scratch_shapes=[pltpu.VMEM((6, 7, 8, 128), jnp.float32)],
        compiler_params=pltpu.CompilerParams(vmem_limit_bytes=16 * MIB),
    )(stress)


def stress_kernel(
    coef_ref, s_ref, g_ref, v_ref, left_ref, right_ref, below_ref, above_ref,
    new_ref, rows_ref, t_ref, d_ref, n_ref, f_ref, p_ref, lb_ref, dcol_ref,
):
    lane = lanes()
    inner = lane % 16
    row = lax.broadcasted_iota(jnp.int32, (8, 128), 0)
    twice = 2.0 * DERIV
    y = lax.axis_index("y")

    def across(ref, *at):
        total = dcol_ref[0] * ref[(*at, pl.ds(0, 1), slice(None))]
        for m in range(1, 7):
            total = total + dcol_ref[m] * ref[(*at, pl.ds(m, 1), slice(None))]
        return total

    zero = jnp.zeros((8, 128), jnp.float32)
    for m in range(7):
        column = zero
        for j in range(7):
            column = jnp.where(row == j, float(twice[j, m]), column)
        dcol_ref[m] = column
    for i in range(7):
        for c in range(6):
            t_ref[c, i] = zero
        for c in range(11):
            lb_ref[c, i] = zero

    def plane(z, carry):
        for i in range(7):
            for c in range(6):
                t_ref[c, i, 0:7, :] = s_ref[c, z, i]
            for c in range(9):
                lb_ref[c, i, 0:7, :] = g_ref[c, z, i]
            for c in range(2):
                lb_ref[9 + c, i, 0:7, :] = v_ref[c, z, i]
        for c in range(6):
            slope = line_apply(twice, [t_ref[c, i] for i in range(7)])
            for i in range(7):
                d_ref[c, i] = slope[i]
        for i in range(7):
            u, v = lb_ref[9, i], lb_ref[10, i]
            away = jnp.where(row == 0, -v, v)
            away = jnp.where((row == 0) | (row == 6), jnp.minimum(away, 0.0), 0.0) * float(-LIFT)
            if i == 0:
                along = jnp.minimum(-u, 0.0) * float(-LIFT)
            if i == 6:
                along = jnp.minimum(u, 0.0) * float(-LIFT)
            grad = [lb_ref[c, i] for c in range(9)]
            tau = [t_ref[c, i] for c in range(6)]
            xx, yy, zz = tau[0] + 0.5, tau[1] + 0.5, tau[2] + 0.5
            full = ((xx, tau[3], tau[4]), (tau[3], yy, tau[5]), (tau[4], tau[5], zz))
            prod = [
                [tree_sum([grad[3 * a + k] * full[k][b] for k in range(3)]) for b in range(3)]
                for a in range(3)
            ]
            pairs = ((0, 0), (1, 1), (2, 2), (0, 1), (0, 2), (1, 2))
            for c, (a, b) in enumerate(pairs):
                forcing = prod[a][b] + prod[b][a] - tau[c]
                advect = u * d_ref[c, i] + v * across(t_ref, c, i)
                low = jnp.broadcast_to(t_ref[c, i, 6:7, :], (8, 128))
                low = pltpu.roll(low, 1, 1)
                got = jnp.broadcast_to(below_ref[z, i : i + 1, :], (8, 128))
                low = jnp.where(inner == 0, pltpu.roll(got, (128 - c) % 128, 1), low)
                high = jnp.broadcast_to(t_ref[c, i, 0:1, :], (8, 128))
                high = pltpu.roll(high, 127, 1)
                got = jnp.broadcast_to(above_ref[z, i : i + 1, :], (8, 128))
                high = jnp.where(inner == 15, pltpu.roll(got, 15 - c, 1), high)
                advect = advect + away * (tau[c] - jnp.where(row == 0, low, high))
                if i == 0:
                    mine = pltpu.roll(t_ref[c, 6], 16, 1)
                    got = pltpu.roll(left_ref[z], (128 - 16 * c) % 128, 1)
                    advect = advect + along * (tau[c] - jnp.where(lane < 16, got, mine))
                if i == 6:
                    mine = pltpu.roll(t_ref[c, 0], 112, 1)
                    got = pltpu.roll(right_ref[z], 112 - 16 * c, 1)
                    advect = advect + along * (tau[c] - jnp.where(lane >= 112, got, mine))
                fresh = tau[c] + DT_STEP * (forcing - advect)
                n_ref[c, i] = fresh
                new_ref[c, z, i] = fresh[0:7, :]
        first = line_apply(twice, [n_ref[0, i] for i in range(7)])
        first = [first[i] + across(n_ref, 3, i) for i in range(7)]
        planar = line_apply(twice, first)
        second = line_apply(twice, [n_ref[3, i] for i in range(7)])
        for i in range(7):
            f_ref[i] = second[i] + across(n_ref, 1, i)
        crossed = line_apply(twice, [n_ref[4, i] for i in range(7)])
        for i in range(7):
            p_ref[0, z, i] = planar[i] + across(f_ref, i)
            p_ref[1, z, i] = n_ref[2, i]
            p_ref[2, z, i] = crossed[i] + across(n_ref, 5, i)
        return carry

    lax.fori_loop(0, 4, plane, 0)

    def one_row(q, carry):
        base = (y * NZ + q) * 12
        coefs = [coef_ref[base + k] for k in range(12)]
        for i in range(7):
            rows_ref[q, i] = tree_sum(
                [coefs[4 * s + z] * p_ref[s, z, i] for s in range(3) for z in range(4)]
            )
        return carry

    lax.fori_loop(0, NZ, one_row, 0)


def stress_step(stress, grad, velocity, faces):
    vmem = pl.BlockSpec(memory_space=pltpu.VMEM)
    return pl.pallas_call(
        stress_kernel,
        out_shape=[
            jax.ShapeDtypeStruct((6, 4, 7, 7, 128), jnp.float32),
            jax.ShapeDtypeStruct((NZ, 7, 8, 128), jnp.float32),
        ],
        in_specs=[pl.BlockSpec(memory_space=pltpu.SMEM)] + [vmem] * 7,
        out_specs=[vmem] * 2,
        scratch_shapes=[
            pltpu.VMEM((6, 7, 8, 128), jnp.float32),
            pltpu.VMEM((6, 7, 8, 128), jnp.float32),
            pltpu.VMEM((6, 7, 8, 128), jnp.float32),
            pltpu.VMEM((7, 8, 128), jnp.float32),
            pltpu.VMEM((3, 4, 7, 8, 128), jnp.float32),
            pltpu.VMEM((11, 7, 8, 128), jnp.float32),
            pltpu.VMEM((7, 8, 128), jnp.float32),
        ],
        compiler_params=pltpu.CompilerParams(vmem_limit_bytes=24 * MIB),
    )(jnp.asarray(source_coefs()), stress, grad, velocity, *faces)


def metric_kernel(m_ref, q_ref):
    x = 2 * lax.axis_index("xh") + lax.axis_index("xl")

    def chunk(k, carry):
        from_xl, from_core, half = k // 4, k // 2 % 2, k % 2
        here = pl.ds(pl.multiple_of(k * 8, 8), 8)
        back = [(x - 2 * s - from_xl + 4) % 4 for s in range(2)]
        for tile in range(19):
            rows = slice(8 * tile, 8 * tile + 8)
            block = jnp.stack(
                [m_ref[(half * 4 + s // 2) * 2 + from_core, back[s % 2], rows, :] for s in range(8)]
            )
            block = jnp.swapaxes(block, 0, 1)
            for j in range(8):
                c, n = divmod(8 * tile + j, 49)
                if c < 3:
                    scale = WEIGHTS[n // 7] * WEIGHTS[n % 7] * (MASS_SCALE if c == 2 else 1.0)
                    q_ref[c, n, here, :] = float(scale) * block[j]
        return carry

    lax.fori_loop(0, 8, chunk, 0)


def metric_fields(gathered):
    vmem = pl.BlockSpec(memory_space=pltpu.VMEM)
    return pl.pallas_call(
        metric_kernel,
        out_shape=jax.ShapeDtypeStruct((3, 49, 64, 128), jnp.float32),
        in_specs=[vmem],
        out_specs=vmem,
        compiler_params=pltpu.CompilerParams(vmem_limit_bytes=24 * MIB),
    )(gathered)


def solve_kernel(
    count_ref, same_ref, other_ref, q_ref, out_ref, r_ref, d_ref, im_ref, mk_ref, x_ref, t_ref
):
    zl, core = lax.axis_index("zl"), lax.axis_index("core")
    z = 2 * lax.axis_index("zh") + zl
    flip = [zl, 1 - zl]
    row_id = 4 * lax.axis_index("y") + 2 * lax.axis_index("xh") + lax.axis_index("xl")
    harmonic = jnp.where(row_id == 1, NZ // 2, row_id // 2).astype(jnp.float32)
    wavesq = harmonic * harmonic * (SPAN_UNIT * SPAN_UNIT)
    own = [pl.ds(pl.multiple_of(((2 * to + core) * 2 + z // 4) * 8, 8), 8) for to in range(2)]
    flipped = DERIV.T
    zero = jnp.zeros((8, 128), jnp.float32)

    def here(k):
        return pl.ds(pl.multiple_of(k * 8, 8), 8)

    def chunk_in(quarter, carry):
        from_xl, half = quarter // 2, quarter % 2
        for ref, from_core in ((same_ref, core), (other_ref, 1 - core)):
            at = here((from_xl * 2 + from_core) * 2 + half)
            for i in range(7):
                block = jnp.stack(
                    [
                        ref[half * 2 + s // 4, flip[s // 2 % 2], 2 * (s % 2) + from_xl, i]
                        for s in range(8)
                    ]
                )
                block = jnp.swapaxes(block, 0, 1)
                for j in range(7):
                    n = i * 7 + j
                    mass = q_ref[2, n, at, :]
                    im_ref[n, at, :] = mass * block[j]
                    mk_ref[n, at, :] = wavesq * mass
                    d_ref[n, at, :] = zero
        return carry

    lax.fori_loop(0, 4, chunk_in, 0)
    for n in range(49):
        x_ref[0, n] = zero
        x_ref[1, n] = zero

    lane = lax.broadcasted_iota(jnp.int32, (64, 128), 1)
    spot = lax.broadcasted_iota(jnp.int32, (64, 128), 0)
    inner, c_pos = lane % 16, spot % 16
    wall = (
        (c_pos == 0) & (lane < 16),
        (c_pos == 15) & (lane >= 112),
        (spot < 16) & (inner == 0),
        (spot >= 48) & (inner == 15),
    )

    def join():
        for j in range(7):
            low, high = im_ref[j], im_ref[42 + j]
            moved = pltpu.roll(high, 16, 1)
            moved = jnp.where(lane < 16, pltpu.roll(moved, 1, 0), moved)
            back = pltpu.roll(low, 112, 1)
            back = jnp.where(lane >= 112, pltpu.roll(back, 63, 0), back)
            im_ref[j] = jnp.where(wall[0], 0.0, low + moved)
            im_ref[42 + j] = jnp.where(wall[1], 0.0, high + back)
        for i in range(7):
            low, high = im_ref[7 * i], im_ref[7 * i + 6]
            other = pltpu.roll(pltpu.roll(high, 113, 1), 16, 0)
            moved = jnp.where(inner == 0, other, pltpu.roll(high, 1, 1))
            other = pltpu.roll(pltpu.roll(low, 15, 1), 48, 0)
            back = jnp.where(inner == 15, other, pltpu.roll(low, 127, 1))
            im_ref[7 * i] = jnp.where(wall[2], 0.0, low + moved)
            im_ref[7 * i + 6] = jnp.where(wall[3], 0.0, high + back)

    def total(acc):
        return jnp.broadcast_to(jnp.sum(acc, axis=(0, 1), keepdims=True), (8, 128))

    def square(line, ends):
        inside = tree_sum([line[m] * line[m] for m in range(1, 6)])
        return ends * (inside + 0.5 * (line[0] * line[0] + line[6] * line[6]))

    def set_residual(k, acc):
        for i in range(7):
            line = []
            for j in range(7):
                value = im_ref[i * 7 + j, here(k), :]
                r_ref[i * 7 + j, here(k), :] = value
                line.append(value)
            acc = acc + square(line, 0.5 if i in (0, 6) else 1.0)
        return acc

    join()
    rho = total(lax.fori_loop(0, 8, set_residual, zero))

    def sweep(t, state):
        rho, beta = state

        def image(k, acc):
            at = here(k)
            for j in range(7):
                line = []
                for i in range(7):
                    n = i * 7 + j
                    value = r_ref[n, at, :] + beta * d_ref[n, at, :]
                    d_ref[n, at, :] = value
                    line.append(value)
                flux = line_apply(DERIV, line)
                flux = [flux[i] * q_ref[0, i * 7 + j, at, :] for i in range(7)]
                part = line_apply(flipped, flux)
                for i in range(7):
                    n = i * 7 + j
                    part[i] = part[i] + mk_ref[n, at, :] * line[i]
                    im_ref[n, at, :] = part[i]
                acc = acc + tree_sum([part[i] * line[i] for i in range(7)])
            for i in range(7):
                line = [d_ref[i * 7 + j, at, :] for j in range(7)]
                flux = line_apply(DERIV, line)
                flux = [flux[j] * q_ref[1, i * 7 + j, at, :] for j in range(7)]
                part = line_apply(flipped, flux)
                for j in range(7):
                    n = i * 7 + j
                    im_ref[n, at, :] = im_ref[n, at, :] + part[j]
                acc = acc + tree_sum([part[j] * line[j] for j in range(7)])
            return acc

        step = rho / total(lax.fori_loop(0, 8, image, zero))
        for n in range(49):
            for to in range(2):
                x_ref[to, n] = x_ref[to, n] + step * d_ref[n, own[to], :]

        def descend(k, acc):
            at = here(k)
            for i in range(7):
                line = []
                for j in range(7):
                    n = i * 7 + j
                    value = r_ref[n, at, :] - step * im_ref[n, at, :]
                    r_ref[n, at, :] = value
                    line.append(value)
                acc = acc + square(line, 0.5 if i in (0, 6) else 1.0)
            return acc

        def proceed():
            join()
            fresh = total(lax.fori_loop(0, 8, descend, zero))
            return fresh, fresh / rho

        return lax.cond(t + 1 < count, proceed, lambda: (rho, beta))

    count = count_ref[row_id]
    lax.fori_loop(0, count, sweep, (rho, zero))

    for i in range(7):
        for to in range(2):
            block = jnp.stack([x_ref[to, i * 7 + j] for j in range(7)] + [zero])
            block = jnp.swapaxes(block, 0, 1)
            for s in range(8):
                t_ref[to, s, i] = block[s]
    for to in range(4):
        for i in range(7):
            value = t_ref[to % 2, z % 4 * 2 + to // 2, i]
            for copy in range(8):
                out_ref[to * 8 + copy, i] = value


def solve(counts, same, other, metrics):
    vmem = pl.BlockSpec(memory_space=pltpu.VMEM)
    field = pltpu.VMEM((49, 64, 128), jnp.float32)
    return pl.pallas_call(
        solve_kernel,
        out_shape=jax.ShapeDtypeStruct((NZ, 7, 8, 128), jnp.float32),
        in_specs=[pl.BlockSpec(memory_space=pltpu.SMEM)] + [vmem] * 3,
        out_specs=vmem,
        scratch_shapes=[
            field, field, field, field,
            pltpu.VMEM((2, 49, 8, 128), jnp.float32),
            pltpu.VMEM((2, 8, 7, 8, 128), jnp.float32),
        ],
        compiler_params=pltpu.CompilerParams(vmem_limit_bytes=40 * MIB),
    )(counts, same, other, metrics)


def pressure_kernel(coef_ref, rows_ref, out_ref):
    y = lax.axis_index("y")
    for zl in range(4):
        coefs = [coef_ref[(y * 4 + zl) * NZ + q] for q in range(NZ)]
        for i in range(7):
            value = tree_sum([coefs[q] * rows_ref[q, i] for q in range(NZ)])
            out_ref[zl, i] = value[0:7, :]


def pressure_planes(rows):
    vmem = pl.BlockSpec(memory_space=pltpu.VMEM)
    return pl.pallas_call(
        pressure_kernel,
        out_shape=jax.ShapeDtypeStruct((4, 7, 7, 128), jnp.float32),
        in_specs=[pl.BlockSpec(memory_space=pltpu.SMEM), vmem],
        out_specs=vmem,
        compiler_params=pltpu.CompilerParams(vmem_limit_bytes=16 * MIB),
    )(jnp.asarray(plane_coefs()), rows)


SWAP = [(0, 1), (1, 0)]
TURNS = [[(at, (at + back) % 4) for at in range(4)] for back in range(1, 4)]


def after(value, other):
    return lax.optimization_barrier((value, other))[0]


def local(stress, velocity_grad, velocity, metric, iteration_counts):
    packed = jnp.pad(metric.reshape(147, 128), ((0, 5), (0, 0)))
    turned = [lax.ppermute(packed, RING_X, turn) for turn in TURNS]
    right, left, up, down = pack_faces(stress)
    ahead = [(c, c + 1) for c in range(15)]
    above = [(e, e + 1) for e in range(3)]
    faces = (
        lax.ppermute(right, FLOW, ahead),
        lax.ppermute(left, FLOW, [(b, a) for a, b in ahead]),
        lax.ppermute(up, CROSS, above),
        lax.ppermute(down, CROSS, [(b, a) for a, b in above]),
    )
    ring = jnp.stack([after(packed, right)] + turned)
    faces = after(faces, ring)
    metrics = metric_fields(lax.all_gather(ring, ("zh", "zl", "core")))
    new_stress, parts = stress_step(stress, velocity_grad, velocity, faces)
    parts = lax.all_to_all(parts, ROWS, 0, 0, tiled=True)
    mine = jnp.sum(parts.reshape(4, 8, 7, 8, 128), axis=1)
    pair = jnp.stack([mine, lax.ppermute(mine, "zl", SWAP)])
    same = lax.all_gather(pair, "zh")
    other = lax.ppermute(same, "core", SWAP)
    answer = solve(iteration_counts, same, other, metrics)
    answer = lax.all_to_all(answer, ROWS, 0, 0, tiled=True)
    return new_stress, pressure_planes(answer)


def solution(mesh):
    fine = Mesh(mesh.devices.reshape(SPLIT), PLANE + ("y",))
    field = P(None, "y", None, None, PLANE)
    return jax.shard_map(
        local,
        mesh=fine,
        in_specs=(field, field, field, P(None, None, None, PLANE), P()),
        out_specs=(field, P("y", None, None, PLANE)),
        check_vma=False,
    )
```

```python
import jax
import jax.numpy as jnp
import numpy as np
from jax import lax
from jax.experimental import pallas as pl
from jax.experimental.pallas import tpu as pltpu
from jax.sharding import Mesh
from jax.sharding import PartitionSpec as P

FLOW = ("zh", "zl", "xh")
CROSS = ("xl", "core")
PLANE = ("zh", "zl", "xh", "xl", "core")
RING_X = ("xh", "xl")
ROWS = ("xh", "xl", "y")
SPLIT = (4, 2, 2, 2, 2, 8)

EY = 16
NZ = 32
DT_STEP = 0.01
SPAN_UNIT = 0.5
MASS_SCALE = 0.25
MIB = 1 << 20


def node_tables():
    nodes = np.array(
        [-1.0, -0.830223896278567, -0.468848793470714, 0.0,
         0.468848793470714, 0.830223896278567, 1.0]
    )
    weights = np.array(
        [1.0 / 21.0, 0.276826047361566, 0.431745381209863, 0.487619047619048,
         0.431745381209863, 0.276826047361566, 1.0 / 21.0]
    )
    bary = np.array(
        [1.0 / np.prod([nodes[c] - nodes[o] for o in range(7) if o != c]) for c in range(7)]
    )
    deriv = np.zeros((7, 7))
    for row in range(7):
        for col in range(7):
            if row != col:
                deriv[row, col] = bary[col] / bary[row] / (nodes[row] - nodes[col])
        deriv[row, row] = -np.sum(deriv[row])
    return deriv, weights


DERIV, WEIGHTS = node_tables()
LIFT = 2.0 / WEIGHTS[0]


def span_tables():
    ids = np.arange(NZ)
    harmonic = np.where(ids == 1, NZ // 2, ids // 2)
    sine = (ids % 2 == 1) & (ids != 1)
    phase = 2.0 * np.pi / NZ * (harmonic[:, None] * ids[None, :] % NZ)
    basis = np.where(sine[:, None], np.sin(phase), np.cos(phase))
    basis = basis * np.where(ids < 2, 1.0 / np.sqrt(NZ), np.sqrt(2.0 / NZ))[:, None]
    wavenum = SPAN_UNIT * harmonic
    slope = np.where(ids < 2, 0.0, np.where(sine, -wavenum, wavenum))
    return basis, slope[:, None] * basis[ids ^ 1], wavenum


BASIS, SLOPE, WAVENUM = span_tables()
ROW_AT = np.array([4 * (q % 8) + q // 8 for q in range(NZ)])


def source_coefs():
    table = np.zeros((8, NZ, 3, 4))
    for y in range(8):
        cols = slice(4 * y, 4 * y + 4)
        table[y, :, 0] = BASIS[ROW_AT, cols]
        table[y, :, 1] = -(WAVENUM[ROW_AT] ** 2)[:, None] * BASIS[ROW_AT, cols]
        table[y, :, 2] = 2.0 * SLOPE[ROW_AT, cols]
    return table.astype(np.float32).reshape(-1)


def plane_coefs():
    table = np.stack([BASIS.T[4 * y : 4 * y + 4][:, ROW_AT] for y in range(8)])
    return table.astype(np.float32).reshape(-1)


def line_apply(mat, f):
    even = [f[m] + f[6 - m] for m in range(3)]
    odd = [f[m] - f[6 - m] for m in range(3)]
    out = [None] * 7
    for i in range(3):
        from_odd = float(0.5 * (mat[i, 0] - mat[i, 6])) * odd[0]
        from_even = float(mat[i, 3]) * f[3]
        for m in range(3):
            from_even = from_even + float(0.5 * (mat[i, m] + mat[i, 6 - m])) * even[m]
            if m:
                from_odd = from_odd + float(0.5 * (mat[i, m] - mat[i, 6 - m])) * odd[m]
        out[i] = from_odd + from_even
        out[6 - i] = from_odd - from_even
    out[3] = float(mat[3, 0]) * odd[0] + float(mat[3, 1]) * odd[1] + float(mat[3, 2]) * odd[2]
    return out


def tree_sum(terms):
    while len(terms) > 1:
        terms = [sum(terms[i : i + 2][1:], terms[i]) for i in range(0, len(terms), 2)]
    return terms[0]


def lanes():
    return lax.broadcasted_iota(jnp.int32, (8, 128), 1)


def pack_kernel(s_ref, right_ref, left_ref, up_ref, down_ref, t_ref):
    lane = lanes()
    block, inner = lane // 16, lane % 16

    def plane(z, carry):
        for c in range(6):
            for i in range(7):
                t_ref[c, i, 0:7, :] = s_ref[c, z, i]
        zero = jnp.zeros((8, 128), jnp.float32)
        right, left = zero, zero
        for c in range(6):
            right = jnp.where(block == c, pltpu.roll(t_ref[c, 6], (16 * (c + 1)) % 128, 1), right)
            left = jnp.where(block == c, pltpu.roll(t_ref[c, 0], 16 * c, 1), left)
        right_ref[z] = right
        left_ref[z] = left
        for i in range(7):
            up, down = zero, zero
            for c in range(6):
                up = jnp.where(inner == c, pltpu.roll(t_ref[c, i], (c - 15) % 128, 1), up)
                down = jnp.where(inner == c, pltpu.roll(t_ref[c, i], c, 1), down)
            up_ref[z, i : i + 1, :] = up[6:7, :]
            down_ref[z, i : i + 1, :] = down[0:1, :]
        up_ref[z, 7:8, :] = zero[0:1, :]
        down_ref[z, 7:8, :] = zero[0:1, :]
        return carry

    for c in range(6):
        for i in range(7):
            t_ref[c, i] = jnp.zeros((8, 128), jnp.float32)
    lax.fori_loop(0, 4, plane, 0)


def pack_faces(stress):
    return pl.pallas_call(
        pack_kernel,
        out_shape=[jax.ShapeDtypeStruct((4, 8, 128), jnp.float32)] * 4,
        in_specs=[pl.BlockSpec(memory_space=pltpu.VMEM)],
        out_specs=[pl.BlockSpec(memory_space=pltpu.VMEM)] * 4,
        scratch_shapes=[pltpu.VMEM((6, 7, 8, 128), jnp.float32)],
        compiler_params=pltpu.CompilerParams(vmem_limit_bytes=16 * MIB),
    )(stress)


def stress_kernel(
    coef_ref, s_ref, g_ref, v_ref, left_ref, right_ref, below_ref, above_ref,
    new_ref, rows_ref, t_ref, d_ref, n_ref, f_ref, p_ref, lb_ref, dcol_ref,
):
    lane = lanes()
    inner = lane % 16
    row = lax.broadcasted_iota(jnp.int32, (8, 128), 0)
    twice = 2.0 * DERIV
    y = lax.axis_index("y")

    def across(ref, *at):
        total = dcol_ref[0] * ref[(*at, pl.ds(0, 1), slice(None))]
        for m in range(1, 7):
            total = total + dcol_ref[m] * ref[(*at, pl.ds(m, 1), slice(None))]
        return total

    zero = jnp.zeros((8, 128), jnp.float32)
    for m in range(7):
        column = zero
        for j in range(7):
            column = jnp.where(row == j, float(twice[j, m]), column)
        dcol_ref[m] = column
    for i in range(7):
        for c in range(6):
            t_ref[c, i] = zero
        for c in range(11):
            lb_ref[c, i] = zero

    def plane(z, carry):
        for i in range(7):
            for c in range(6):
                t_ref[c, i, 0:7, :] = s_ref[c, z, i]
            for c in range(9):
                lb_ref[c, i, 0:7, :] = g_ref[c, z, i]
            for c in range(2):
                lb_ref[9 + c, i, 0:7, :] = v_ref[c, z, i]
        for c in range(6):
            slope = line_apply(twice, [t_ref[c, i] for i in range(7)])
            for i in range(7):
                d_ref[c, i] = slope[i]
        for i in range(7):
            u, v = lb_ref[9, i], lb_ref[10, i]
            away = jnp.where(row == 0, -v, v)
            away = jnp.where((row == 0) | (row == 6), jnp.minimum(away, 0.0), 0.0) * float(-LIFT)
            if i == 0:
                along = jnp.minimum(-u, 0.0) * float(-LIFT)
            if i == 6:
                along = jnp.minimum(u, 0.0) * float(-LIFT)
            grad = [lb_ref[c, i] for c in range(9)]
            tau = [t_ref[c, i] for c in range(6)]
            xx, yy, zz = tau[0] + 0.5, tau[1] + 0.5, tau[2] + 0.5
            full = ((xx, tau[3], tau[4]), (tau[3], yy, tau[5]), (tau[4], tau[5], zz))
            prod = [
                [tree_sum([grad[3 * a + k] * full[k][b] for k in range(3)]) for b in range(3)]
                for a in range(3)
            ]
            pairs = ((0, 0), (1, 1), (2, 2), (0, 1), (0, 2), (1, 2))
            for c, (a, b) in enumerate(pairs):
                forcing = prod[a][b] + prod[b][a] - tau[c]
                advect = u * d_ref[c, i] + v * across(t_ref, c, i)
                low = jnp.broadcast_to(t_ref[c, i, 6:7, :], (8, 128))
                low = pltpu.roll(low, 1, 1)
                got = jnp.broadcast_to(below_ref[z, i : i + 1, :], (8, 128))
                low = jnp.where(inner == 0, pltpu.roll(got, (128 - c) % 128, 1), low)
                high = jnp.broadcast_to(t_ref[c, i, 0:1, :], (8, 128))
                high = pltpu.roll(high, 127, 1)
                got = jnp.broadcast_to(above_ref[z, i : i + 1, :], (8, 128))
                high = jnp.where(inner == 15, pltpu.roll(got, 15 - c, 1), high)
                advect = advect + away * (tau[c] - jnp.where(row == 0, low, high))
                if i == 0:
                    mine = pltpu.roll(t_ref[c, 6], 16, 1)
                    got = pltpu.roll(left_ref[z], (128 - 16 * c) % 128, 1)
                    advect = advect + along * (tau[c] - jnp.where(lane < 16, got, mine))
                if i == 6:
                    mine = pltpu.roll(t_ref[c, 0], 112, 1)
                    got = pltpu.roll(right_ref[z], 112 - 16 * c, 1)
                    advect = advect + along * (tau[c] - jnp.where(lane >= 112, got, mine))
                fresh = tau[c] + DT_STEP * (forcing - advect)
                n_ref[c, i] = fresh
                new_ref[c, z, i] = fresh[0:7, :]
        first = line_apply(twice, [n_ref[0, i] for i in range(7)])
        first = [first[i] + across(n_ref, 3, i) for i in range(7)]
        planar = line_apply(twice, first)
        second = line_apply(twice, [n_ref[3, i] for i in range(7)])
        for i in range(7):
            f_ref[i] = second[i] + across(n_ref, 1, i)
        crossed = line_apply(twice, [n_ref[4, i] for i in range(7)])
        for i in range(7):
            p_ref[0, z, i] = planar[i] + across(f_ref, i)
            p_ref[1, z, i] = n_ref[2, i]
            p_ref[2, z, i] = crossed[i] + across(n_ref, 5, i)
        return carry

    lax.fori_loop(0, 4, plane, 0)

    def one_row(q, carry):
        base = (y * NZ + q) * 12
        coefs = [coef_ref[base + k] for k in range(12)]
        for i in range(7):
            rows_ref[q, i] = tree_sum(
                [coefs[4 * s + z] * p_ref[s, z, i] for s in range(3) for z in range(4)]
            )
        return carry

    lax.fori_loop(0, NZ, one_row, 0)


def stress_step(stress, grad, velocity, faces):
    vmem = pl.BlockSpec(memory_space=pltpu.VMEM)
    return pl.pallas_call(
        stress_kernel,
        out_shape=[
            jax.ShapeDtypeStruct((6, 4, 7, 7, 128), jnp.float32),
            jax.ShapeDtypeStruct((NZ, 7, 8, 128), jnp.float32),
        ],
        in_specs=[pl.BlockSpec(memory_space=pltpu.SMEM)] + [vmem] * 7,
        out_specs=[vmem] * 2,
        scratch_shapes=[
            pltpu.VMEM((6, 7, 8, 128), jnp.float32),
            pltpu.VMEM((6, 7, 8, 128), jnp.float32),
            pltpu.VMEM((6, 7, 8, 128), jnp.float32),
            pltpu.VMEM((7, 8, 128), jnp.float32),
            pltpu.VMEM((3, 4, 7, 8, 128), jnp.float32),
            pltpu.VMEM((11, 7, 8, 128), jnp.float32),
            pltpu.VMEM((7, 8, 128), jnp.float32),
        ],
        compiler_params=pltpu.CompilerParams(vmem_limit_bytes=24 * MIB),
    )(jnp.asarray(source_coefs()), stress, grad, velocity, *faces)


def metric_kernel(m_ref, q_ref):
    x = 2 * lax.axis_index("xh") + lax.axis_index("xl")

    def chunk(k, carry):
        from_xl, from_core, half = k // 4, k // 2 % 2, k % 2
        here = pl.ds(pl.multiple_of(k * 8, 8), 8)
        back = [(x - 2 * s - from_xl + 4) % 4 for s in range(2)]
        for tile in range(19):
            rows = slice(8 * tile, 8 * tile + 8)
            block = jnp.stack(
                [m_ref[(half * 4 + s // 2) * 2 + from_core, back[s % 2], rows, :] for s in range(8)]
            )
            block = jnp.swapaxes(block, 0, 1)
            for j in range(8):
                c, n = divmod(8 * tile + j, 49)
                if c < 3:
                    scale = WEIGHTS[n // 7] * WEIGHTS[n % 7] * (MASS_SCALE if c == 2 else 1.0)
                    q_ref[c, n, here, :] = float(scale) * block[j]
        return carry

    lax.fori_loop(0, 8, chunk, 0)


def metric_fields(gathered):
    vmem = pl.BlockSpec(memory_space=pltpu.VMEM)
    return pl.pallas_call(
        metric_kernel,
        out_shape=jax.ShapeDtypeStruct((3, 49, 64, 128), jnp.float32),
        in_specs=[vmem],
        out_specs=vmem,
        compiler_params=pltpu.CompilerParams(vmem_limit_bytes=24 * MIB),
    )(gathered)


def by_chunks(body, start, together):
    def several(k, carry):
        for step in range(together):
            carry = body(k * together + step, carry)
        return carry

    return lax.fori_loop(0, 8 // together, several, start)


def solve_kernel(
    count_ref, same_ref, other_ref, q_ref, out_ref, r_ref, d_ref, im_ref, mk_ref, x_ref, t_ref
):
    zl, core = lax.axis_index("zl"), lax.axis_index("core")
    z = 2 * lax.axis_index("zh") + zl
    flip = [zl, 1 - zl]
    row_id = 4 * lax.axis_index("y") + 2 * lax.axis_index("xh") + lax.axis_index("xl")
    harmonic = jnp.where(row_id == 1, NZ // 2, row_id // 2).astype(jnp.float32)
    wavesq = harmonic * harmonic * (SPAN_UNIT * SPAN_UNIT)
    own = [pl.ds(pl.multiple_of(((2 * to + core) * 2 + z // 4) * 8, 8), 8) for to in range(2)]
    flipped = DERIV.T
    zero = jnp.zeros((8, 128), jnp.float32)

    def here(k):
        return pl.ds(pl.multiple_of(k * 8, 8), 8)

    def chunk_in(quarter, carry):
        from_xl, half = quarter // 2, quarter % 2
        for ref, from_core in ((same_ref, core), (other_ref, 1 - core)):
            at = here((from_xl * 2 + from_core) * 2 + half)
            for i in range(7):
                block = jnp.stack(
                    [
                        ref[half * 2 + s // 4, flip[s // 2 % 2], 2 * (s % 2) + from_xl, i]
                        for s in range(8)
                    ]
                )
                block = jnp.swapaxes(block, 0, 1)
                for j in range(7):
                    n = i * 7 + j
                    mass = q_ref[2, n, at, :]
                    im_ref[n, at, :] = mass * block[j]
                    mk_ref[n, at, :] = wavesq * mass
                    d_ref[n, at, :] = zero
        return carry

    lax.fori_loop(0, 4, chunk_in, 0)
    for n in range(49):
        x_ref[0, n] = zero
        x_ref[1, n] = zero

    lane = lax.broadcasted_iota(jnp.int32, (64, 128), 1)
    spot = lax.broadcasted_iota(jnp.int32, (64, 128), 0)
    inner, c_pos = lane % 16, spot % 16
    wall = (
        (c_pos == 0) & (lane < 16),
        (c_pos == 15) & (lane >= 112),
        (spot < 16) & (inner == 0),
        (spot >= 48) & (inner == 15),
    )

    def join():
        for j in range(7):
            low, high = im_ref[j], im_ref[42 + j]
            moved = pltpu.roll(high, 16, 1)
            moved = jnp.where(lane < 16, pltpu.roll(moved, 1, 0), moved)
            back = pltpu.roll(low, 112, 1)
            back = jnp.where(lane >= 112, pltpu.roll(back, 63, 0), back)
            im_ref[j] = jnp.where(wall[0], 0.0, low + moved)
            im_ref[42 + j] = jnp.where(wall[1], 0.0, high + back)
        for i in range(7):
            low, high = im_ref[7 * i], im_ref[7 * i + 6]
            other = pltpu.roll(pltpu.roll(high, 113, 1), 16, 0)
            moved = jnp.where(inner == 0, other, pltpu.roll(high, 1, 1))
            other = pltpu.roll(pltpu.roll(low, 15, 1), 48, 0)
            back = jnp.where(inner == 15, other, pltpu.roll(low, 127, 1))
            im_ref[7 * i] = jnp.where(wall[2], 0.0, low + moved)
            im_ref[7 * i + 6] = jnp.where(wall[3], 0.0, high + back)

    def total(acc):
        return jnp.broadcast_to(jnp.sum(acc, axis=(0, 1), keepdims=True), (8, 128))

    def square(line, ends):
        inside = tree_sum([line[m] * line[m] for m in range(1, 6)])
        return ends * (inside + 0.5 * (line[0] * line[0] + line[6] * line[6]))

    def set_residual(k, acc):
        for i in range(7):
            line = []
            for j in range(7):
                value = im_ref[i * 7 + j, here(k), :]
                r_ref[i * 7 + j, here(k), :] = value
                line.append(value)
            acc = acc + square(line, 0.5 if i in (0, 6) else 1.0)
        return acc

    join()
    rho = total(by_chunks(set_residual, zero, 8))

    def sweep(t, state):
        rho, beta = state

        def image(k, acc):
            at = here(k)
            for j in range(7):
                line = []
                for i in range(7):
                    n = i * 7 + j
                    value = r_ref[n, at, :] + beta * d_ref[n, at, :]
                    d_ref[n, at, :] = value
                    line.append(value)
                flux = line_apply(DERIV, line)
                flux = [flux[i] * q_ref[0, i * 7 + j, at, :] for i in range(7)]
                part = line_apply(flipped, flux)
                for i in range(7):
                    n = i * 7 + j
                    part[i] = part[i] + mk_ref[n, at, :] * line[i]
                    im_ref[n, at, :] = part[i]
                acc = acc + tree_sum([part[i] * line[i] for i in range(7)])
            for i in range(7):
                line = [d_ref[i * 7 + j, at, :] for j in range(7)]
                flux = line_apply(DERIV, line)
                flux = [flux[j] * q_ref[1, i * 7 + j, at, :] for j in range(7)]
                part = line_apply(flipped, flux)
                for j in range(7):
                    n = i * 7 + j
                    im_ref[n, at, :] = im_ref[n, at, :] + part[j]
                acc = acc + tree_sum([part[j] * line[j] for j in range(7)])
            return acc

        step = rho / total(by_chunks(image, zero, 2))
        for n in range(49):
            for to in range(2):
                x_ref[to, n] = x_ref[to, n] + step * d_ref[n, own[to], :]

        def descend(k, acc):
            at = here(k)
            for i in range(7):
                line = []
                for j in range(7):
                    n = i * 7 + j
                    value = r_ref[n, at, :] - step * im_ref[n, at, :]
                    r_ref[n, at, :] = value
                    line.append(value)
                acc = acc + square(line, 0.5 if i in (0, 6) else 1.0)
            return acc

        def proceed():
            join()
            fresh = total(by_chunks(descend, zero, 8))
            return fresh, fresh / rho

        return lax.cond(t + 1 < count, proceed, lambda: (rho, beta))

    count = count_ref[row_id]
    lax.fori_loop(0, count, sweep, (rho, zero))

    for i in range(7):
        for to in range(2):
            block = jnp.stack([x_ref[to, i * 7 + j] for j in range(7)] + [zero])
            block = jnp.swapaxes(block, 0, 1)
            for s in range(8):
                t_ref[to, s, i] = block[s]
    for to in range(4):
        for i in range(7):
            value = t_ref[to % 2, z % 4 * 2 + to // 2, i]
            for copy in range(8):
                out_ref[to * 8 + copy, i] = value


def solve(counts, same, other, metrics):
    vmem = pl.BlockSpec(memory_space=pltpu.VMEM)
    field = pltpu.VMEM((49, 64, 128), jnp.float32)
    return pl.pallas_call(
        solve_kernel,
        out_shape=jax.ShapeDtypeStruct((NZ, 7, 8, 128), jnp.float32),
        in_specs=[pl.BlockSpec(memory_space=pltpu.SMEM)] + [vmem] * 3,
        out_specs=vmem,
        scratch_shapes=[
            field, field, field, field,
            pltpu.VMEM((2, 49, 8, 128), jnp.float32),
            pltpu.VMEM((2, 8, 7, 8, 128), jnp.float32),
        ],
        compiler_params=pltpu.CompilerParams(vmem_limit_bytes=40 * MIB),
    )(counts, same, other, metrics)


def pressure_kernel(coef_ref, rows_ref, out_ref):
    y = lax.axis_index("y")
    for zl in range(4):
        coefs = [coef_ref[(y * 4 + zl) * NZ + q] for q in range(NZ)]
        for i in range(7):
            value = tree_sum([coefs[q] * rows_ref[q, i] for q in range(NZ)])
            out_ref[zl, i] = value[0:7, :]


def pressure_planes(rows):
    vmem = pl.BlockSpec(memory_space=pltpu.VMEM)
    return pl.pallas_call(
        pressure_kernel,
        out_shape=jax.ShapeDtypeStruct((4, 7, 7, 128), jnp.float32),
        in_specs=[pl.BlockSpec(memory_space=pltpu.SMEM), vmem],
        out_specs=vmem,
        compiler_params=pltpu.CompilerParams(vmem_limit_bytes=16 * MIB),
    )(jnp.asarray(plane_coefs()), rows)


SWAP = [(0, 1), (1, 0)]
TURNS = [[(at, (at + back) % 4) for at in range(4)] for back in range(1, 4)]


def after(value, other):
    return lax.optimization_barrier((value, other))[0]


def local(stress, velocity_grad, velocity, metric, iteration_counts):
    packed = jnp.pad(metric.reshape(147, 128), ((0, 5), (0, 0)))
    turned = [lax.ppermute(packed, RING_X, turn) for turn in TURNS]
    right, left, up, down = pack_faces(stress)
    ahead = [(c, c + 1) for c in range(15)]
    above = [(e, e + 1) for e in range(3)]
    faces = (
        lax.ppermute(right, FLOW, ahead),
        lax.ppermute(left, FLOW, [(b, a) for a, b in ahead]),
        lax.ppermute(up, CROSS, above),
        lax.ppermute(down, CROSS, [(b, a) for a, b in above]),
    )
    ring = jnp.stack([after(packed, right)] + turned)
    faces = after(faces, ring)
    metrics = metric_fields(lax.all_gather(ring, ("zh", "zl", "core")))
    new_stress, parts = stress_step(stress, velocity_grad, velocity, faces)
    parts = lax.all_to_all(parts, ROWS, 0, 0, tiled=True)
    mine = jnp.sum(parts.reshape(4, 8, 7, 8, 128), axis=1)
    pair = jnp.stack([mine, lax.ppermute(mine, "zl", SWAP)])
    same = lax.all_gather(pair, "zh")
    other = lax.ppermute(same, "core", SWAP)
    answer = solve(iteration_counts, same, other, metrics)
    answer = lax.all_to_all(answer, ROWS, 0, 0, tiled=True)
    return new_stress, pressure_planes(answer)


def solution(mesh):
    fine = Mesh(mesh.devices.reshape(SPLIT), PLANE + ("y",))
    field = P(None, "y", None, None, PLANE)
    return jax.shard_map(
        local,
        mesh=fine,
        in_specs=(field, field, field, P(None, None, None, PLANE), P()),
        out_specs=(field, P("y", None, None, PLANE)),
        check_vma=False,
    )
```
